32 devices in a mesh: dp: 32 (over z, y, x, core).
Axes of the slice: x: 2, y: 2, z: 4, core: 2. Of those that a mesh axis runs over, the one named last changes fastest.
Arguments:
- inputs: bfloat16 [64, 1024, 512], P('dp'), may hold values from -6 to 6
- valid_len: int32 [64], P('dp'), may hold values from 615 to 1024
- norm_first: bfloat16 [512], P('dp'), may hold values from 0.5 to 1.5
- w_qkv: bfloat16 [512, 1536], P('dp'), may hold values from -0.25 to 0.25
- w_out: bfloat16 [512, 512], P('dp'), may hold values from -1.5 to 1.5
- relative_bucket_table: bfloat16 [8, 16], replicated, may hold values from -4 to 4
- norm_second: bfloat16 [512], P('dp'), may hold values from 0.5 to 1.5
- w_up: bfloat16 [512, 2048], P('dp'), may hold values from -0.25 to 0.25
- w_down: bfloat16 [2048, 512], P('dp'), may hold values from -0.125 to 0.125
- output_gradient: bfloat16 [64, 1024, 512], P('dp'), may hold values from -6 to 6
Outputs:
- output: bfloat16 [64, 1024, 512], P('dp')
- grad_inputs: bfloat16 [64, 1024, 512], P('dp')
- grad_norm_first: float32 [512], P('dp')
- grad_w_qkv: float32 [512, 1536], P('dp')
- output_weight_gradient: float32 [512, 512], P('dp')
- grad_rel_table: float32 [8, 16], replicated
- grad_norm_second: float32 [512], P('dp')
- grad_w_up: float32 [512, 2048], P('dp')
- down_weight_gradient: float32 [2048, 512], P('dp')
The draws below stay inside these ranges and needn't reach their ends.
All inputs are finite; a program needn't handle non-finite values.
Results may differ from the reference program's by a relative error of at most 0.013.
Values may be sent and summed in bfloat16 or wider, within the bound.
A program may use at most 256 MiB of HBM per device.

```python
import jax
import jax.numpy as jnp
import numpy as np
from jax import lax

D = 512
HEADS = 8
HEAD_DIM = 64
FF = 2048
BUCKETS = 16
SEQ_LEN = 1024
SEQS = 64


def draw_valid_len(key, part):
    key = jax.random.fold_in(key, 11)
    first_key, second_key, third_key = jax.random.split(key, 3)
    shortest = SEQ_LEN - 2 * SEQ_LEN // 5
    lengths = jax.random.randint(first_key, (SEQS,), shortest, SEQ_LEN + 1, dtype=jnp.int32)
    full_index = jax.random.randint(second_key, (), 0, SEQS, dtype=jnp.int32)
    short_index = (full_index + 1 + jax.random.randint(third_key, (), 0, SEQS - 1, dtype=jnp.int32)) % SEQS
    lengths = lengths.at[full_index].set(SEQ_LEN)
    return lengths.at[short_index].set(shortest)


def block_levels(stream_key, shape, cuts, smallest, high):
    def one(dim, shards_of):
        heights = jax.random.uniform(jax.random.fold_in(jax.random.fold_in(stream_key, 6), dim), (shards_of,), jnp.float32, smallest / len(cuts), high / len(cuts))
        return jnp.repeat(jnp.exp(heights), shape[dim] // shards_of).reshape((-1,) + (1,) * (len(shape) - dim - 1))

    factor_of = one(*cuts[0])
    for cut in cuts[1:]:
        factor_of = factor_of * one(*cut)
    return factor_of


def bell_draw(key, extent, scale, bound, cuts=(), kind=jnp.bfloat16):
    gain = block_levels(key, extent, cuts, -0.22, 0.18) if cuts else 1.0
    entries = jax.random.normal(key, extent, jnp.float32) * scale * gain
    return jnp.minimum(jnp.maximum(entries, -bound), bound).astype(kind)


def setup_inputs(seed: int = 0) -> dict:
    streams_of = jax.random.split(jax.random.key(seed), 11)
    return {
        "inputs": bell_draw(streams_of[0], (SEQS, SEQ_LEN, D), 1.0, 6.0, ((0, 32),)),
        "valid_len": draw_valid_len(jax.random.fold_in(streams_of[10], 71), 0),
        "norm_first": jnp.clip(1.0 + 0.1 * jax.random.normal(streams_of[2], (D,), jnp.float32), 0.5, 1.5).astype(jnp.bfloat16),
        "w_qkv": bell_draw(streams_of[3], (D, 3 * D), D ** -0.5, 0.25, ((0, 32),)),
        "w_out": bell_draw(streams_of[4], (D, D), (D // 32) ** -0.5, 1.5, ((0, 32),)),
        "relative_bucket_table": bell_draw(streams_of[5], (HEADS, BUCKETS), 1.0, 4.0),
        "norm_second": jnp.clip(1.0 + 0.1 * jax.random.normal(streams_of[6], (D,), jnp.float32), 0.5, 1.5).astype(jnp.bfloat16),
        "w_up": bell_draw(streams_of[7], (D, FF), D ** -0.5, 0.25, ((0, 32),)),
        "w_down": bell_draw(streams_of[8], (FF, D), FF ** -0.5, 0.125, ((0, 32),)),
        "output_gradient": bell_draw(streams_of[9], (SEQS, SEQ_LEN, D), 1.0, 6.0, ((0, 32),)),
    }


@jax.custom_vjp
def lowered_weights(v):
    return lax.optimization_barrier(v.astype(jnp.bfloat16)).astype(jnp.float32)

@jax.custom_vjp
def lowered_backward_weights(v):
    return v

def low_keep(v):
    return (lowered_weights(v), None)

def low_pass(kept, grad):
    return (grad,)

def back_keep(v):
    return (v, None)

def back_low(kept, grad):
    return (lowered_weights(grad),)
lowered_weights.defvjp(low_keep, low_pass)
lowered_backward_weights.defvjp(back_keep, back_low)
epsilon = 1e-05
masked_score = -1e+30
exact_precision = lax.Precision.HIGHEST
bucket_low = np.array([0, 1, 2, 3, 4, 5, 6, 7, 8, 12, 16, 32, 64, 128, 256, 512], np.int32)
bucket_high = np.array([1, 2, 3, 4, 5, 6, 7, 8, 12, 16, 32, 64, 128, 256, 512, 1 << 30], np.int32)

def layer_norm(values, scale_gain):
    centered = values - lax.optimization_barrier(jnp.mean(values, axis=-1, keepdims=True))
    spread = lax.optimization_barrier(jnp.mean(centered * centered, axis=-1, keepdims=True))
    return centered * lax.rsqrt(spread + epsilon) * scale_gain

def bucket_mask(first_row, row_count, length):
    query_pos = first_row + jnp.arange(row_count, dtype=jnp.int32)
    key_pos = jnp.arange(length, dtype=jnp.int32)
    distance = query_pos[:, None] - key_pos[None, :]
    lower = jnp.asarray(bucket_low)[:, None, None]
    upper = jnp.asarray(bucket_high)[:, None, None]
    inner_activation = (distance[None] >= lower) & (distance[None] < upper)
    return (distance, key_pos, inner_activation)

def attention_block(block_index, query_rows, key_rows, value_rows, valid_rows, bucket_bias_table):
    length = key_rows.shape[1]
    row_count = min(512, length)
    first_row = block_index * row_count
    distance, key_pos, inner_activation = bucket_mask(first_row, row_count, length)
    block_queries = lax.dynamic_slice_in_dim(query_rows, first_row, row_count, 1)
    raw_scores = jnp.einsum('sqhd,skhd->shqk', block_queries, key_rows, precision=exact_precision) * HEAD_DIM ** (-0.5)
    relative_position_bias = jnp.einsum('jc,cma->jma', bucket_bias_table, inner_activation.astype(jnp.float32), precision=exact_precision)
    scores = lowered_backward_weights(raw_scores + relative_position_bias[None])
    allowed = (distance >= 0)[None] & (key_pos[None, None, :] < valid_rows[:, None, None])
    scores = jnp.where(allowed[:, None], scores, masked_score)
    row_max = lax.optimization_barrier(jnp.max(scores, axis=-1, keepdims=True))
    weights = jnp.exp(scores - row_max)
    probabilities = lowered_weights(weights / lax.optimization_barrier(jnp.sum(weights, axis=-1, keepdims=True)))
    return jnp.einsum('shqk,skhd->sqhd', probabilities, value_rows, precision=exact_precision)

def group_forward(residual_stream, valid_rows, gain_first, query_key_value_matrix, output_matrix, bucket_bias_table, gain_second, up_matrix, down_matrix):
    group_size, length, width = residual_stream.shape
    first_normalized = lowered_weights(layer_norm(residual_stream, gain_first))
    projected_output = lowered_backward_weights(lowered_weights(jnp.einsum('apk,kq->apq', first_normalized, query_key_value_matrix, precision=exact_precision)))
    projected_output = projected_output.reshape(group_size, length, 3, HEADS, HEAD_DIM)
    query_rows = projected_output[:, :, 0]
    key_rows = projected_output[:, :, 1]
    value_rows = projected_output[:, :, 2]
    row_count = min(512, length)

    def one_block(block_index):
        return attention_block(block_index, query_rows, key_rows, value_rows, valid_rows, bucket_bias_table)
    blocks = lax.map(jax.checkpoint(one_block), jnp.arange(length // row_count, dtype=jnp.int32))
    attended = jnp.moveaxis(blocks, 0, 1).reshape(group_size, length, width)
    attention_mixed = lowered_backward_weights(lowered_weights(attended))
    attention_result = residual_stream + lowered_backward_weights(jnp.einsum('jmu,uf->jmf', attention_mixed, output_matrix, precision=exact_precision))
    second_normalized = lowered_weights(layer_norm(attention_result, gain_second))
    preactivation_values = lowered_backward_weights(jnp.einsum('qmj,ja->qma', second_normalized, up_matrix, precision=exact_precision))
    hidden_state = lowered_weights(jax.nn.gelu(preactivation_values, approximate=True))
    return attention_result + lowered_backward_weights(jnp.einsum('hor,rt->hot', hidden_state, down_matrix, precision=exact_precision))

def reference(inputs, valid_len, norm_first, w_qkv, w_out, relative_bucket_table, norm_second, w_up, w_down, output_gradient):
    group_size = min(SEQS, max(1, 4096 // SEQ_LEN))
    group_count = SEQS // group_size

    def forward(residual_stream, gain_first, query_key_value_matrix, output_matrix, bucket_bias_table, gain_second, up_matrix, down_matrix):

        def one_group(group_items):
            return group_forward(group_items[0], group_items[1], gain_first, query_key_value_matrix, output_matrix, bucket_bias_table, gain_second, up_matrix, down_matrix)
        grouped = lax.map(jax.checkpoint(one_group), (residual_stream.reshape(group_count, group_size, SEQ_LEN, D), valid_len.reshape(group_count, group_size)))
        return grouped.reshape(SEQS, SEQ_LEN, D)
    result, pullback = jax.vjp(forward, inputs.astype(jnp.float32), norm_first.astype(jnp.float32), w_qkv.astype(jnp.float32), w_out.astype(jnp.float32), relative_bucket_table.astype(jnp.float32), norm_second.astype(jnp.float32), w_up.astype(jnp.float32), w_down.astype(jnp.float32))
    grads = pullback(output_gradient.astype(jnp.float32))
    return (result.astype(jnp.bfloat16), grads[0].astype(jnp.bfloat16), grads[1], grads[2], grads[3], grads[4], grads[5], grads[6], grads[7])
```

```python
import functools

import jax
import jax.numpy as jnp
import numpy as np
from jax import lax
from jax.experimental import pallas as pl
from jax.experimental.pallas import tpu as pltpu
from jax.sharding import PartitionSpec as P

MESH = pl.DeviceIdType.MESH
F32 = jnp.float32
BF = jnp.bfloat16
EPS = 1e-05


AXES = ("z", "y", "x", "core")


def device_grid(devices):
    return (devices // 8, 2, 2, 2)


def grid_position(sizes):
    rest = lax.axis_index("dp")
    place = []
    for size in reversed(sizes):
        place.append(lax.rem(rest, size))
        rest = lax.div(rest, size)
    return tuple(reversed(place))


def device_at(place, sizes):
    index = place[0]
    for axis in range(1, 4):
        index = index * sizes[axis] + place[axis]
    return index


def moved(place, sizes, axis, step):
    other = list(place)
    other[axis] = lax.rem(place[axis] + step, sizes[axis])
    return tuple(other)


def greet(sizes):
    place = grid_position(sizes)
    barrier = pltpu.get_barrier_semaphore()
    count = 0
    for axis in range(4):
        for step in range(1, sizes[axis]):
            pl.semaphore_signal(
                barrier,
                inc=1,
                device_id=(device_at(moved(place, sizes, axis, step), sizes),),
                device_id_type=MESH,
            )
            count += 1
    pl.semaphore_wait(barrier, count)


class Gather:
    def __init__(self, sizes, order, own, whole, local_sem, send_sems, recv_sems):
        self.sizes, self.order = sizes, order
        self.own, self.whole = own, whole
        self.local_sem, self.send_sems, self.recv_sems = local_sem, send_sems, recv_sems

    def copies(self, phase):
        place = grid_position(self.sizes)
        done = self.order[:phase]
        index = tuple(slice(None) if a in done else place[a] for a in range(4))
        axis = self.order[phase]
        part = self.whole.at[index]
        return [
            pltpu.make_async_remote_copy(
                src_ref=self.own if phase == 0 else part,
                dst_ref=part,
                send_sem=self.send_sems.at[phase, step],
                recv_sem=self.recv_sems.at[phase, step],
                device_id=(device_at(moved(place, self.sizes, axis, step), self.sizes),),
                device_id_type=MESH,
            )
            for step in range(1, self.sizes[axis])
        ]

    def local(self):
        return pltpu.make_async_copy(
            self.own, self.whole.at[grid_position(self.sizes)], self.local_sem
        )

    def start(self, phase):
        if phase == 0:
            self.local().start()
        for copy in self.copies(phase):
            copy.start()

    def finish(self, phase):
        if phase == 0:
            self.local().wait()
        for copy in self.copies(phase):
            copy.wait()


class Scatter:
    def __init__(self, sizes, order, terms, sums, landing, result, send_sems, recv_sems):
        self.sizes, self.order = sizes, order
        self.held = [terms] + list(sums)
        self.landing, self.result = landing, result
        self.send_sems, self.recv_sems = send_sems, recv_sems

    @staticmethod
    def shapes(sizes, order, block):
        left, sums, landing = set(range(4)), [], []
        for phase, axis in enumerate(order):
            left.discard(axis)
            lead = tuple(sizes[a] for a in sorted(left))
            landing.append((sizes[axis] if sizes[axis] > 2 else 1,) + lead + block)
            if phase < 3:
                sums.append(lead + block)
        return sums, landing

    def pick(self, phase, coordinate):
        axis = self.order[phase]
        left = [a for a in range(4) if a not in self.order[:phase]]
        return tuple(coordinate if a == axis else slice(None) for a in left)

    def copies(self, phase):
        place = grid_position(self.sizes)
        axis = self.order[phase]
        out = []
        for step in range(1, self.sizes[axis]):
            other = moved(place, self.sizes, axis, step)
            out.append(
                pltpu.make_async_remote_copy(
                    src_ref=self.held[phase].at[self.pick(phase, other[axis])],
                    dst_ref=self.landing[phase].at[place[axis] if self.sizes[axis] > 2 else 0],
                    send_sem=self.send_sems.at[phase, step],
                    recv_sem=self.recv_sems.at[phase, step],
                    device_id=(device_at(other, self.sizes),),
                    device_id_type=MESH,
                )
            )
        return out

    def start(self, phase):
        for copy in self.copies(phase):
            copy.start()

    def finish(self, phase):
        for copy in self.copies(phase):
            copy.wait()
        place = grid_position(self.sizes)
        axis = self.order[phase]
        left = [a for a in range(4) if a not in self.order[: phase + 1]]
        held, landed = self.held[phase], self.landing[phase]
        lead = [self.sizes[a] for a in left]
        target = self.held[phase + 1] if phase < 3 else self.result

        def one(at):
            spot = tuple(at)
            full = list(spot)
            full.insert(sorted(left + [axis]).index(axis), place[axis])
            if self.sizes[axis] == 2:
                total = held[tuple(full)].astype(jnp.float32) + landed[(0,) + spot].astype(
                    jnp.float32
                )
            else:
                landed[(place[axis],) + spot] = held[tuple(full)]
                total = landed[(0,) + spot].astype(jnp.float32)
                for source in range(1, self.sizes[axis]):
                    total = total + landed[(source,) + spot].astype(jnp.float32)
            if phase < 3:
                target[spot] = total.astype(target.dtype)
            else:
                target[...] = total.astype(target.dtype)

        if not left:
            one(())
        else:
            def body(count, unused):
                at = []
                for size in reversed(lead):
                    at.append(lax.rem(count, size))
                    count = lax.div(count, size)
                one(reversed(at))
                return unused
            lax.fori_loop(0, int(np.prod(lead)), body, 0)


LOW=(0,1,2,3,4,5,6,7,8,12,16,32,64,128,256,512)
T=256
NEG=-1e30
def cp(**k): return pltpu.CompilerParams(vmem_limit_bytes=56*2**20, **k)
def dot_nt(a,b): return lax.dot_general(a,b,(((1,),(1,)),((),())),preferred_element_type=jnp.float32)
def dot_nn(a,b): return jnp.dot(a,b,preferred_element_type=jnp.float32)
def dot_tn(a,b): return lax.dot_general(a,b,(((0,),(0,)),((),())),preferred_element_type=jnp.float32)

def bias_of(dist, row):
    out=jnp.zeros(dist.shape,jnp.float32)+row[:,0:1]
    for b in range(1,16):
        out=jnp.where(dist>=LOW[b],row[:,b:b+1],out)
    return jnp.where(dist<0,NEG,out)

def build_bias(table_ref, hp, bias, transposed):
    lane=lax.broadcasted_iota(jnp.int32,(1,2*T),1)
    m=jnp.where(lane<T,lane,lane-2*T)
    for h in range(2):
        row=table_ref[0,h:h+1,:]
        for bd in range(3):
            w=bias_of(bd*T+(m if transposed else -m),row)
            tile=pltpu.roll(jnp.broadcast_to(w,(T,2*T)),0,1,stride=1,stride_axis=0)
            bias[h,bd]=tile[:,:T]
        bias[h,3]=jnp.broadcast_to(row[:,15:16],(T,T))

def split3(v):
    hi=v.astype(jnp.bfloat16); r=v-hi.astype(jnp.float32)
    mid=r.astype(jnp.bfloat16); lo=(r-mid.astype(jnp.float32)).astype(jnp.bfloat16)
    return hi,mid,lo

def halves(h, main, extra, rows):
    lane=lax.broadcasted_iota(jnp.int32,(rows,128),1)
    out=jnp.where((lane//64)==h,main,jnp.zeros((),main.dtype))
    base=64*(1-h)
    for n,e in enumerate(extra):
        if e is not None:
            out=jnp.where(lane==base+n,jnp.broadcast_to(e,(rows,128)).astype(jnp.bfloat16),out)
    return out

def fwd_kernel(vl_ref,table_ref,q_ref,k_ref,v_ref,mixed_ref,qa_ref,bias):
    hp=pl.program_id(0); s=pl.program_id(1)
    @pl.when(s==0)
    def _(): build_bias(table_ref,hp,bias,False)
    L=q_ref.shape[1]; nb=L//T
    one=jnp.ones((),jnp.bfloat16)
    key=lax.broadcasted_iota(jnp.int32,(L,1),0)
    mask=jnp.where(key<vl_ref[s],0.0,NEG)
    lane=lax.broadcasted_iota(jnp.int32,(T,128),1)
    ks=[halves(h,k_ref[0],[1.0,1.0,1.0,mask],L) for h in range(2)]
    for qb in range(nb):
        kk=(qb+1)*T
        qt=q_ref[0,qb*T:(qb+1)*T,:]*jnp.asarray(0.125,jnp.bfloat16)
        outs=[]
        for h in range(2):
            qh=halves(h,qt,[None,None,None,1.0],T)
            sc=dot_nt(qh,ks[h][:kk])
            sc=jnp.concatenate([sc[:,kb*T:(kb+1)*T]+bias[h,qb-kb] for kb in range(qb+1)],axis=1)
            mx=jnp.max(sc,axis=1,keepdims=True)
            p=jnp.exp(sc-mx)
            l=jnp.sum(p,axis=1,keepdims=True)
            o=dot_nn(p.astype(jnp.bfloat16),v_ref[0,:kk,:])
            outs.append(o*(1.0/l))
            hi,mid,lo=split3(-(mx+jnp.log(l)))
            qa_ref[0,0,h,qb*T:(qb+1)*T,:]=halves(h,qt,[hi,mid,lo,1.0],T)
        mixed_ref[0,qb*T:(qb+1)*T,:]=jnp.where(lane<64,outs[0],outs[1]).astype(jnp.bfloat16)

def attn_fwd(vl,table,qkv):
    S,L,W=qkv.shape; HP=W//3//128
    return pl.pallas_call(fwd_kernel,grid=(HP,S),
        in_specs=[pl.BlockSpec(memory_space=pltpu.SMEM),pl.BlockSpec((1,2,16),lambda h,s:(h,0,0)),
          pl.BlockSpec((1,L,128),lambda h,s:(s,0,h)),pl.BlockSpec((1,L,128),lambda h,s:(s,0,HP+h)),pl.BlockSpec((1,L,128),lambda h,s:(s,0,2*HP+h))],
        out_specs=[pl.BlockSpec((1,L,128),lambda h,s:(s,0,h)),pl.BlockSpec((1,1,2,L,128),lambda h,s:(s,h,0,0,0))],
        out_shape=[jax.ShapeDtypeStruct((S,L,HP*128),jnp.bfloat16),jax.ShapeDtypeStruct((S,HP,2,L,128),jnp.bfloat16)],
        scratch_shapes=[pltpu.VMEM((2,4,T,T),jnp.float32)],
        compiler_params=cp())(vl,table.astype(jnp.float32).reshape(HP,2,16),qkv,qkv,qkv)

def bwd_kernel(mode,vl_ref,table_ref,qa_ref,k_ref,v_ref,o_ref,g_ref,dq_ref,dk_ref,dv_ref,tab_ref,bias,gacc,far,dqt):
    hp=pl.program_id(0); s=pl.program_id(1)
    L=k_ref.shape[1]; nb=L//T
    @pl.when(s==0)
    def _():
        build_bias(table_ref,hp,bias,True)
        gacc[...]=jnp.zeros_like(gacc); far[...]=jnp.zeros_like(far)
    key=lax.broadcasted_iota(jnp.int32,(L,1),0)
    mask=jnp.where(key<vl_ref[s],0.0,NEG)
    lane=lax.broadcasted_iota(jnp.int32,(T,128),1)
    g=g_ref[0]
    prod=g.astype(jnp.float32)*o_ref[0].astype(jnp.float32)
    lane_l=lax.broadcasted_iota(jnp.int32,(L,128),1)
    ks=[halves(h,k_ref[0],[1.0,1.0,1.0,mask],L) for h in range(2)]
    vs=[halves(h,v_ref[0],[1.0,1.0,1.0],L) for h in range(2)]
    gs=[]
    for h in range(2):
        d=jnp.sum(jnp.where((lane_l//64)==h,prod,0.0),axis=1,keepdims=True)
        hi,mid,lo=split3(-d)
        gs.append(halves(h,g,[hi,mid,lo],L))
    if mode==0:
        kt=(k_ref[0]*jnp.asarray(0.125,jnp.bfloat16)).T
    dqs=[[None]*nb,[None]*nb]
    for kb in range(nb):
        dks=[];dvs=[]
        for h in range(2):
            qh=qa_ref[0,0,h]
            st=dot_nt(ks[h][kb*T:(kb+1)*T],qh[kb*T:])
            dp=dot_nt(vs[h][kb*T:(kb+1)*T],gs[h][kb*T:])
            st=jnp.concatenate([st[:,i*T:(i+1)*T]+bias[h,i] for i in range(nb-kb)],axis=1)
            p=jnp.exp(st)
            ds=p*dp
            pb=p.astype(jnp.bfloat16); dsb=ds.astype(jnp.bfloat16)
            dvs.append(dot_nn(pb,gs[h][kb*T:])); dks.append(dot_nn(dsb,qh[kb*T:]))
            for i in range(min(nb-kb,3)):
                gacc[h,i]+=ds[:,i*T:(i+1)*T]
            if nb-kb>3:
                far[h:h+1,:]+=jnp.sum(ds[:,3*T:],axis=0,keepdims=True)
            if mode==0:
                r=dot_nn(kt[h*64:(h+1)*64,kb*T:(kb+1)*T],dsb)
                if kb==0: dqt[h*64:(h+1)*64,:]=r
                else: dqt[h*64:(h+1)*64,kb*T:]+=r
            else:
                r=dot_tn(dsb,k_ref[0,kb*T:(kb+1)*T,:])
                if kb==0: dqt[h]=r
                else: dqt[h,kb*T:]+=r
        dk_ref[0,kb*T:(kb+1)*T,:]=jnp.where(lane<64,dks[0],dks[1]).astype(jnp.bfloat16)
        dv_ref[0,kb*T:(kb+1)*T,:]=jnp.where(lane<64,dvs[0],dvs[1]).astype(jnp.bfloat16)
    if mode==0:
        dq_ref[0]=dqt[...].T.astype(jnp.bfloat16)
    else:
        dq_ref[0]=(jnp.where(lane_l<64,dqt[0],dqt[1])*0.125).astype(jnp.bfloat16)
    @pl.when(s==pl.num_programs(1)-1)
    def _():
        lane2=lax.broadcasted_iota(jnp.int32,(1,2*T),1)
        m=jnp.where(lane2<T,lane2,lane2-2*T)
        bl=lax.broadcasted_iota(jnp.int32,(1,128),1)
        for h in range(2):
            row=jnp.where(bl==15,jnp.sum(far[h:h+1,:],axis=1,keepdims=True),0.0)
            for bd in range(3):
                w=jnp.concatenate([gacc[h,bd],jnp.zeros((T,T),jnp.float32)],axis=1)
                acc=w[:8]
                for a in range(1,T//8):
                    acc=acc+pltpu.roll(w[8*a:8*a+8],2*T-8*a,1)
                diag=acc[0:1]
                for a in range(1,8):
                    diag=diag+pltpu.roll(acc[a:a+1],2*T-a,1)
                dist=bd*T+m
                for b in range(16):
                    if LOW[b]>=(bd+1)*T or (b<15 and LOW[b+1]<=(bd-1)*T): continue
                    sel=dist>=LOW[b]
                    if b<15: sel=sel&(dist<LOW[b+1])
                    row=row+jnp.where(bl==b,jnp.sum(jnp.where(sel,diag,0.0),axis=1,keepdims=True),0.0)
            tab_ref[0,h:h+1,:]=row

def attn_bwd(vl,table,qa,qkv,mixed,gm,mode=0):
    S,L,W=qkv.shape; HP=W//3//128
    blk=lambda off:pl.BlockSpec((1,L,128),lambda h,s,off=off:(s,0,off+h))
    sh=jax.ShapeDtypeStruct((S,L,HP*128),jnp.bfloat16)
    return pl.pallas_call(functools.partial(bwd_kernel,mode),grid=(HP,S),
        in_specs=[pl.BlockSpec(memory_space=pltpu.SMEM),pl.BlockSpec((1,2,16),lambda h,s:(h,0,0)),
          pl.BlockSpec((1,1,2,L,128),lambda h,s:(s,h,0,0,0)),blk(HP),blk(2*HP),blk(0),blk(0)],
        out_specs=[blk(0),blk(0),blk(0),pl.BlockSpec((1,8,128),lambda h,s:(h,0,0))],
        out_shape=[sh,sh,sh,jax.ShapeDtypeStruct((HP,8,128),jnp.float32)],
        scratch_shapes=[pltpu.VMEM((2,4,T,T),jnp.float32),pltpu.VMEM((2,3,T,T),jnp.float32),pltpu.VMEM((8,T),jnp.float32),
           pltpu.VMEM((128,L) if mode==0 else (2,L,128),jnp.float32)],
        compiler_params=cp())(vl,table.astype(jnp.float32).reshape(HP,2,16),qa,qkv,qkv,mixed,gm)


def ln_parts(v):
    c=v-jnp.mean(v,axis=1,keepdims=True)
    r=lax.rsqrt(jnp.mean(c*c,axis=1,keepdims=True)+EPS)
    return c*r, r
def ln_back(e_in,gain,xhat,r):
    e=e_in*gain
    gv=r*(e-jnp.mean(e,axis=1,keepdims=True)-xhat*jnp.mean(e*xhat,axis=1,keepdims=True))
    return gv, jnp.sum(e_in*xhat,axis=0,keepdims=True)

def qkv_kernel(x_ref,g_ref,w_ref,n_ref,o_ref):
    xhat,_=ln_parts(x_ref[...].astype(F32))
    n=(xhat*g_ref[...].astype(F32)).astype(BF)
    n_ref[...]=n
    o_ref[...]=dot_nn(n,w_ref[...]).astype(BF)
def qkv_fwd(x,gain,w,B=512):
    R,D=x.shape; N=w.shape[1]
    return pl.pallas_call(qkv_kernel,grid=(R//B,),
      in_specs=[pl.BlockSpec((B,D),lambda i:(i,0)),pl.BlockSpec((1,D),lambda i:(0,0)),pl.BlockSpec((D,N),lambda i:(0,0))],
      out_specs=[pl.BlockSpec((B,D),lambda i:(i,0)),pl.BlockSpec((B,N),lambda i:(i,0))],
      out_shape=[jax.ShapeDtypeStruct((R,D),BF),jax.ShapeDtypeStruct((R,N),BF)],compiler_params=cp())(x,gain,w)

def ffn_kernel(x_ref,m_ref,og_ref,g_ref,wo_ref,wu_ref,wd_ref,out_ref,ga_ref,gm_ref,gwo_ref,gwu_ref,gwd_ref,gg_ref,ao,au,ad):
    i=pl.program_id(0)
    m=m_ref[...]; og=og_ref[...]
    after=x_ref[...].astype(F32)+dot_nn(m,wo_ref[...])
    xhat,r=ln_parts(after)
    gain=g_ref[...].astype(F32)
    n=(xhat*gain).astype(BF)
    pre=dot_nn(n,wu_ref[...])
    dh=dot_nt(og,wd_ref[...])
    c=0.7978845608028654
    sq=pre*pre
    t=jnp.tanh(pre*(c+c*0.044715*sq))
    half=0.5*(1.0+t)
    hid=(pre*half).astype(BF)
    dg=half+(0.5*pre)*(1.0-t*t)*(c+3*c*0.044715*sq)
    gp=(dh*dg).astype(BF)
    out_ref[...]=(after+dot_nn(hid,wd_ref[...])).astype(BF)
    pd=dot_tn(hid,og); pu=dot_tn(n,gp)
    dn=dot_nt(gp,wu_ref[...])
    gv,gg=ln_back(dn,gain,xhat,r)
    ga=og.astype(F32)+gv
    ga_ref[...]=ga
    gb=ga.astype(BF)
    po=dot_tn(m,gb)
    gm_ref[...]=dot_nt(gb,wo_ref[...]).astype(BF)
    @pl.when(i==0)
    def _():
        ad[...]=pd; au[...]=pu; ao[...]=po; gg_ref[...]=gg
    @pl.when(i>0)
    def _():
        ad[...]+=pd; au[...]+=pu; ao[...]+=po; gg_ref[...]+=gg
    @pl.when(i==pl.num_programs(0)-1)
    def _():
        gwo_ref[...]=ao[...].astype(BF); gwu_ref[...]=au[...].astype(BF); gwd_ref[...]=ad[...].astype(BF)
def ffn(x,m,og,gain,wo,wu,wd,B=512):
    R,D=x.shape; FF=wu.shape[1]
    row=pl.BlockSpec((B,D),lambda i:(i,0))
    full=lambda a,b:pl.BlockSpec((a,b),lambda i:(0,0))
    return pl.pallas_call(ffn_kernel,grid=(R//B,),
      in_specs=[row,row,row,full(1,D),full(D,D),full(D,FF),full(FF,D)],
      out_specs=[row,row,row,full(D,D),full(D,FF),full(FF,D),full(1,D)],
      out_shape=[jax.ShapeDtypeStruct((R,D),BF),jax.ShapeDtypeStruct((R,D),F32),jax.ShapeDtypeStruct((R,D),BF),
        jax.ShapeDtypeStruct((D,D),BF),jax.ShapeDtypeStruct((D,FF),BF),jax.ShapeDtypeStruct((FF,D),BF),jax.ShapeDtypeStruct((1,D),F32)],
      scratch_shapes=[pltpu.VMEM((D,D),F32),pltpu.VMEM((D,FF),F32),pltpu.VMEM((FF,D),F32)],
      compiler_params=cp())(x,m,og,gain,wo,wu,wd)

def qkvb_kernel(x_ref,n_ref,dq_ref,dk_ref,dv_ref,ga_ref,g_ref,w_ref,gi_ref,gw_ref,gg_ref,acc):
    i=pl.program_id(0)
    D=x_ref.shape[1]
    xhat,r=ln_parts(x_ref[...].astype(F32))
    n=n_ref[...]
    d=jnp.concatenate([dq_ref[...],dk_ref[...],dv_ref[...]],axis=1)
    pw=dot_tn(n,d)
    dn=dot_nt(d,w_ref[...])
    gv,gg=ln_back(dn,g_ref[...].astype(F32),xhat,r)
    gi_ref[...]=(ga_ref[...]+gv).astype(BF)
    @pl.when(i==0)
    def _():
        acc[...]=pw; gg_ref[...]=gg
    @pl.when(i>0)
    def _():
        acc[...]+=pw; gg_ref[...]+=gg
    @pl.when(i==pl.num_programs(0)-1)
    def _():
        gw_ref[...]=acc[...].astype(BF)
def qkv_bwd(x,n,dq,dk,dv,ga,gain,w,B=512):
    R,D=x.shape; N=w.shape[1]
    row=pl.BlockSpec((B,D),lambda i:(i,0))
    full=lambda a,b:pl.BlockSpec((a,b),lambda i:(0,0))
    return pl.pallas_call(qkvb_kernel,grid=(R//B,),
      in_specs=[row]*6+[full(1,D),full(D,N)],
      out_specs=[row,full(D,N),full(1,D)],
      out_shape=[jax.ShapeDtypeStruct((R,D),BF),jax.ShapeDtypeStruct((D,N),BF),jax.ShapeDtypeStruct((1,D),F32)],
      scratch_shapes=[pltpu.VMEM((D,N),F32)],
      compiler_params=cp())(x,n,dq,dk,dv,ga,gain,w)


def gather_kernel(sizes, orders, *refs):
    n = len(orders)
    own, whole, (local, send, recv) = refs[:n], refs[n:2 * n], refs[2 * n:]
    greet(sizes)
    parts = [Gather(sizes, orders[k], own[k], whole[k], local.at[k], send.at[k], recv.at[k]) for k in range(n)]
    for part in parts:
        part.start(0)
    for phase in range(4):
        for part in parts:
            part.finish(phase)
            if phase < 3:
                part.start(phase + 1)


def gather_all(sizes, arrays, orders):
    n = len(arrays)
    anyspace = pl.BlockSpec(memory_space=pl.ANY)
    return pl.pallas_call(
        functools.partial(gather_kernel, sizes, orders),
        in_specs=[anyspace] * n,
        out_specs=[anyspace] * n,
        out_shape=[jax.ShapeDtypeStruct(sizes + a.shape, a.dtype) for a in arrays],
        scratch_shapes=[pltpu.SemaphoreType.DMA((n,)), pltpu.SemaphoreType.DMA((n, 4, max(sizes))), pltpu.SemaphoreType.DMA((n, 4, max(sizes)))],
        compiler_params=pltpu.CompilerParams(collective_id=1, has_side_effects=True),
    )(*arrays)


def pack_small(sizes, small, gain_first, gain_second, table):
    for z in range(sizes[0]):
        block = [gain_first[:, z * 128:(z + 1) * 128], gain_second[:, z * 128:(z + 1) * 128], jnp.zeros((6, 128), F32)]
        block += [table[pair, 0:2, :] for pair in range(table.shape[0])]
        block = jnp.concatenate(block, axis=0)

        def body(count, unused):
            small[z, lax.div(count, 4), lax.rem(lax.div(count, 2), 2), lax.rem(count, 2)] = block
            return unused

        lax.fori_loop(0, 8, body, 0)


def scatter_kernel(sizes, orders, plan, *refs):
    n = len(orders)
    terms, (gain_first, gain_second, table), results = refs[:n - 1], refs[n - 1:n + 2], refs[n + 2:2 * n + 2]
    rest = list(refs[2 * n + 2:])
    small = rest.pop(0)
    send, recv = rest[-2:]
    pack_small(sizes, small, gain_first, gain_second, table)
    parts = []
    for k in range(n):
        sums, landing = plan[k]
        s = [rest.pop(0) for _ in sums]
        l = [rest.pop(0) for _ in landing]
        parts.append(Scatter(sizes, orders[k], small if k == n - 1 else terms[k], s, l, results[k], send.at[k], recv.at[k]))
    greet(sizes)
    for part in parts:
        part.start(0)
    for phase in range(4):
        for part in parts:
            part.finish(phase)
            if phase < 3:
                part.start(phase + 1)


def scatter_all(sizes, arrays, orders, gain_first, gain_second, table):
    arrays = [a.reshape(sizes + (a.shape[0] // int(np.prod(sizes)), a.shape[1])) for a in arrays]
    blocks = [a.shape[4:] for a in arrays] + [(16, 128)]
    types = [a.dtype for a in arrays] + [F32]
    n = len(blocks)
    plan = [Scatter.shapes(sizes, orders[k], blocks[k]) for k in range(n)]
    scratch = [pltpu.VMEM(sizes + (16, 128), F32)]
    for k in range(n):
        scratch += [pltpu.VMEM(s, types[k]) for s in plan[k][0] + plan[k][1]]
    scratch += [pltpu.SemaphoreType.DMA((n, 4, max(sizes)))] * 2
    vm = pl.BlockSpec(memory_space=pltpu.VMEM)
    return pl.pallas_call(
        functools.partial(scatter_kernel, sizes, orders, plan),
        in_specs=[vm] * (n + 2),
        out_specs=[vm] * n,
        out_shape=[jax.ShapeDtypeStruct(b, F32) for b in blocks],
        scratch_shapes=scratch,
        compiler_params=cp(collective_id=2, has_side_effects=True),
    )(*arrays, gain_first, gain_second, table)


def on_device(devices, inputs, valid_len, norm_first, w_qkv, w_out, relative_bucket_table, norm_second, w_up, w_down, output_gradient):
    S, L, D = inputs.shape
    R = S * L
    owned_rows = D // devices
    fast = devices == 32 and owned_rows == 16
    if fast:
        sizes = device_grid(devices)
        gains = jnp.zeros((16, 128), BF).at[0, :16].set(norm_first).at[1, :16].set(norm_second)
        got = gather_all(sizes, [w_qkv, gains, w_out, w_up, w_down], GATHER_ORDERS)
        wq, wo, wu, wd = [a.reshape(-1, a.shape[-1]) for a in (got[0], got[2], got[3], got[4])]
        both = got[1].reshape(devices, 16, 128)
        g1, g2 = both[:, 0, :16].reshape(1, D), both[:, 1, :16].reshape(1, D)
    else:
        g1, wq, wo, g2, wu, wd = [
            lax.all_gather(a, "dp", axis=0, tiled=True) for a in (norm_first, w_qkv, w_out, norm_second, w_up, w_down)
        ]
        g1, g2 = g1.reshape(1, D), g2.reshape(1, D)
    x = inputs.reshape(R, D)
    og = output_gradient.reshape(R, D)
    n1, qkv = qkv_fwd(x, g1, wq)
    qkv = qkv.reshape(S, L, 3 * D)
    mixed, qa = attn_fwd(valid_len, relative_bucket_table, qkv)
    out, ga, gm, gwo, gwu, gwd, gg2 = ffn(x, mixed.reshape(R, D), og, g2, wo, wu, wd)
    dq, dk, dv, tab = attn_bwd(valid_len, relative_bucket_table, qa, qkv, mixed, gm.reshape(S, L, D))
    gi, gwq, gg1 = qkv_bwd(x, n1, dq.reshape(R, D), dk.reshape(R, D), dv.reshape(R, D), ga, g1, wq)
    if fast:
        rq, ro, ru, rd, small = scatter_all(sizes, [gwq, gwo, gwu, gwd], SCATTER_ORDERS, gg1, gg2, tab)
        first = 16 * lax.rem(lax.axis_index("dp"), 8)
        r1 = lax.dynamic_slice(small[0], (first,), (16,))
        r2 = lax.dynamic_slice(small[1], (first,), (16,))
        rt = small[8:16, :16]
    else:
        rq, ro, ru, rd, r1, r2 = [
            lax.psum_scatter(a.astype(F32), "dp", scatter_dimension=0, tiled=True) for a in (gwq, gwo, gwu, gwd, gg1[0], gg2[0])
        ]
        rt = lax.psum(tab[:, :2, :16].reshape(relative_bucket_table.shape), "dp")
    return (out.reshape(S, L, D), gi.reshape(S, L, D), r1, rq, ro, rt, r2, ru, rd)


GATHER_ORDERS = ((0, 1, 2, 3), (0, 1, 2, 3), (0, 2, 1, 3), (0, 1, 2, 3), (0, 2, 1, 3))
SCATTER_ORDERS = ((3, 2, 1, 0), (3, 1, 2, 0), (3, 2, 1, 0), (3, 1, 2, 0), (3, 2, 1, 0))


def solution(mesh):
    placed = (
        P("dp", None, None), P("dp"), P("dp"), P("dp", None), P("dp", None), P(), P("dp"), P("dp", None), P("dp", None),
        P("dp", None, None),
    )
    return jax.shard_map(
        functools.partial(on_device, mesh.shape["dp"]),
        mesh=mesh,
        in_specs=placed,
        out_specs=(
            P("dp", None, None), P("dp", None, None), P("dp"), P("dp", None), P("dp", None), P(), P("dp"), P("dp", None),
            P("dp", None),
        ),
        check_vma=False,
    )
```

```python
import functools
import itertools

import jax
import jax.numpy as jnp
import numpy as np
from jax import lax
from jax.experimental import pallas as pl
from jax.experimental.pallas import tpu as pltpu
from jax.sharding import PartitionSpec as P

MESH = pl.DeviceIdType.MESH
F32 = jnp.float32
BF = jnp.bfloat16
EPS = 1e-05


def device_grid(devices):
    return (devices // 8, 2, 2, 2)


def grid_position(sizes):
    rest = lax.axis_index("dp")
    place = []
    for size in reversed(sizes):
        place.append(lax.rem(rest, size))
        rest = lax.div(rest, size)
    return tuple(reversed(place))


def flat(place, sizes):
    index = place[0]
    for one, size in zip(place[1:], sizes[1:]):
        index = index * size + one
    return index


def moves(sizes, group):
    return [m for m in itertools.product(*[range(sizes[a]) for a in group]) if any(m)]


def moved(place, sizes, group, move):
    other = list(place)
    for axis, step in zip(group, move):
        if step:
            other[axis] = lax.rem(place[axis] + step, sizes[axis])
    return tuple(other)


def greet(sizes, groups):
    place = grid_position(sizes)
    barrier = pltpu.get_barrier_semaphore()
    count = 0
    for group in groups:
        for move in moves(sizes, group):
            pl.semaphore_signal(
                barrier,
                inc=1,
                device_id=(flat(moved(place, sizes, group, move), sizes),),
                device_id_type=MESH,
            )
            count += 1
    pl.semaphore_wait(barrier, count)


class Gather:
    def __init__(self, sizes, order, own, whole, local_sem, send_sems, recv_sems):
        self.sizes, self.order = sizes, order
        self.own, self.whole = own, whole
        self.local_sem, self.send_sems, self.recv_sems = local_sem, send_sems, recv_sems

    def copies(self, phase):
        place = grid_position(self.sizes)
        done = [a for group in self.order[:phase] for a in group]
        group = self.order[phase]
        part = self.whole.at[tuple(slice(None) if a in done else place[a] for a in range(4))]
        return [
            pltpu.make_async_remote_copy(
                src_ref=self.own if phase == 0 else part,
                dst_ref=part,
                send_sem=self.send_sems.at[phase, k],
                recv_sem=self.recv_sems.at[phase, k],
                device_id=(flat(moved(place, self.sizes, group, move), self.sizes),),
                device_id_type=MESH,
            )
            for k, move in enumerate(moves(self.sizes, group))
        ]

    def local(self):
        return pltpu.make_async_copy(self.own, self.whole.at[grid_position(self.sizes)], self.local_sem)

    def start(self, phase):
        if phase == 0:
            self.local().start()
        for copy in self.copies(phase):
            copy.start()

    def finish(self, phase):
        if phase == 0:
            self.local().wait()
        for copy in self.copies(phase):
            copy.wait()


class Scatter:
    def __init__(self, sizes, order, terms, sums, landing, result, send_sems, recv_sems):
        self.sizes, self.order = sizes, order
        self.held = [terms] + list(sums)
        self.landing, self.result = landing, result
        self.send_sems, self.recv_sems = send_sems, recv_sems

    @staticmethod
    def shapes(sizes, order, block):
        left, sums, landing = set(range(4)), [], []
        for phase, group in enumerate(order):
            left -= set(group)
            lead = tuple(sizes[a] for a in sorted(left))
            slots = int(np.prod([sizes[a] for a in group]))
            landing.append((slots if slots > 2 else 1,) + lead + block)
            if phase < len(order) - 1:
                sums.append(lead + block)
        return sums, landing

    def before(self, phase):
        done = [a for group in self.order[:phase] for a in group]
        return [a for a in range(4) if a not in done]

    def slot(self, phase, place):
        group = self.order[phase]
        if self.landing[phase].shape[0] == 1:
            return 0
        return flat([place[a] for a in group], [self.sizes[a] for a in group])

    def copies(self, phase):
        place = grid_position(self.sizes)
        group = self.order[phase]
        out = []
        for k, move in enumerate(moves(self.sizes, group)):
            other = moved(place, self.sizes, group, move)
            part = tuple(other[a] if a in group else slice(None) for a in self.before(phase))
            out.append(
                pltpu.make_async_remote_copy(
                    src_ref=self.held[phase].at[part],
                    dst_ref=self.landing[phase].at[self.slot(phase, place)],
                    send_sem=self.send_sems.at[phase, k],
                    recv_sem=self.recv_sems.at[phase, k],
                    device_id=(flat(other, self.sizes),),
                    device_id_type=MESH,
                )
            )
        return out

    def start(self, phase):
        for copy in self.copies(phase):
            copy.start()

    def finish(self, phase):
        for copy in self.copies(phase):
            copy.wait()
        place = grid_position(self.sizes)
        group = self.order[phase]
        held, landed = self.held[phase], self.landing[phase]
        before = self.before(phase)
        left = [a for a in before if a not in group]
        last = phase == len(self.order) - 1
        target = self.result if last else self.held[phase + 1]

        def one(at):
            spot = dict(zip(left, at))
            mine = held[tuple(place[a] if a in group else spot[a] for a in before)]
            at = tuple(at)
            if landed.shape[0] == 1:
                total = mine.astype(F32) + landed[(0,) + at].astype(F32)
            else:
                landed[(self.slot(phase, place),) + at] = mine
                total = landed[(0,) + at].astype(F32)
                for source in range(1, landed.shape[0]):
                    total = total + landed[(source,) + at].astype(F32)
            if at:
                target[at] = total.astype(target.dtype)
            else:
                target[...] = total.astype(target.dtype)

        if not left:
            one(())
        else:
            lead = [self.sizes[a] for a in left]

            def body(count, unused):
                at = []
                for size in reversed(lead):
                    at.append(lax.rem(count, size))
                    count = lax.div(count, size)
                one(at[::-1])
                return unused

            lax.fori_loop(0, int(np.prod(lead)), body, 0)


def semaphores(items):
    return [pltpu.SemaphoreType.DMA((items, 4, 16)), pltpu.SemaphoreType.DMA((items, 4, 16))]


def run_schedule(step, schedule, parts):
    for at, actions in sorted(schedule.items()):

        @pl.when(step == at)
        def _(actions=actions):
            for action, item, phase in actions:
                getattr(parts[item], action)(phase)


LOW=(0,1,2,3,4,5,6,7,8,12,16,32,64,128,256,512)
T=256
NEG=-1e30
def cp(**k): return pltpu.CompilerParams(vmem_limit_bytes=56*2**20, **k)
def dot_nt(a,b): return lax.dot_general(a,b,(((1,),(1,)),((),())),preferred_element_type=jnp.float32)
def dot_nn(a,b): return jnp.dot(a,b,preferred_element_type=jnp.float32)
def dot_tn(a,b): return lax.dot_general(a,b,(((0,),(0,)),((),())),preferred_element_type=jnp.float32)

def bias_of(dist, row):
    out=jnp.zeros(dist.shape,jnp.float32)+row[:,0:1]
    for b in range(1,16):
        out=jnp.where(dist>=LOW[b],row[:,b:b+1],out)
    return jnp.where(dist<0,NEG,out)

def table_row(table_ref,head):
    whole=table_ref[...].astype(jnp.float32)
    at=lax.broadcasted_iota(jnp.int32,whole.shape,0)
    return jnp.sum(jnp.where(at==head,whole,0.0),axis=0,keepdims=True)

def build_bias(table_ref, hp, bias, transposed):
    lane=lax.broadcasted_iota(jnp.int32,(1,2*T),1)
    m=jnp.where(lane<T,lane,lane-2*T)
    for h in range(2):
        row=table_row(table_ref,2*hp+h)
        for bd in range(3):
            w=bias_of(bd*T+(m if transposed else -m),row)
            tile=pltpu.roll(jnp.broadcast_to(w,(T,2*T)),0,1,stride=1,stride_axis=0)
            bias[h,bd]=tile[:,:T]
        bias[h,3]=jnp.broadcast_to(row[:,15:16],(T,T))

def split3(v):
    hi=v.astype(jnp.bfloat16); r=v-hi.astype(jnp.float32)
    mid=r.astype(jnp.bfloat16); lo=(r-mid.astype(jnp.float32)).astype(jnp.bfloat16)
    return hi,mid,lo

def halves(h, main, extra, rows):
    lane=lax.broadcasted_iota(jnp.int32,(rows,128),1)
    out=jnp.where((lane//64)==h,main,jnp.zeros((),main.dtype))
    base=64*(1-h)
    for n,e in enumerate(extra):
        if e is not None:
            out=jnp.where(lane==base+n,jnp.broadcast_to(e,(rows,128)).astype(jnp.bfloat16),out)
    return out

def ln_parts(v):
    c=v-jnp.mean(v,axis=1,keepdims=True)
    r=lax.rsqrt(jnp.mean(c*c,axis=1,keepdims=True)+EPS)
    return c*r, r
def ln_back(e_in,gain,xhat,r):
    e=e_in*gain
    gv=r*(e-jnp.mean(e,axis=1,keepdims=True)-xhat*jnp.mean(e*xhat,axis=1,keepdims=True))
    return (gv,)

def ffn_kernel(x_ref,m_ref,og_ref,g_ref,wo_ref,wu_ref,wd_ref,out_ref,ga_ref,gm_ref,gwo_ref,gwu_ref,gwd_ref,ao,au,ad):
    i=pl.program_id(0)
    m=m_ref[...]; og=og_ref[...]
    after=x_ref[...].astype(F32)+dot_nn(m,wo_ref[...])
    xhat,r=ln_parts(after)
    gain=g_ref[...].astype(F32)
    n=(xhat*gain).astype(BF)
    pre=dot_nn(n,wu_ref[...])
    dh=dot_nt(og,wd_ref[...])
    c=0.7978845608028654
    sq=pre*pre
    t=jnp.tanh(pre*(c+c*0.044715*sq))
    half=0.5*(1.0+t)
    hid=(pre*half).astype(BF)
    dg=half+(0.5*pre)*(1.0-t*t)*(c+3*c*0.044715*sq)
    gp=(dh*dg).astype(BF)
    out_ref[...]=(after+dot_nn(hid,wd_ref[...])).astype(BF)
    pd=dot_tn(hid,og); pu=dot_tn(n,gp)
    dn=dot_nt(gp,wu_ref[...])
    (gv,)=ln_back(dn,gain,xhat,r)
    ga=og.astype(F32)+gv
    ga_ref[...]=ga
    gb=ga.astype(BF)
    po=dot_tn(m,gb)
    gm_ref[...]=dot_nt(gb,wo_ref[...]).astype(BF)
    @pl.when(i==0)
    def _():
        ad[...]=pd; au[...]=pu; ao[...]=po
    @pl.when(i>0)
    def _():
        ad[...]+=pd; au[...]+=pu; ao[...]+=po
    @pl.when(i==pl.num_programs(0)-1)
    def _():
        gwo_ref[...]=ao[...].astype(BF); gwu_ref[...]=au[...].astype(BF); gwd_ref[...]=ad[...].astype(BF)
def ffn(x,m,og,gain,wo,wu,wd,B=512):
    R,D=x.shape; FF=wu.shape[1]
    row=pl.BlockSpec((B,D),lambda i:(i,0))
    full=lambda a,b:pl.BlockSpec((a,b),lambda i:(0,0))
    return pl.pallas_call(ffn_kernel,grid=(R//B,),
      in_specs=[row,row,row,full(1,D),full(D,D),full(D,FF),full(FF,D)],
      out_specs=[row,row,row,full(D,D),full(D,FF),full(FF,D)],
      out_shape=[jax.ShapeDtypeStruct((R,D),BF),jax.ShapeDtypeStruct((R,D),F32),jax.ShapeDtypeStruct((R,D),BF),
        jax.ShapeDtypeStruct((D,D),BF),jax.ShapeDtypeStruct((D,FF),BF),jax.ShapeDtypeStruct((FF,D),BF)],
      scratch_shapes=[pltpu.VMEM((D,D),F32),pltpu.VMEM((D,FF),F32),pltpu.VMEM((FF,D),F32)],
      compiler_params=cp())(x,m,og,gain,wo,wu,wd)


SPREAD = ((0, 1, 2), (3,))
GATHER_ORDERS = {
    "gains": SPREAD, "q0": SPREAD, "q1": SPREAD,
    "q2": ((0,), (1,), (2,), (3,)), "q3": ((0,), (2,), (1,), (3,)),
    "out": ((0,), (1,), (2,), (3,)), "up": ((0,), (1,), (2,), (3,)), "down": ((0,), (2,), (1,), (3,)),
}
GATHER_SCHEDULE = {
    1: [("finish", "q1", 0), ("start", "q1", 1), ("finish", "q2", 0), ("start", "q2", 1), ("finish", "up", 0), ("start", "up", 1), ("start", "out", 0)],
    2: [("finish", "q1", 1), ("finish", "q2", 1), ("start", "q2", 2), ("finish", "down", 0), ("start", "down", 1), ("start", "q3", 0), ("finish", "up", 1), ("start", "up", 2)],
    3: [("finish", "q2", 2), ("start", "q2", 3), ("finish", "out", 0), ("start", "out", 1), ("finish", "q3", 0), ("start", "q3", 1), ("finish", "down", 1), ("start", "down", 2)],
    4: [("finish", "q2", 3), ("finish", "q3", 1), ("start", "q3", 2), ("finish", "out", 1), ("start", "out", 2)],
    5: [("finish", "q3", 2), ("start", "q3", 3), ("finish", "up", 2), ("start", "up", 3), ("finish", "out", 2), ("start", "out", 3)],
    6: [("finish", "q3", 3), ("finish", "down", 2), ("start", "down", 3)],
    7: [("finish", "up", 3), ("finish", "out", 3)],
}


def first_kernel(sizes, *refs):
    remote = sizes is not None
    refs = list(refs)
    take = lambda count: [refs.pop(0) for _ in range(count)]
    vl_ref, table_ref, x_ref = take(3)
    if remote:
        gains_own, wq_own, wo_own, wu_own, wd_own = take(5)
    else:
        g_ref, w_ref = take(2)
    mixed_ref, qa_ref, qkv_ref, n_ref = take(4)
    if remote:
        g1_ref, g2_ref, wq_out, wo_ref, wu_ref, wd_ref = take(6)
    bias, xhat = take(2)
    hp = pl.program_id(0)
    s = pl.program_id(1)
    pairs = pl.num_programs(0)
    S, L = qkv_ref.shape[1:3]
    step = hp * S + s
    R, D = x_ref.shape
    B = 512
    if remote:
        q_own, wq, gains, local, send, recv, out_sem = take(7)
        names = list(GATHER_ORDERS)
        own = dict(gains=gains_own, out=wo_own, up=wu_own, down=wd_own)
        whole = dict(gains=gains, out=wo_ref, up=wu_ref, down=wd_ref)
        for pair in range(4):
            own["q%d" % pair], whole["q%d" % pair] = q_own.at[pair], wq.at[pair]
        parts = {
            name: Gather(sizes, GATHER_ORDERS[name], own[name], whole[name], local.at[k], send.at[k], recv.at[k])
            for k, name in enumerate(names)
        }
        out_copy = lambda pair: pltpu.make_async_copy(wq.at[pair], wq_out.at[pair], out_sem.at[pair])

    @pl.when(step == 0)
    def _():
        if remote:
            for pair in range(4):
                for part in range(3):
                    q_own[pair, :, part * 128:(part + 1) * 128] = wq_own[:, (part * 4 + pair) * 128:(part * 4 + pair + 1) * 128]
            greet(sizes, SPREAD)
            parts["q0"].start(0)
            parts["gains"].start(0)

        def norm(block, unused):
            at = pl.ds(pl.multiple_of(block * B, B), B)
            xhat[at, :] = ln_parts(x_ref[at, :].astype(F32))[0]
            return unused

        lax.fori_loop(0, R // B, norm, 0)
        if remote:
            parts["gains"].finish(0)
            parts["q0"].finish(0)
            parts["gains"].start(1)
            parts["q0"].start(1)
            parts["q1"].start(0)
            parts["q2"].start(0)
            parts["up"].start(0)
            parts["down"].start(0)
            parts["gains"].finish(1)
            tiles = []
            for z in range(sizes[0]):
                tile = jnp.zeros((16, 128), F32)
                for y, a, c in itertools.product(*[range(size) for size in sizes[1:]]):
                    tile = tile + gains[z, y, a, c].astype(F32)
                tiles.append(tile)
            tile = jnp.concatenate(tiles, axis=1)
            g1_ref[...] = tile[0:1, :]
            g2_ref[...] = tile[1:2, :]
            gain = tile[0:1, :]
        else:
            gain = g_ref[...]

        def scale(block, unused):
            at = pl.ds(pl.multiple_of(block * B, B), B)
            n_ref[at, :] = (xhat[at, :] * gain).astype(BF)
            return unused

        lax.fori_loop(0, R // B, scale, 0)
        if remote:
            parts["q0"].finish(1)

    if remote:
        run_schedule(step, GATHER_SCHEDULE, parts)

    @pl.when(s == 0)
    def _():
        build_bias(table_ref, hp, bias, False)
        weights = wq[hp].reshape(D, 384) if remote else w_ref[0]
        if remote:
            out_copy(hp).start()
        for seq in range(S):
            for half in range(L // B):
                row = seq * L + half * B
                qkv_ref[0, seq, half * B:(half + 1) * B, :] = dot_nn(n_ref[row:row + B, :], weights).astype(BF)

    attend(vl_ref[s], qkv_ref.at[0, s], mixed_ref.at[0], qa_ref.at[0, 0], bias)

    if remote:

        @pl.when(step == pairs * S - 1)
        def _():
            parts["down"].finish(3)
            for pair in range(4):
                out_copy(pair).wait()


def attend(valid, qkv_ref, mixed_ref, qa_ref, bias):
    L = qkv_ref.shape[0]
    nb = L // T
    key = lax.broadcasted_iota(jnp.int32, (L, 1), 0)
    mask = jnp.where(key < valid, 0.0, NEG)
    lane = lax.broadcasted_iota(jnp.int32, (T, 128), 1)
    ks = [halves(h, qkv_ref[:, 128:256], [1.0, 1.0, 1.0, mask], L) for h in range(2)]
    v = qkv_ref[:, 256:384]
    for qb in range(nb):
        kk = (qb + 1) * T
        qt = qkv_ref[qb * T:(qb + 1) * T, 0:128] * jnp.asarray(0.125, BF)
        outs = []
        for h in range(2):
            qh = halves(h, qt, [None, None, None, 1.0], T)
            sc = dot_nt(qh, ks[h][:kk])
            sc = jnp.concatenate([sc[:, kb * T:(kb + 1) * T] + bias[h, qb - kb] for kb in range(qb + 1)], axis=1)
            mx = jnp.max(sc, axis=1, keepdims=True)
            p = jnp.exp(sc - mx)
            l = jnp.sum(p, axis=1, keepdims=True)
            o = dot_nn(p.astype(BF), v[:kk])
            outs.append(o * (1.0 / l))
            hi, mid, lo = split3(-(mx + jnp.log(l)))
            qa_ref[h, qb * T:(qb + 1) * T, :] = halves(h, qt, [hi, mid, lo, 1.0], T)
        mixed_ref[qb * T:(qb + 1) * T, :] = jnp.where(lane < 64, outs[0], outs[1]).astype(BF)


def whole_block(shape):
    return pl.BlockSpec(shape, lambda *unused: (0,) * len(shape))


def first_half(sizes, vl, table, x, S, weights):
    R, D = x.shape
    L = R // S
    HP = D // 128
    remote = sizes is not None
    anyspace = pl.BlockSpec(memory_space=pl.ANY)
    in_specs = [pl.BlockSpec(memory_space=pltpu.SMEM), whole_block(table.shape), whole_block((R, D))]
    out_specs = [
        pl.BlockSpec((1, L, 128), lambda h, s: (s, 0, h)),
        pl.BlockSpec((1, 1, 2, L, 128), lambda h, s: (s, h, 0, 0, 0)),
        pl.BlockSpec((1, S, L, 384), lambda h, s: (h, 0, 0, 0)),
        whole_block((R, D)),
    ]
    out_shape = [
        jax.ShapeDtypeStruct((S, L, D), BF),
        jax.ShapeDtypeStruct((S, HP, 2, L, 128), BF),
        jax.ShapeDtypeStruct((HP, S, L, 384), BF),
        jax.ShapeDtypeStruct((R, D), BF),
    ]
    scratch = [pltpu.VMEM((2, 4, T, T), F32), pltpu.VMEM((R, D), F32)]
    if remote:
        gains, wq, wo, wu, wd = weights
        in_specs += [whole_block(gains.shape), whole_block(wq.shape), anyspace, anyspace, anyspace]
        out_specs += [whole_block((1, D)), whole_block((1, D))] + [anyspace] * 4
        out_shape += [jax.ShapeDtypeStruct((1, D), F32)] * 2
        out_shape += [jax.ShapeDtypeStruct((HP,) + sizes + (16, 384), BF)]
        out_shape += [jax.ShapeDtypeStruct(sizes + w.shape, BF) for w in (wo, wu, wd)]
        scratch += [
            pltpu.VMEM((HP, 16, 384), BF),
            pltpu.VMEM((HP,) + sizes + (16, 384), BF),
            pltpu.VMEM(sizes + (16, 128), BF),
            pltpu.SemaphoreType.DMA((len(GATHER_ORDERS),)),
        ] + semaphores(len(GATHER_ORDERS)) + [pltpu.SemaphoreType.DMA((HP,))]
        params = cp(collective_id=1, has_side_effects=True)
    else:
        gain, wq = weights
        in_specs += [whole_block((1, D)), pl.BlockSpec((1, D, 384), lambda h, s: (h, 0, 0))]
        params = cp()
    return pl.pallas_call(
        functools.partial(first_kernel, sizes), grid=(HP, S), in_specs=in_specs, out_specs=out_specs, out_shape=out_shape,
        scratch_shapes=scratch, compiler_params=params,
    )(vl, table, x, *weights)


SCATTER_ORDERS = {
    "out": ((3,), (2,), (1,), (0,)), "up": ((3,), (2,), (1,), (0,)), "down": ((3,), (1,), (2,), (0,)),
    "q0": ((3,), (1,), (2,), (0,)), "q1": ((3,), (2,), (1,), (0,)), "q2": ((3,), (1,), (2,), (0,)), "q3": ((3,), (0, 1, 2)),
}
SCATTER_SCHEDULE = {
    0: [("start", "up", 0), ("start", "down", 0), ("start", "out", 0)],
    1: [("finish", "up", 0), ("start", "up", 1), ("finish", "down", 0), ("start", "down", 1), ("finish", "out", 0), ("start", "out", 1)],
    2: [("start", "q0", 0)],
    3: [("finish", "q0", 0), ("start", "q0", 1), ("finish", "out", 1), ("start", "out", 2)],
    4: [("finish", "up", 1), ("start", "up", 2), ("finish", "down", 1), ("start", "down", 2), ("start", "q1", 0), ("finish", "out", 2), ("start", "out", 3)],
    5: [("finish", "q1", 0), ("start", "q1", 1), ("finish", "q0", 1), ("start", "q0", 2)],
    6: [("finish", "up", 2), ("start", "up", 3), ("finish", "down", 2), ("start", "down", 3), ("start", "q2", 0), ("finish", "out", 3)],
    7: [("finish", "q1", 1), ("start", "q1", 2), ("finish", "q2", 0), ("start", "q2", 1), ("finish", "q0", 2), ("start", "q0", 3)],
    8: [("start", "q3", 0), ("start", "table", 0), ("finish", "q2", 1), ("start", "q2", 2), ("finish", "q1", 2), ("start", "q1", 3)],
    9: [("finish", "q3", 0), ("start", "q3", 1), ("finish", "table", 0), ("start", "table", 1), ("finish", "up", 3), ("finish", "q0", 3)],
    10: [("finish", "q2", 2), ("start", "q2", 3), ("finish", "down", 3), ("finish", "table", 1)],
    11: [("finish", "q1", 3)],
}
SCATTER_TAIL = [("finish", "q2", 3), ("finish", "q3", 1)]


def last_kernel(sizes, plan, *refs):
    remote = sizes is not None
    refs = list(refs)
    take = lambda count: [refs.pop(0) for _ in range(count)]
    vl_ref, table_ref, qa_ref, qkv_ref, o_ref, g_ref, n_ref, w_ref, gain_ref, x_ref, ga_ref = take(11)
    if remote:
        wo_terms, wu_terms, wd_terms = take(3)
    gi_ref, tab_ref = take(2)
    if remote:
        results = dict(zip(SCATTER_ORDERS, take(7)))
    else:
        (gw_ref,) = take(1)
    bias, gacc, far, dqt, grads = take(5)
    t = pl.program_id(0)
    pairs = grads.shape[0]
    S = grads.shape[1] // qkv_ref.shape[2]
    steps = pairs * S
    hp = lax.div(t, S)
    s = lax.rem(t, S)
    L = qkv_ref.shape[2]
    R = S * L
    D = x_ref.shape[1]
    if remote:
        wq_terms, tab_own, tab_all, local = take(4)
        terms = dict(out=wo_terms, up=wu_terms, down=wd_terms)
        for pair in range(4):
            terms["q%d" % pair] = wq_terms.at[pair]
        send, recv = refs[-2:]
        parts = {}
        for k, name in enumerate(SCATTER_ORDERS):
            sums, landing = plan[name]
            parts[name] = Scatter(
                sizes, SCATTER_ORDERS[name], terms[name], take(len(sums)), take(len(landing)), results[name], send.at[k], recv.at[k]
            )
        parts["table"] = Gather(sizes, SPREAD, tab_own, tab_all, local, send.at[len(plan)], recv.at[len(plan)])

        @pl.when(t == 0)
        def _():
            greet(sizes, SPREAD)

        run_schedule(t, SCATTER_SCHEDULE, parts)

    @pl.when(t < steps)
    def _():
        @pl.when(s == 0)
        def _():
            build_bias(table_ref, hp, bias, True)
            gacc[...] = jnp.zeros_like(gacc)
            far[...] = jnp.zeros_like(far)

        at = pl.multiple_of(s * L, L)
        attend_back(vl_ref[s], qa_ref.at[0, 0], qkv_ref.at[0, 0], o_ref[0], g_ref[0], grads, hp, at, bias, gacc, far, dqt)

        @pl.when(s == S - 1)
        def _():
            rows = table_terms(gacc, far)
            place = pl.ds(pl.multiple_of(hp * 8, 8), 8)
            (tab_own if remote else tab_ref)[place, :] = rows
            for part in range(3):
                gw = dot_tn(n_ref[...], grads[hp, :, part * 128:(part + 1) * 128]).astype(BF)
                if remote:
                    wq_terms[hp, :, :, :, :, :, part * 128:(part + 1) * 128] = gw.reshape(sizes + (16, 128))
                else:
                    gw_ref[hp, :, part * 128:(part + 1) * 128] = gw

    @pl.when(t >= steps)
    def _():
        B = x_ref.shape[0]
        at = pl.ds(pl.multiple_of((t - steps) * B, B), B)
        xhat, r = ln_parts(x_ref[...].astype(F32))
        dn = None
        for pair in range(pairs):
            weights = w_ref[pair]
            term = dot_nt(grads[pair, at, :], weights)
            dn = term if dn is None else dn + term
        gi_ref[...] = (ga_ref[...] + ln_back(dn, gain_ref[...], xhat, r)[0]).astype(BF)

    if remote:

        @pl.when(t == pl.num_programs(0) - 1)
        def _():
            for action, item, phase in SCATTER_TAIL:
                getattr(parts[item], action)(phase)
            total = None
            for at in itertools.product(*[range(size) for size in sizes]):
                block = tab_all[at]
                total = block if total is None else total + block
            tab_ref[...] = total


def table_terms(gacc, far):
    lane2 = lax.broadcasted_iota(jnp.int32, (1, 2 * T), 1)
    m = jnp.where(lane2 < T, lane2, lane2 - 2 * T)
    bl = lax.broadcasted_iota(jnp.int32, (1, 128), 1)
    rows = []
    for h in range(2):
        row = jnp.where(bl == 15, jnp.sum(far[h:h + 1, :], axis=1, keepdims=True), 0.0)
        for bd in range(3):
            w = jnp.concatenate([gacc[h, bd], jnp.zeros((T, T), F32)], axis=1)
            acc = w[:8]
            for a in range(1, T // 8):
                acc = acc + pltpu.roll(w[8 * a:8 * a + 8], 2 * T - 8 * a, 1)
            diag = acc[0:1]
            for a in range(1, 8):
                diag = diag + pltpu.roll(acc[a:a + 1], 2 * T - a, 1)
            dist = bd * T + m
            for b in range(16):
                if LOW[b] >= (bd + 1) * T or (b < 15 and LOW[b + 1] <= (bd - 1) * T):
                    continue
                sel = dist >= LOW[b]
                if b < 15:
                    sel = sel & (dist < LOW[b + 1])
                row = row + jnp.where(bl == b, jnp.sum(jnp.where(sel, diag, 0.0), axis=1, keepdims=True), 0.0)
        rows.append(row)
    return jnp.concatenate(rows + [jnp.zeros((6, 128), F32)], axis=0)


def attend_back(valid, qa_ref, qkv_ref, o, g, grads, hp, first, bias, gacc, far, dqt):
    L = qkv_ref.shape[0]
    nb = L // T
    key = lax.broadcasted_iota(jnp.int32, (L, 1), 0)
    mask = jnp.where(key < valid, 0.0, NEG)
    lane = lax.broadcasted_iota(jnp.int32, (T, 128), 1)
    prod = g.astype(F32) * o.astype(F32)
    lane_l = lax.broadcasted_iota(jnp.int32, (L, 128), 1)
    k = qkv_ref[:, 128:256]
    ks = [halves(h, k, [1.0, 1.0, 1.0, mask], L) for h in range(2)]
    vs = [halves(h, qkv_ref[:, 256:384], [1.0, 1.0, 1.0], L) for h in range(2)]
    gs = []
    for h in range(2):
        d = jnp.sum(jnp.where((lane_l // 64) == h, prod, 0.0), axis=1, keepdims=True)
        hi, mid, lo = split3(-d)
        gs.append(halves(h, g, [hi, mid, lo], L))
    kt = (k * jnp.asarray(0.125, BF)).T
    for kb in range(nb):
        dks, dvs = [], []
        for h in range(2):
            qh = qa_ref[h]
            st = dot_nt(ks[h][kb * T:(kb + 1) * T], qh[kb * T:])
            dp = dot_nt(vs[h][kb * T:(kb + 1) * T], gs[h][kb * T:])
            st = jnp.concatenate([st[:, i * T:(i + 1) * T] + bias[h, i] for i in range(nb - kb)], axis=1)
            p = jnp.exp(st)
            ds = p * dp
            pb = p.astype(BF)
            dsb = ds.astype(BF)
            dvs.append(dot_nn(pb, gs[h][kb * T:]))
            dks.append(dot_nn(dsb, qh[kb * T:]))
            for i in range(min(nb - kb, 3)):
                gacc[h, i] += ds[:, i * T:(i + 1) * T]
            if nb - kb > 3:
                far[h:h + 1, :] += jnp.sum(ds[:, 3 * T:], axis=0, keepdims=True)
            r = dot_nn(kt[h * 64:(h + 1) * 64, kb * T:(kb + 1) * T], dsb)
            if kb == 0:
                dqt[h * 64:(h + 1) * 64, :] = r
            else:
                dqt[h * 64:(h + 1) * 64, kb * T:] += r
        at = pl.ds(first + kb * T, T)
        grads[hp, at, 128:256] = jnp.where(lane < 64, dks[0], dks[1]).astype(BF)
        grads[hp, at, 256:384] = jnp.where(lane < 64, dvs[0], dvs[1]).astype(BF)
    grads[hp, pl.ds(first, L), 0:128] = dqt[...].T.astype(BF)


def last_half(sizes, vl, table, qa, qkv, mixed, gm, n1, wq, gain, x, ga, ffn_grads):
    HP, S, L, W = qkv.shape
    R, D = x.shape
    B = 512
    steps = HP * S
    remote = sizes is not None
    pair = lambda t: jnp.minimum(t, steps - 1) // S
    seq = lambda t: jnp.minimum(t, steps - 1) % S
    late = pl.BlockSpec((B, D), lambda t: (jnp.maximum(t - steps, 0), 0))
    in_specs = [
        pl.BlockSpec(memory_space=pltpu.SMEM),
        whole_block(table.shape),
        pl.BlockSpec((1, 1, 2, L, 128), lambda t: (seq(t), pair(t), 0, 0, 0)),
        pl.BlockSpec((1, 1, L, W), lambda t: (pair(t), seq(t), 0, 0)),
        pl.BlockSpec((1, L, 128), lambda t: (seq(t), 0, pair(t))),
        pl.BlockSpec((1, L, 128), lambda t: (seq(t), 0, pair(t))),
        whole_block((R, D)),
        whole_block((HP, D, W)),
        whole_block((1, D)),
        late,
        late,
    ]
    out_specs = [late, whole_block((8 * HP, 128))]
    out_shape = [jax.ShapeDtypeStruct((R, D), BF), jax.ShapeDtypeStruct((8 * HP, 128), F32)]
    scratch = [
        pltpu.VMEM((2, 4, T, T), F32), pltpu.VMEM((2, 3, T, T), F32), pltpu.VMEM((8, T), F32), pltpu.VMEM((128, L), F32),
        pltpu.VMEM((HP, R, W), BF),
    ]
    args = [vl, table, qa, qkv, mixed, gm, n1, wq, gain, x, ga]
    plan = None
    if remote:
        count = int(np.prod(sizes))
        terms = [a.reshape(sizes + (a.shape[0] // count, a.shape[1])) for a in ffn_grads]
        args += terms
        in_specs += [whole_block(a.shape) for a in terms]
        blocks = dict(zip(("out", "up", "down"), [a.shape[4:] for a in terms]))
        for k in range(HP):
            blocks["q%d" % k] = (16, W)
        plan = {name: Scatter.shapes(sizes, SCATTER_ORDERS[name], blocks[name]) for name in SCATTER_ORDERS}
        out_specs += [whole_block(blocks[name]) for name in SCATTER_ORDERS]
        out_shape += [jax.ShapeDtypeStruct(blocks[name], F32) for name in SCATTER_ORDERS]
        scratch += [
            pltpu.VMEM((HP,) + sizes + (16, W), BF), pltpu.VMEM((8 * HP, 128), F32), pltpu.VMEM(sizes + (8 * HP, 128), F32),
            pltpu.SemaphoreType.DMA,
        ]
        for name in SCATTER_ORDERS:
            scratch += [pltpu.VMEM(shape, BF) for shape in plan[name][0] + plan[name][1]]
        scratch += semaphores(len(SCATTER_ORDERS) + 1)
        params = cp(collective_id=2, has_side_effects=True)
    else:
        out_specs += [whole_block((HP, D, W))]
        out_shape += [jax.ShapeDtypeStruct((HP, D, W), BF)]
        params = cp()
    return pl.pallas_call(
        functools.partial(last_kernel, sizes, plan), grid=(steps + R // B,), in_specs=in_specs, out_specs=out_specs,
        out_shape=out_shape, scratch_shapes=scratch, compiler_params=params,
    )(*args)


def finish_kernel(*refs):
    refs = list(refs)
    take = lambda count: [refs.pop(0) for _ in range(count)]
    tab_ref, ro_ref, ru_ref, rd_ref = take(4)
    pieces = take(4)
    gains_ref, wq_ref, wu_ref = take(3)
    tab_out, wq_out, wo_out, wu_out, wd_out, g1_out, g2_out = refs
    table = jnp.concatenate([tab_ref[8 * pair:8 * pair + 2, :] for pair in range(4)], axis=0)
    tab_out[...] = table[:, :16]
    wo_out[...] = ro_ref[...]
    wu_out[...] = ru_ref[...]
    wd_out[...] = rd_ref[...]
    for pair in range(4):
        for part in range(3):
            wq_out[:, (part * 4 + pair) * 128:(part * 4 + pair + 1) * 128] = pieces[pair][:, part * 128:(part + 1) * 128]
    lane = lax.broadcasted_iota(jnp.int32, (16, 128), 1)
    row = lax.broadcasted_iota(jnp.int32, (16, 128), 0)
    own = lane == row + 16 * lax.rem(lax.axis_index("dp"), 8)
    square = lax.broadcasted_iota(jnp.int32, (16, 16), 0) == lax.broadcasted_iota(jnp.int32, (16, 16), 1)
    gains = gains_ref[...].astype(F32)
    for k, (w, grad, out) in enumerate(((wq_ref, wq_out, g1_out), (wu_ref, wu_out, g2_out))):
        gain = jnp.sum(jnp.where(own, gains[k:k + 1, :], 0.0), axis=1, keepdims=True)
        dots = jnp.sum(w[...].astype(F32) * grad[...], axis=1, keepdims=True)
        out[...] = jnp.sum(jnp.where(square, dots / gain, 0.0), axis=0, keepdims=True)


def finish(tab, results, gains, wq, wu):
    ro, ru, rd = results[:3]
    out_shape = [
        jax.ShapeDtypeStruct((8, 16), F32), jax.ShapeDtypeStruct(wq.shape, F32), jax.ShapeDtypeStruct(ro.shape, F32),
        jax.ShapeDtypeStruct(ru.shape, F32), jax.ShapeDtypeStruct(rd.shape, F32), jax.ShapeDtypeStruct((1, 16), F32),
        jax.ShapeDtypeStruct((1, 16), F32),
    ]
    return pl.pallas_call(finish_kernel, out_shape=out_shape, compiler_params=cp())(tab, *results, gains, wq, wu)


def on_device(devices, inputs, valid_len, norm_first, w_qkv, w_out, relative_bucket_table, norm_second, w_up, w_down, output_gradient):
    S, L, D = inputs.shape
    R = S * L
    HP = D // 128
    FFW = w_up.shape[1]
    fast = devices == 32 and D == 512 and S == 2
    table = relative_bucket_table
    x = inputs.reshape(R, D)
    og = output_gradient.reshape(R, D)
    by_pair = lambda w: w.reshape(D, 3, HP, 128).transpose(2, 0, 1, 3).reshape(HP, D, 384)
    if fast:
        sizes = device_grid(devices)
        mine = jnp.arange(128) // 16 == lax.rem(lax.axis_index("dp"), 8)
        place = lambda g: jnp.where(mine, jnp.tile(g, 8), jnp.zeros((), BF))
        row = jnp.arange(16)[:, None]
        gains = jnp.where(row == 0, place(norm_first), jnp.where(row == 1, place(norm_second), jnp.zeros((), BF)))
        mixed, qa, qkv, n1, g1, g2, wq, wo, wu, wd = first_half(
            sizes, valid_len, table, x, S, [gains, w_qkv, w_out, w_up, w_down]
        )
        wq, wo, wu, wd = wq.reshape(HP, D, 384), wo.reshape(D, D), wu.reshape(D, FFW), wd.reshape(FFW, D)
    else:
        sizes = None
        g1, wq, wo, g2, wu, wd = [
            lax.all_gather(a, "dp", axis=0, tiled=True) for a in (norm_first, w_qkv, w_out, norm_second, w_up, w_down)
        ]
        g1, g2 = g1.reshape(1, D).astype(F32), g2.reshape(1, D).astype(F32)
        wq = by_pair(wq)
        mixed, qa, qkv, n1 = first_half(None, valid_len, table, x, S, [g1, wq])
    out, ga, gm, gwo, gwu, gwd = ffn(x, mixed.reshape(R, D), og, g2, wo, wu, wd)
    got = last_half(
        sizes, valid_len, table, qa, qkv, mixed, gm.reshape(S, L, D), n1, wq, g1, x, ga, [gwo, gwu, gwd]
    )
    gi, tab = got[:2]
    if fast:
        rt, rq, ro, ru, rd, r1, r2 = finish(tab, got[2:], gains, w_qkv, w_up)
        r1, r2 = r1.reshape(-1), r2.reshape(-1)
    else:
        gwq = got[2].reshape(HP, D, 3, 128).transpose(1, 2, 0, 3).reshape(D, 3 * D)
        rq, ro, ru, rd = [
            lax.psum_scatter(a.astype(F32), "dp", scatter_dimension=0, tiled=True) for a in (gwq, gwo, gwu, gwd)
        ]
        r1 = jnp.sum(w_qkv.astype(F32) * rq, axis=1) / norm_first.astype(F32)
        r2 = jnp.sum(w_up.astype(F32) * ru, axis=1) / norm_second.astype(F32)
        rt = lax.psum(tab.reshape(HP, 8, 128)[:, :2, :16].reshape(table.shape), "dp")
    return (out.reshape(S, L, D), gi.reshape(S, L, D), r1, rq, ro, rt, r2, ru, rd)


def solution(mesh):
    placed = (
        P("dp", None, None), P("dp"), P("dp"), P("dp", None), P("dp", None), P(), P("dp"), P("dp", None), P("dp", None),
        P("dp", None, None),
    )
    return jax.shard_map(
        functools.partial(on_device, mesh.shape["dp"]),
        mesh=mesh,
        in_specs=placed,
        out_specs=(
            P("dp", None, None), P("dp", None, None), P("dp"), P("dp", None), P("dp", None), P(), P("dp"), P("dp", None),
            P("dp", None),
        ),
        check_vma=False,
    )
```

```python
import functools
import itertools

import jax
import jax.numpy as jnp
import numpy as np
from jax import lax
from jax.experimental import pallas as pl
from jax.experimental.pallas import tpu as pltpu
from jax.sharding import PartitionSpec as P

MESH = pl.DeviceIdType.MESH
F32 = jnp.float32
BF = jnp.bfloat16
EPS = 1e-05


def device_grid(devices):
    return (devices // 8, 2, 2, 2)


def grid_position(sizes):
    rest = lax.axis_index("dp")
    place = []
    for size in reversed(sizes):
        place.append(lax.rem(rest, size))
        rest = lax.div(rest, size)
    return tuple(reversed(place))


def flat(place, sizes):
    index = place[0]
    for one, size in zip(place[1:], sizes[1:]):
        index = index * size + one
    return index


def moves(sizes, group):
    return [m for m in itertools.product(*[range(sizes[a]) for a in group]) if any(m)]


def moved(place, sizes, group, move):
    other = list(place)
    for axis, step in zip(group, move):
        if step:
            other[axis] = lax.rem(place[axis] + step, sizes[axis])
    return tuple(other)


def greet(sizes, groups):
    place = grid_position(sizes)
    barrier = pltpu.get_barrier_semaphore()
    for group in groups:
        for move in moves(sizes, group):
            pl.semaphore_signal(
                barrier,
                inc=1,
                device_id=(flat(moved(place, sizes, group, move), sizes),),
                device_id_type=MESH,
            )


def await_greetings(sizes, groups):
    pl.semaphore_wait(pltpu.get_barrier_semaphore(), sum(len(moves(sizes, group)) for group in groups))


class Gather:
    def __init__(self, sizes, order, own, whole, local_sem, send_sems, recv_sems, first):
        self.sizes, self.order, self.first = sizes, order, first
        self.own, self.whole = own, whole
        self.local_sem, self.send_sems, self.recv_sems = local_sem, send_sems, recv_sems

    def copies(self, phase):
        place = grid_position(self.sizes)
        done = [a for group in self.order[:phase] for a in group]
        group = self.order[phase]
        part = self.whole.at[tuple(slice(None) if a in done else place[a] for a in range(4))]
        return [
            pltpu.make_async_remote_copy(
                src_ref=self.own if phase == 0 else part,
                dst_ref=part,
                send_sem=self.send_sems.at[self.first + sum(len(moves(self.sizes, g)) for g in self.order[:phase]) + k],
                recv_sem=self.recv_sems.at[self.first + sum(len(moves(self.sizes, g)) for g in self.order[:phase]) + k],
                device_id=(flat(moved(place, self.sizes, group, move), self.sizes),),
                device_id_type=MESH,
            )
            for k, move in enumerate(moves(self.sizes, group))
        ]

    def local(self):
        return pltpu.make_async_copy(self.own, self.whole.at[grid_position(self.sizes)], self.local_sem)

    def start(self, phase):
        if phase == 0:
            self.local().start()
        for copy in self.copies(phase):
            copy.start()

    def finish(self, phase):
        if phase == 0:
            self.local().wait()
        for copy in self.copies(phase):
            copy.wait()


class Scatter:
    def __init__(self, sizes, order, terms, sums, landing, result, send_sems, recv_sems, first):
        self.sizes, self.order, self.first = sizes, order, first
        self.held = [terms] + list(sums)
        self.landing, self.result = landing, result
        self.send_sems, self.recv_sems = send_sems, recv_sems

    @staticmethod
    def shapes(sizes, order, block):
        left, sums, landing = set(range(4)), [], []
        for phase, group in enumerate(order):
            left -= set(group)
            lead = tuple(sizes[a] for a in sorted(left))
            slots = int(np.prod([sizes[a] for a in group]))
            landing.append((slots if slots > 2 else 1,) + lead + block)
            if phase < len(order) - 1:
                sums.append(lead + block)
        return sums, landing

    def before(self, phase):
        done = [a for group in self.order[:phase] for a in group]
        return [a for a in range(4) if a not in done]

    def slot(self, phase, place):
        group = self.order[phase]
        if self.landing[phase].shape[0] == 1:
            return 0
        return flat([place[a] for a in group], [self.sizes[a] for a in group])

    def copies(self, phase):
        place = grid_position(self.sizes)
        group = self.order[phase]
        out = []
        for k, move in enumerate(moves(self.sizes, group)):
            other = moved(place, self.sizes, group, move)
            part = tuple(other[a] if a in group else slice(None) for a in self.before(phase))
            out.append(
                pltpu.make_async_remote_copy(
                    src_ref=self.held[phase].at[part],
                    dst_ref=self.landing[phase].at[self.slot(phase, place)],
                    send_sem=self.send_sems.at[self.first + sum(len(moves(self.sizes, g)) for g in self.order[:phase]) + k],
                    recv_sem=self.recv_sems.at[self.first + sum(len(moves(self.sizes, g)) for g in self.order[:phase]) + k],
                    device_id=(flat(other, self.sizes),),
                    device_id_type=MESH,
                )
            )
        return out

    def start(self, phase):
        for copy in self.copies(phase):
            copy.start()

    def finish(self, phase):
        for copy in self.copies(phase):
            copy.wait()
        place = grid_position(self.sizes)
        group = self.order[phase]
        held, landed = self.held[phase], self.landing[phase]
        before = self.before(phase)
        left = [a for a in before if a not in group]
        last = phase == len(self.order) - 1
        target = self.result if last else self.held[phase + 1]

        def one(at):
            spot = dict(zip(left, at))
            mine = held[tuple(place[a] if a in group else spot[a] for a in before)]
            at = tuple(at)
            if landed.shape[0] == 1:
                total = mine.astype(F32) + landed[(0,) + at].astype(F32)
            else:
                landed[(self.slot(phase, place),) + at] = mine
                total = landed[(0,) + at].astype(F32)
                for source in range(1, landed.shape[0]):
                    total = total + landed[(source,) + at].astype(F32)
            if at:
                target[at] = total.astype(target.dtype)
            else:
                target[...] = total.astype(target.dtype)

        if not left:
            one(())
        else:
            lead = [self.sizes[a] for a in left]

            def body(count, unused):
                at = []
                for size in reversed(lead):
                    at.append(lax.rem(count, size))
                    count = lax.div(count, size)
                one(at[::-1])
                return unused

            lax.fori_loop(0, int(np.prod(lead)), body, 0)


def firsts(sizes, orders):
    counts = [sum(len(moves(sizes, group)) for group in order) for order in orders]
    return [sum(counts[:k]) for k in range(len(counts))], sum(counts)


def semaphores(sizes, orders):
    return [pltpu.SemaphoreType.DMA((firsts(sizes, orders)[1],))] * 2


def run_actions(actions, parts):
    for action, item, phase in actions:
        getattr(parts[item], action)(phase)


def run_schedule(tick, schedule, parts):
    for at, actions in sorted(schedule.items()):

        @pl.when(tick == at)
        def _(actions=actions):
            run_actions(actions, parts)


LOW=(0,1,2,3,4,5,6,7,8,12,16,32,64,128,256,512)
T=256
NEG=-1e30
def cp(**k): return pltpu.CompilerParams(vmem_limit_bytes=56*2**20, **k)
def dot_nt(a,b): return lax.dot_general(a,b,(((1,),(1,)),((),())),preferred_element_type=jnp.float32)
def dot_nn(a,b): return jnp.dot(a,b,preferred_element_type=jnp.float32)
def dot_tn(a,b): return lax.dot_general(a,b,(((0,),(0,)),((),())),preferred_element_type=jnp.float32)

def bias_of(dist, row):
    out=jnp.zeros(dist.shape,jnp.float32)+row[:,0:1]
    for b in range(1,16):
        out=jnp.where(dist>=LOW[b],row[:,b:b+1],out)
    return jnp.where(dist<0,NEG,out)

def table_row(table_ref,head):
    whole=table_ref[...].astype(jnp.float32)
    at=lax.broadcasted_iota(jnp.int32,whole.shape,0)
    return jnp.sum(jnp.where(at==head,whole,0.0),axis=0,keepdims=True)

H = 128
VARIED = (0, 1, 2, 4)


def build_bias(row, store):
    lane = lax.broadcasted_iota(jnp.int32, (1, 2 * H), 1)
    m = jnp.where(lane < H, lane, lane - 2 * H)
    for n, delta in enumerate(VARIED):
        for transposed in (False, True):
            w = bias_of(delta * H + (m if transposed else -m), row)
            tile = pltpu.roll(jnp.broadcast_to(w, (H, 2 * H)), 0, 1, stride=1, stride_axis=0)
            store(n, transposed, tile[:, :H])


def biased(tile, delta, bias, row):
    if delta < 0:
        return jnp.full((H, H), NEG, F32)
    if delta in VARIED:
        return tile + bias[VARIED.index(delta)]
    return tile + row[:, 14:15] if delta == 3 else tile + row[:, 15:16]

def split3(v):
    hi=v.astype(jnp.bfloat16); r=v-hi.astype(jnp.float32)
    mid=r.astype(jnp.bfloat16); lo=(r-mid.astype(jnp.float32)).astype(jnp.bfloat16)
    return hi,mid,lo

def halves(h, main, extra, rows):
    lane=lax.broadcasted_iota(jnp.int32,(rows,128),1)
    out=jnp.where((lane//64)==h,main,jnp.zeros((),main.dtype))
    base=64*(1-h)
    for n,e in enumerate(extra):
        if e is not None:
            out=jnp.where(lane==base+n,jnp.broadcast_to(e,(rows,128)).astype(jnp.bfloat16),out)
    return out

def ln_parts(v):
    c=v-jnp.mean(v,axis=1,keepdims=True)
    r=lax.rsqrt(jnp.mean(c*c,axis=1,keepdims=True)+EPS)
    return c*r, r
def ln_back(e_in,gain,xhat,r):
    e=e_in*gain
    gv=r*(e-jnp.mean(e,axis=1,keepdims=True)-xhat*jnp.mean(e*xhat,axis=1,keepdims=True))
    return (gv,)

def ffn_kernel(x_ref,m_ref,og_ref,g_ref,wo_ref,wu_ref,wd_ref,out_ref,ga_ref,gm_ref,gwo_ref,gwu_ref,gwd_ref,ao,au,ad):
    i=pl.program_id(0)
    m=m_ref[...]; og=og_ref[...]
    after=x_ref[...].astype(F32)+dot_nn(m,wo_ref[...])
    xhat,r=ln_parts(after)
    gain=g_ref[...].astype(F32)
    n=(xhat*gain).astype(BF)
    pre=dot_nn(n,wu_ref[...])
    dh=dot_nt(og,wd_ref[...])
    c=0.7978845608028654
    sq=pre*pre
    t=jnp.tanh(pre*(c+c*0.044715*sq))
    half=0.5*(1.0+t)
    hid=(pre*half).astype(BF)
    dg=half+(0.5*pre)*(1.0-t*t)*(c+3*c*0.044715*sq)
    gp=(dh*dg).astype(BF)
    out_ref[...]=(after+dot_nn(hid,wd_ref[...])).astype(BF)
    pd=dot_tn(hid,og); pu=dot_tn(n,gp)
    dn=dot_nt(gp,wu_ref[...])
    (gv,)=ln_back(dn,gain,xhat,r)
    ga=og.astype(F32)+gv
    ga_ref[...]=ga
    gb=ga.astype(BF)
    po=dot_tn(m,gb)
    gm_ref[...]=dot_nt(gb,wo_ref[...]).astype(BF)
    @pl.when(i==0)
    def _():
        ad[...]=pd; au[...]=pu; ao[...]=po
    @pl.when(i>0)
    def _():
        ad[...]+=pd; au[...]+=pu; ao[...]+=po
    @pl.when(i==pl.num_programs(0)-1)
    def _():
        gwo_ref[...]=ao[...].astype(BF); gwu_ref[...]=au[...].astype(BF); gwd_ref[...]=ad[...].astype(BF)
def ffn(x,m,og,gain,wo,wu,wd,B=512):
    R,D=x.shape; FF=wu.shape[1]
    row=pl.BlockSpec((B,D),lambda i:(i,0))
    full=lambda a,b:pl.BlockSpec((a,b),lambda i:(0,0))
    return pl.pallas_call(ffn_kernel,grid=(R//B,),
      in_specs=[row,row,row,full(1,D),full(D,D),full(D,FF),full(FF,D)],
      out_specs=[row,row,row,full(D,D),full(D,FF),full(FF,D)],
      out_shape=[jax.ShapeDtypeStruct((R,D),BF),jax.ShapeDtypeStruct((R,D),F32),jax.ShapeDtypeStruct((R,D),BF),
        jax.ShapeDtypeStruct((D,D),BF),jax.ShapeDtypeStruct((D,FF),BF),jax.ShapeDtypeStruct((FF,D),BF)],
      scratch_shapes=[pltpu.VMEM((D,D),F32),pltpu.VMEM((D,FF),F32),pltpu.VMEM((FF,D),F32)],
      compiler_params=cp())(x,m,og,gain,wo,wu,wd)


SPREAD = ((0, 1, 2), (3,))
ZXY, YZX, XZY, XYZ = (((a,), (b,), (c,), (3,)) for a, b, c in ((0, 2, 1), (1, 0, 2), (2, 0, 1), (2, 1, 0)))
GATHER_ORDERS = {
    "q0": SPREAD, "gains": SPREAD, "q2": XZY, "q1": ZXY, "down1": XZY, "q3": ZXY, "down0": ZXY, "up0": YZX, "out": XYZ, "up1": YZX,
}


def timetable(starts):
    table = {}
    for item, ticks in starts.items():
        for phase, tick in enumerate(ticks):
            if phase:
                table.setdefault(tick, []).append(("finish", item, phase - 1))
            if phase < len(ticks) - 1:
                table.setdefault(tick, []).append(("start", item, phase))
    return table


GATHER_SCHEDULE = timetable(
    {
        "q2": (-1, 0, 2, 4, 5), "q1": (0, 2, 3, 3, 3), "down1": (-1, 0, 3, 6, 8), "q3": (0, 3, 4, 6, 7),
        "down0": (0, 3, 5, 7, 8), "up0": (-1, 0, 4, 7, 8), "out": (-1, 0, 2, 7, 9), "up1": (-1, 0, 6, 8, 9),
    }
)


def own_lanes():
    row = lax.broadcasted_iota(jnp.int32, (16, 128), 0)
    lane = lax.broadcasted_iota(jnp.int32, (16, 128), 1)
    return lane == row + 16 * lax.rem(lax.axis_index("dp"), 8)


def placed_gains(first_ref, second_ref):
    row = lax.broadcasted_iota(jnp.int32, (16, 16), 0)
    both = jnp.where(row == 0, first_ref[...].reshape(1, 16).astype(F32), 0.0)
    both = jnp.where(row == 1, second_ref[...].reshape(1, 16).astype(F32), both)
    return dot_nn(both.astype(BF), jnp.where(own_lanes(), 1.0, 0.0).astype(BF)).astype(BF)


def first_kernel(sizes, *refs):
    remote = sizes is not None
    refs = list(refs)
    take = lambda count: [refs.pop(0) for _ in range(count)]
    vl_ref, table_ref, x_ref = take(3)
    if remote:
        first_ref, second_ref, wq_own, wo_own, wu_own, wd_own = take(6)
    else:
        g_ref, w_ref = take(2)
    mixed_ref, qa_ref, qkv_ref, nt_ref, bt_ref = take(5)
    if remote:
        g1_ref, g2_ref, wq_out, wo_ref, wu_ref, wd_ref = take(6)
    bias, bias_t, xhat, xhat_t, n_s, nt_s, held_sem = take(7)
    keep = [pltpu.make_async_copy(nt_s, nt_ref, held_sem.at[0]), pltpu.make_async_copy(bias_t, bt_ref, held_sem.at[1])]
    hp = pl.program_id(0)
    s = pl.program_id(1)
    pairs = pl.num_programs(0)
    S, L = qkv_ref.shape[1:3]
    step = hp * S + s
    R, D = x_ref.shape
    B = 512
    if remote:
        q_own, wq, gains_own, gains, local, send, recv, out_sem = take(8)
        names = list(GATHER_ORDERS)
        own = dict(gains=gains_own, out=wo_own)
        whole = dict(gains=gains, out=wo_ref)
        for half in range(2):
            cols = slice(half * wu_own.shape[1] // 2, (half + 1) * wu_own.shape[1] // 2)
            rows = slice(half * wd_own.shape[0] // 2, (half + 1) * wd_own.shape[0] // 2)
            own["up%d" % half], whole["up%d" % half] = wu_own.at[:, cols], wu_ref.at[:, :, :, :, :, cols]
            own["down%d" % half], whole["down%d" % half] = wd_own.at[rows], wd_ref.at[:, :, :, :, rows]
        for pair in range(4):
            own["q%d" % pair], whole["q%d" % pair] = q_own.at[pair], wq.at[pair]
        place = firsts(sizes, GATHER_ORDERS.values())[0]
        parts = {
            name: Gather(sizes, GATHER_ORDERS[name], own[name], whole[name], local.at[k], send, recv, place[k])
            for k, name in enumerate(names)
        }
        out_copy = lambda pair: pltpu.make_async_copy(wq.at[pair], wq_out.at[pair], out_sem.at[pair])

    @pl.when(step == 0)
    def _():
        if remote:
            greet(sizes, SPREAD)
            gains_own[...] = placed_gains(first_ref, second_ref)
            for pair in range(4):
                for part in range(3):
                    q_own[pair, :, part * 128:(part + 1) * 128] = wq_own[:, (part * 4 + pair) * 128:(part * 4 + pair + 1) * 128]

        def all_biases(head, unused):
            def store(n, transposed, tile):
                (bias_t if transposed else bias)[head, n] = tile

            build_bias(table_row(table_ref, head), store)
            return unused

        lax.fori_loop(0, 2 * pairs, all_biases, 0)

        def norm(block, unused):
            at = pl.ds(pl.multiple_of(block * B, B), B)
            xh = ln_parts(x_ref[at, :].astype(F32))[0]
            xhat[at, :] = xh
            return unused

        lax.fori_loop(0, R // B, norm, 0)
        if remote:
            await_greetings(sizes, SPREAD)
            parts["q0"].start(0)
            parts["gains"].start(0)
            run_actions(GATHER_SCHEDULE[-1], parts)

        def turn(block, unused):
            at = pl.ds(pl.multiple_of(block * B, B), B)
            xhat_t[:, at] = xhat[at, :].T
            return unused

        lax.fori_loop(0, R // B, turn, 0)
        if remote:
            parts["gains"].finish(0)
            parts["q0"].finish(0)
            parts["gains"].start(1)
            parts["q0"].start(1)
            run_actions(GATHER_SCHEDULE[0], parts)
            parts["gains"].finish(1)
            tiles = []
            for z in range(sizes[0]):
                tile = jnp.zeros((16, 128), F32)
                for y, a, c in itertools.product(*[range(size) for size in sizes[1:]]):
                    tile = tile + gains[z, y, a, c].astype(F32)
                tiles.append(tile)
            tile = jnp.concatenate(tiles, axis=1)
            g1_ref[...] = tile[0:1, :]
            g2_ref[...] = tile[1:2, :]
            gain = tile[0:1, :]
        else:
            gain = g_ref[...]
        gain_t = jnp.broadcast_to(gain, (8, D)).T[:, 0:1]

        def scale(block, unused):
            at = pl.ds(pl.multiple_of(block * B, B), B)
            n_s[at, :] = (xhat[at, :] * gain).astype(BF)
            nt_s[:, at] = (xhat_t[:, at] * gain_t).astype(BF)
            return unused

        lax.fori_loop(0, R // B, scale, 0)
        for copy in keep:
            copy.start()
        if remote:
            parts["q0"].finish(1)

    if remote:
        run_schedule(step + 1, {tick: GATHER_SCHEDULE[tick] for tick in GATHER_SCHEDULE if 0 < tick < 9}, parts)

    @pl.when(s == 0)
    def _():
        weights = wq[hp].reshape(D, 384) if remote else w_ref[0]
        if remote:
            out_copy(hp).start()
        for seq in range(S):
            for half in range(L // B):
                row = seq * L + half * B
                qkv_ref[0, seq, half * B:(half + 1) * B, :] = dot_nn(n_s[row:row + B, :], weights).astype(BF)

    attend(vl_ref[s], qkv_ref.at[0, s], mixed_ref.at[0], qa_ref.at[0, 0], bias, table_ref, hp)

    @pl.when(step == pairs * S - 1)
    def _():
        for copy in keep:
            copy.wait()
        if remote:
            run_actions(GATHER_SCHEDULE[9], parts)
            for pair in range(4):
                out_copy(pair).wait()


def attend(valid, qkv_ref, mixed_ref, qa_ref, bias, table_ref, hp):
    L = qkv_ref.shape[0]
    nb = L // T
    key = lax.broadcasted_iota(jnp.int32, (L, 1), 0)
    mask = jnp.where(key < valid, 0.0, NEG)
    lane = lax.broadcasted_iota(jnp.int32, (T, 128), 1)
    ks = [halves(h, qkv_ref[:, 128:256], [1.0, 1.0, 1.0, mask], L) for h in range(2)]
    v = qkv_ref[:, 256:384]
    rows = [table_row(table_ref, 2 * hp + h) for h in range(2)]
    for qb in range(nb):
        kk = (qb + 1) * T
        qt = qkv_ref[qb * T:(qb + 1) * T, 0:128] * jnp.asarray(0.125, BF)
        outs = []
        for h in range(2):
            qh = halves(h, qt, [None, None, None, 1.0], T)
            sc = dot_nt(qh, ks[h][:kk])
            sc = jnp.concatenate(
                [
                    jnp.concatenate(
                        [
                            biased(sc[i * H:(i + 1) * H, j * H:(j + 1) * H], 2 * qb + i - j, bias.at[2 * hp + h], rows[h])
                            for j in range(kk // H)
                        ],
                        axis=1,
                    )
                    for i in range(2)
                ],
                axis=0,
            )
            mx = jnp.max(sc, axis=1, keepdims=True)
            p = jnp.exp(sc - mx)
            l = jnp.sum(p, axis=1, keepdims=True)
            o = dot_nn(p.astype(BF), v[:kk])
            outs.append(o * (1.0 / l))
            hi, mid, lo = split3(-(mx + jnp.log(l)))
            qa_ref[h, qb * T:(qb + 1) * T, :] = halves(h, qt, [hi, mid, lo, 1.0], T)
        mixed_ref[qb * T:(qb + 1) * T, :] = jnp.where(lane < 64, outs[0], outs[1]).astype(BF)


def whole_block(shape):
    return pl.BlockSpec(shape, lambda *unused: (0,) * len(shape))


def first_half(sizes, vl, table, x, S, weights):
    R, D = x.shape
    L = R // S
    HP = D // 128
    remote = sizes is not None
    anyspace = pl.BlockSpec(memory_space=pl.ANY)
    in_specs = [pl.BlockSpec(memory_space=pltpu.SMEM), whole_block(table.shape), whole_block((R, D))]
    out_specs = [
        pl.BlockSpec((1, L, 128), lambda h, s: (s, 0, h)),
        pl.BlockSpec((1, 1, 2, L, 128), lambda h, s: (s, h, 0, 0, 0)),
        pl.BlockSpec((1, S, L, 384), lambda h, s: (h, 0, 0, 0)),
        anyspace,
        anyspace,
    ]
    out_shape = [
        jax.ShapeDtypeStruct((S, L, D), BF),
        jax.ShapeDtypeStruct((S, HP, 2, L, 128), BF),
        jax.ShapeDtypeStruct((HP, S, L, 384), BF),
        jax.ShapeDtypeStruct((D, R), BF),
        jax.ShapeDtypeStruct((2 * HP, len(VARIED), H, H), F32),
    ]
    scratch = [
        pltpu.VMEM((2 * HP, len(VARIED), H, H), F32), pltpu.VMEM((2 * HP, len(VARIED), H, H), F32), pltpu.VMEM((R, D), F32),
        pltpu.VMEM((D, R), F32), pltpu.VMEM((R, D), BF), pltpu.VMEM((D, R), BF), pltpu.SemaphoreType.DMA((2,)),
    ]
    if remote:
        first, second, wq, wo, wu, wd = weights
        in_specs += [whole_block(first.shape), whole_block(second.shape), whole_block(wq.shape), anyspace, anyspace, anyspace]
        out_specs += [whole_block((1, D)), whole_block((1, D))] + [anyspace] * 4
        out_shape += [jax.ShapeDtypeStruct((1, D), F32)] * 2
        out_shape += [jax.ShapeDtypeStruct((HP,) + sizes + (16, 384), BF)]
        out_shape += [jax.ShapeDtypeStruct(sizes + w.shape, BF) for w in (wo, wu, wd)]
        scratch += [
            pltpu.VMEM((HP, 16, 384), BF),
            pltpu.VMEM((HP,) + sizes + (16, 384), BF),
            pltpu.VMEM((16, 128), BF),
            pltpu.VMEM(sizes + (16, 128), BF),
            pltpu.SemaphoreType.DMA((len(GATHER_ORDERS),)),
        ] + semaphores(sizes, GATHER_ORDERS.values()) + [pltpu.SemaphoreType.DMA((HP,))]
        params = cp(collective_id=1, has_side_effects=True)
    else:
        gain, wq = weights
        in_specs += [whole_block((1, D)), pl.BlockSpec((1, D, 384), lambda h, s: (h, 0, 0))]
        params = cp()
    return pl.pallas_call(
        functools.partial(first_kernel, sizes), grid=(HP, S), in_specs=in_specs, out_specs=out_specs, out_shape=out_shape,
        scratch_shapes=scratch, compiler_params=params,
    )(vl, table, x, *weights)


CXYZ, CYXZ, CXZY, CYZX = (((3,), (a,), (b,), (c,)) for a, b, c in ((2, 1, 0), (1, 2, 0), (2, 0, 1), (1, 0, 2)))
DIRECT = ((3,), (0, 1, 2))
SCATTER_ORDERS = {
    "up0": CYXZ, "down0": CXYZ, "out": CYZX, "up1": CXZY, "down1": CYXZ, "q0": CYZX, "q1": CXZY, "q2": DIRECT, "q3": DIRECT,
}
SCATTER_SCHEDULE = timetable(
    {
        "q3": (8, 9, 12), "out": (1, 2, 3, 5, 6), "up0": (1, 2, 4, 5, 7), "up1": (1, 2, 4, 6, 7), "q1": (4, 5, 6, 7, 8),
        "q0": (2, 3, 5, 7, 8), "down0": (1, 3, 5, 6, 8), "down1": (1, 3, 6, 7, 9), "q2": (6, 7, 11), "table": (8, 9, 11),
    }
)


def last_kernel(sizes, plan, *refs):
    remote = sizes is not None
    refs = list(refs)
    take = lambda count: [refs.pop(0) for _ in range(count)]
    vl_ref, table_ref, bias, qa_ref, qkv_ref, o_ref, g_ref, nt_ref, w_ref, gain_ref, x_ref, ga_ref = take(12)
    if remote:
        wo_terms, wu_terms, wd_terms = take(3)
    gi_ref, tab_ref = take(2)
    if remote:
        results = dict(zip(SCATTER_ORDERS, take(9)))
    else:
        (gw_ref,) = take(1)
    gacc, far, dqt, grads = take(4)
    t = pl.program_id(0)
    pairs = grads.shape[0]
    S = grads.shape[1] // qkv_ref.shape[2]
    steps = pairs * S
    hp = lax.div(t, S)
    s = lax.rem(t, S)
    L = qkv_ref.shape[2]
    R = S * L
    D = x_ref.shape[1]
    if remote:
        wq_terms, tab_own, tab_all, local = take(4)
        terms = dict(out=wo_terms)
        for half in range(2):
            cols = slice(half * wu_terms.shape[5] // 2, (half + 1) * wu_terms.shape[5] // 2)
            rows = slice(half * wd_terms.shape[4] // 2, (half + 1) * wd_terms.shape[4] // 2)
            terms["up%d" % half] = wu_terms.at[:, :, :, :, :, cols]
            terms["down%d" % half] = wd_terms.at[:, :, :, :, rows]
        for pair in range(4):
            terms["q%d" % pair] = wq_terms.at[pair]
        send, recv = refs[-2:]
        place = firsts(sizes, [*SCATTER_ORDERS.values(), SPREAD])[0]
        parts = {}
        for k, name in enumerate(SCATTER_ORDERS):
            sums, landing = plan[name]
            parts[name] = Scatter(
                sizes, SCATTER_ORDERS[name], terms[name], take(len(sums)), take(len(landing)), results[name], send, recv, place[k]
            )
        parts["table"] = Gather(sizes, SPREAD, tab_own, tab_all, local, send, recv, place[-1])

        @pl.when(t == 0)
        def _():
            greet(sizes, SPREAD)

        @pl.when(t == 1)
        def _():
            await_greetings(sizes, SPREAD)

        run_schedule(t, {at: SCATTER_SCHEDULE[at] for at in SCATTER_SCHEDULE if at < 12}, parts)

    @pl.when(t < steps)
    def _():
        @pl.when(s == 0)
        def _():
            gacc[...] = jnp.zeros_like(gacc)
            far[...] = jnp.zeros_like(far)

        at = pl.multiple_of(s * L, L)
        attend_back(vl_ref[s], qa_ref.at[0, 0], qkv_ref.at[0, 0], o_ref[0], g_ref[0], grads, hp, at, bias, table_ref, gacc, far, dqt)

        @pl.when(s == S - 1)
        def _():
            rows = table_terms(gacc, far)
            place = pl.ds(pl.multiple_of(hp * 8, 8), 8)
            (tab_own if remote else tab_ref)[place, :] = rows
            gw = dot_nn(nt_ref[...], grads[hp]).astype(BF)
            if remote:
                wq_terms[hp] = gw.reshape(sizes + (16, 384))
            else:
                gw_ref[hp] = gw

    @pl.when(t >= steps)
    def _():
        B = x_ref.shape[0]
        at = pl.ds(pl.multiple_of((t - steps) * B, B), B)
        xhat, r = ln_parts(x_ref[...].astype(F32))
        dn = dot_nt(
            jnp.concatenate([grads[pair, at, :] for pair in range(pairs)], axis=1),
            jnp.concatenate([w_ref[pair] for pair in range(pairs)], axis=1),
        )
        gi_ref[...] = (ga_ref[...] + ln_back(dn, gain_ref[...], xhat, r)[0]).astype(BF)

    if remote:

        @pl.when(t == pl.num_programs(0) - 1)
        def _():
            run_actions(SCATTER_SCHEDULE[12], parts)
            total = None
            for at in itertools.product(*[range(size) for size in sizes]):
                block = tab_all[at]
                total = block if total is None else total + block
            tab_ref[...] = total


def table_terms(gacc, far):
    lane = lax.broadcasted_iota(jnp.int32, (1, 2 * H), 1)
    m = jnp.where(lane < H, lane, lane - 2 * H)
    bl = lax.broadcasted_iota(jnp.int32, (1, 128), 1)
    rows = []
    for h in range(2):
        row = jnp.zeros((1, 128), F32)
        for b in (14, 15):
            row = row + jnp.where(bl == b, jnp.sum(jnp.sum(far[h, b - 14], axis=0, keepdims=True), axis=1, keepdims=True), 0.0)
        for n, delta in enumerate(VARIED):
            w = jnp.concatenate([gacc[h, n], jnp.zeros((H, H), F32)], axis=1)
            acc = w[:8]
            for a in range(1, H // 8):
                acc = acc + pltpu.roll(w[8 * a:8 * a + 8], 2 * H - 8 * a, 1)
            diag = acc[0:1]
            for a in range(1, 8):
                diag = diag + pltpu.roll(acc[a:a + 1], 2 * H - a, 1)
            dist = delta * H + m
            for b in range(16):
                if LOW[b] >= (delta + 1) * H or (b < 15 and LOW[b + 1] <= (delta - 1) * H):
                    continue
                sel = dist >= LOW[b]
                if b < 15:
                    sel = sel & (dist < LOW[b + 1])
                row = row + jnp.where(bl == b, jnp.sum(jnp.where(sel, diag, 0.0), axis=1, keepdims=True), 0.0)
        rows.append(row)
    return jnp.concatenate(rows + [jnp.zeros((6, 128), F32)], axis=0)


def attend_back(valid, qa_ref, qkv_ref, o, g, grads, hp, first, bias, table_ref, gacc, far, dqt):
    L = qkv_ref.shape[0]
    rows = [table_row(table_ref, 2 * hp + h) for h in range(2)]
    nb = L // T
    key = lax.broadcasted_iota(jnp.int32, (L, 1), 0)
    mask = jnp.where(key < valid, 0.0, NEG)
    lane = lax.broadcasted_iota(jnp.int32, (T, 128), 1)
    prod = g.astype(F32) * o.astype(F32)
    lane_l = lax.broadcasted_iota(jnp.int32, (L, 128), 1)
    k = qkv_ref[:, 128:256]
    ks = [halves(h, k, [1.0, 1.0, 1.0, mask], L) for h in range(2)]
    vs = [halves(h, qkv_ref[:, 256:384], [1.0, 1.0, 1.0], L) for h in range(2)]
    gs = []
    for h in range(2):
        d = jnp.sum(jnp.where((lane_l // 64) == h, prod, 0.0), axis=1, keepdims=True)
        hi, mid, lo = split3(-d)
        gs.append(halves(h, g, [hi, mid, lo], L))
    kt = (k * jnp.asarray(0.125, BF)).T
    for kb in range(nb):
        dks, dvs = [], []
        for h in range(2):
            qh = qa_ref[h]
            st = dot_nt(ks[h][kb * T:(kb + 1) * T], qh[kb * T:])
            dp = dot_nt(vs[h][kb * T:(kb + 1) * T], gs[h][kb * T:])
            st = jnp.concatenate(
                [
                    jnp.concatenate(
                        [biased(st[j * H:(j + 1) * H, i * H:(i + 1) * H], i - j, bias.at[0, h], rows[h]) for i in range(2 * (nb - kb))],
                        axis=1,
                    )
                    for j in range(2)
                ],
                axis=0,
            )
            p = jnp.exp(st)
            ds = p * dp
            pb = p.astype(BF)
            dsb = ds.astype(BF)
            dvs.append(dot_nn(pb, gs[h][kb * T:]))
            dks.append(dot_nn(dsb, qh[kb * T:]))
            for delta in range(2 * (nb - kb)):
                both = [ds[j * H:(j + 1) * H, i * H:(i + 1) * H] for j in range(2) for i in range(2 * (nb - kb)) if i - j == delta]
                both = both[0] if len(both) == 1 else both[0] + both[1]
                if delta in VARIED:
                    gacc[h, VARIED.index(delta)] += both
                else:
                    far[h, 0 if delta == 3 else 1] += jnp.sum(both.reshape(H // 8, 8, H), axis=0)
            r = dot_nn(kt[h * 64:(h + 1) * 64, kb * T:(kb + 1) * T], dsb)
            if kb == 0:
                dqt[h * 64:(h + 1) * 64, :] = r
            else:
                dqt[h * 64:(h + 1) * 64, kb * T:] += r
        at = pl.ds(first + kb * T, T)
        grads[hp, at, 128:256] = jnp.where(lane < 64, dks[0], dks[1]).astype(BF)
        grads[hp, at, 256:384] = jnp.where(lane < 64, dvs[0], dvs[1]).astype(BF)
    grads[hp, pl.ds(first, L), 0:128] = dqt[...].T.astype(BF)


def last_half(sizes, vl, table, bias_t, qa, qkv, mixed, gm, nt, wq, gain, x, ga, ffn_grads):
    HP, S, L, W = qkv.shape
    R, D = x.shape
    B = 512
    steps = HP * S
    remote = sizes is not None
    pair = lambda t: jnp.minimum(t, steps - 1) // S
    seq = lambda t: jnp.minimum(t, steps - 1) % S
    late = pl.BlockSpec((B, D), lambda t: (jnp.maximum(t - steps, 0), 0))
    in_specs = [
        pl.BlockSpec(memory_space=pltpu.SMEM),
        whole_block(table.shape),
        pl.BlockSpec((1, 2, len(VARIED), H, H), lambda t: (pair(t), 0, 0, 0, 0)),
        pl.BlockSpec((1, 1, 2, L, 128), lambda t: (seq(t), pair(t), 0, 0, 0)),
        pl.BlockSpec((1, 1, L, W), lambda t: (pair(t), seq(t), 0, 0)),
        pl.BlockSpec((1, L, 128), lambda t: (seq(t), 0, pair(t))),
        pl.BlockSpec((1, L, 128), lambda t: (seq(t), 0, pair(t))),
        whole_block((D, R)),
        whole_block((HP, D, W)),
        whole_block((1, D)),
        late,
        late,
    ]
    out_specs = [late, whole_block((8 * HP, 128))]
    out_shape = [jax.ShapeDtypeStruct((R, D), BF), jax.ShapeDtypeStruct((8 * HP, 128), F32)]
    scratch = [
        pltpu.VMEM((2, len(VARIED), H, H), F32), pltpu.VMEM((2, 2, 8, H), F32), pltpu.VMEM((128, L), F32),
        pltpu.VMEM((HP, R, W), BF),
    ]
    args = [vl, table, bias_t.reshape(HP, 2, len(VARIED), H, H), qa, qkv, mixed, gm, nt, wq, gain, x, ga]
    plan = None
    if remote:
        count = int(np.prod(sizes))
        terms = [a.reshape(sizes + (a.shape[0] // count, a.shape[1])) for a in ffn_grads]
        args += terms
        in_specs += [whole_block(a.shape) for a in terms]
        (_, D_), (_, U_), (rows_, _) = [a.shape[4:] for a in terms]
        blocks = dict(out=(16, D_), up0=(16, U_ // 2), up1=(16, U_ // 2), down0=(rows_ // 2, D_), down1=(rows_ // 2, D_))
        for k in range(HP):
            blocks["q%d" % k] = (16, W)
        plan = {name: Scatter.shapes(sizes, SCATTER_ORDERS[name], blocks[name]) for name in SCATTER_ORDERS}
        out_specs += [whole_block(blocks[name]) for name in SCATTER_ORDERS]
        out_shape += [jax.ShapeDtypeStruct(blocks[name], F32) for name in SCATTER_ORDERS]
        scratch += [
            pltpu.VMEM((HP,) + sizes + (16, W), BF), pltpu.VMEM((8 * HP, 128), F32), pltpu.VMEM(sizes + (8 * HP, 128), F32),
            pltpu.SemaphoreType.DMA,
        ]
        for name in SCATTER_ORDERS:
            scratch += [pltpu.VMEM(shape, BF) for shape in plan[name][0] + plan[name][1]]
        scratch += semaphores(sizes, [*SCATTER_ORDERS.values(), SPREAD])
        params = cp(collective_id=2, has_side_effects=True)
    else:
        out_specs += [whole_block((HP, D, W))]
        out_shape += [jax.ShapeDtypeStruct((HP, D, W), BF)]
        params = cp()
    return pl.pallas_call(
        functools.partial(last_kernel, sizes, plan), grid=(steps + R // B,), in_specs=in_specs, out_specs=out_specs,
        out_shape=out_shape, scratch_shapes=scratch, compiler_params=params,
    )(*args)


def finish_kernel(*refs):
    refs = list(refs)
    take = lambda count: [refs.pop(0) for _ in range(count)]
    tab_ref, ru0_ref, rd0_ref, ro_ref, ru1_ref, rd1_ref = take(6)
    pieces = take(4)
    first_ref, second_ref, wq_ref, wu_ref = take(4)
    tab_out, wq_out, wo_out, wu_out, wd_out, g1_out, g2_out = refs
    table = jnp.concatenate([tab_ref[8 * pair:8 * pair + 2, :] for pair in range(4)], axis=0)
    tab_out[...] = table[:, :16]
    wo_out[...] = ro_ref[...]
    for half, (ru_ref, rd_ref) in enumerate(((ru0_ref, rd0_ref), (ru1_ref, rd1_ref))):
        wu_out[:, half * ru_ref.shape[1]:(half + 1) * ru_ref.shape[1]] = ru_ref[...]
        wd_out[half * rd_ref.shape[0]:(half + 1) * rd_ref.shape[0], :] = rd_ref[...]
    for pair in range(4):
        for part in range(3):
            wq_out[:, (part * 4 + pair) * 128:(part * 4 + pair + 1) * 128] = pieces[pair][:, part * 128:(part + 1) * 128]
    square = lax.broadcasted_iota(jnp.int32, (16, 16), 0) == lax.broadcasted_iota(jnp.int32, (16, 16), 1)
    for first, w, grad, out in ((first_ref, wq_ref, wq_out, g1_out), (second_ref, wu_ref, wu_out, g2_out)):
        gain = first[...].reshape(1, 16).astype(F32)
        dots = jnp.sum(w[...].astype(F32) * grad[...], axis=1, keepdims=True)
        out[...] = jnp.sum(jnp.where(square, dots, 0.0), axis=0, keepdims=True) / gain


def finish(tab, results, first, second, wq, wu):
    out_shape = [
        jax.ShapeDtypeStruct((8, 16), F32), jax.ShapeDtypeStruct(wq.shape, F32), jax.ShapeDtypeStruct((wu.shape[0], wq.shape[1] // 3), F32),
        jax.ShapeDtypeStruct(wu.shape, F32), jax.ShapeDtypeStruct((2 * results[1].shape[0], wq.shape[1] // 3), F32), jax.ShapeDtypeStruct((1, 16), F32),
        jax.ShapeDtypeStruct((1, 16), F32),
    ]
    return pl.pallas_call(finish_kernel, out_shape=out_shape, compiler_params=cp())(tab, *results, first, second, wq, wu)


def on_device(devices, inputs, valid_len, norm_first, w_qkv, w_out, relative_bucket_table, norm_second, w_up, w_down, output_gradient):
    S, L, D = inputs.shape
    R = S * L
    HP = D // 128
    FFW = w_up.shape[1]
    fast = devices == 32 and D == 512 and S == 2
    table = relative_bucket_table
    x = inputs.reshape(R, D)
    og = output_gradient.reshape(R, D)
    by_pair = lambda w: w.reshape(D, 3, HP, 128).transpose(2, 0, 1, 3).reshape(HP, D, 384)
    if fast:
        sizes = device_grid(devices)
        mixed, qa, qkv, nt, bias_t, g1, g2, wq, wo, wu, wd = first_half(
            sizes, valid_len, table, x, S, [norm_first, norm_second, w_qkv, w_out, w_up, w_down]
        )
        wq, wo, wu, wd = wq.reshape(HP, D, 384), wo.reshape(D, D), wu.reshape(D, FFW), wd.reshape(FFW, D)
    else:
        sizes = None
        g1, wq, wo, g2, wu, wd = [
            lax.all_gather(a, "dp", axis=0, tiled=True) for a in (norm_first, w_qkv, w_out, norm_second, w_up, w_down)
        ]
        g1, g2 = g1.reshape(1, D).astype(F32), g2.reshape(1, D).astype(F32)
        wq = by_pair(wq)
        mixed, qa, qkv, nt, bias_t = first_half(None, valid_len, table, x, S, [g1, wq])
    out, ga, gm, gwo, gwu, gwd = ffn(x, mixed.reshape(R, D), og, g2, wo, wu, wd)
    got = last_half(
        sizes, valid_len, table, bias_t, qa, qkv, mixed, gm.reshape(S, L, D), nt, wq, g1, x, ga, [gwo, gwu, gwd]
    )
    gi, tab = got[:2]
    if fast:
        rt, rq, ro, ru, rd, r1, r2 = finish(tab, got[2:], norm_first, norm_second, w_qkv, w_up)
        r1, r2 = r1.reshape(-1), r2.reshape(-1)
    else:
        gwq = got[2].reshape(HP, D, 3, 128).transpose(1, 2, 0, 3).reshape(D, 3 * D)
        rq, ro, ru, rd = [
            lax.psum_scatter(a.astype(F32), "dp", scatter_dimension=0, tiled=True) for a in (gwq, gwo, gwu, gwd)
        ]
        r1 = jnp.sum(w_qkv.astype(F32) * rq, axis=1) / norm_first.astype(F32)
        r2 = jnp.sum(w_up.astype(F32) * ru, axis=1) / norm_second.astype(F32)
        rt = lax.psum(tab.reshape(HP, 8, 128)[:, :2, :16].reshape(table.shape), "dp")
    return (out.reshape(S, L, D), gi.reshape(S, L, D), r1, rq, ro, rt, r2, ru, rd)


def solution(mesh):
    placed = (
        P("dp", None, None), P("dp"), P("dp"), P("dp", None), P("dp", None), P(), P("dp"), P("dp", None), P("dp", None),
        P("dp", None, None),
    )
    return jax.shard_map(
        functools.partial(on_device, mesh.shape["dp"]),
        mesh=mesh,
        in_specs=placed,
        out_specs=(
            P("dp", None, None), P("dp", None, None), P("dp"), P("dp", None), P("dp", None), P(), P("dp"), P("dp", None),
            P("dp", None),
        ),
        check_vma=False,
    )
```

```python
import functools
import itertools

import jax
import jax.numpy as jnp
import numpy as np
from jax import lax
from jax.experimental import pallas as pl
from jax.experimental.pallas import tpu as pltpu
from jax.sharding import PartitionSpec as P

MESH = pl.DeviceIdType.MESH
F32 = jnp.float32
BF = jnp.bfloat16
EPS = 1e-05


def device_grid(devices):
    return (devices // 8, 2, 2, 2)


def grid_position(sizes):
    rest = lax.axis_index("dp")
    place = []
    for size in reversed(sizes):
        place.append(lax.rem(rest, size))
        rest = lax.div(rest, size)
    return tuple(reversed(place))


def flat(place, sizes):
    index = place[0]
    for one, size in zip(place[1:], sizes[1:]):
        index = index * size + one
    return index


def moves(sizes, group):
    return [m for m in itertools.product(*[range(sizes[a]) for a in group]) if any(m)]


def moved(place, sizes, group, move):
    other = list(place)
    for axis, step in zip(group, move):
        if step:
            other[axis] = lax.rem(place[axis] + step, sizes[axis])
    return tuple(other)


def greet(sizes, groups):
    place = grid_position(sizes)
    barrier = pltpu.get_barrier_semaphore()
    for group in groups:
        for move in moves(sizes, group):
            pl.semaphore_signal(
                barrier,
                inc=1,
                device_id=(flat(moved(place, sizes, group, move), sizes),),
                device_id_type=MESH,
            )


def await_greetings(sizes, groups):
    pl.semaphore_wait(pltpu.get_barrier_semaphore(), sum(len(moves(sizes, group)) for group in groups))


class Gather:
    def __init__(self, sizes, order, own, whole, local_sem, send_sems, recv_sems, first):
        self.sizes, self.order, self.first = sizes, order, first
        self.own, self.whole = own, whole
        self.local_sem, self.send_sems, self.recv_sems = local_sem, send_sems, recv_sems

    def copies(self, phase):
        place = grid_position(self.sizes)
        done = [a for group in self.order[:phase] for a in group]
        group = self.order[phase]
        part = self.whole.at[tuple(slice(None) if a in done else place[a] for a in range(4))]
        return [
            pltpu.make_async_remote_copy(
                src_ref=self.own if phase == 0 else part,
                dst_ref=part,
                send_sem=self.send_sems.at[self.first + sum(len(moves(self.sizes, g)) for g in self.order[:phase]) + k],
                recv_sem=self.recv_sems.at[self.first + sum(len(moves(self.sizes, g)) for g in self.order[:phase]) + k],
                device_id=(flat(moved(place, self.sizes, group, move), self.sizes),),
                device_id_type=MESH,
            )
            for k, move in enumerate(moves(self.sizes, group))
        ]

    def local(self):
        return pltpu.make_async_copy(self.own, self.whole.at[grid_position(self.sizes)], self.local_sem)

    def start(self, phase):
        if phase == 0:
            self.local().start()
        for copy in self.copies(phase):
            copy.start()

    def finish(self, phase):
        if phase == 0:
            self.local().wait()
        for copy in self.copies(phase):
            copy.wait()


class Scatter:
    def __init__(self, sizes, order, terms, sums, landing, result, send_sems, recv_sems, first):
        self.sizes, self.order, self.first = sizes, order, first
        self.held = [terms] + list(sums)
        self.landing, self.result = landing, result
        self.send_sems, self.recv_sems = send_sems, recv_sems

    @staticmethod
    def shapes(sizes, order, block):
        left, sums, landing = set(range(4)), [], []
        for phase, group in enumerate(order):
            left -= set(group)
            lead = tuple(sizes[a] for a in sorted(left))
            slots = int(np.prod([sizes[a] for a in group]))
            landing.append((slots if slots > 2 else 1,) + lead + block)
            if phase < len(order) - 1:
                sums.append(lead + block)
        return sums, landing

    def before(self, phase):
        done = [a for group in self.order[:phase] for a in group]
        return [a for a in range(4) if a not in done]

    def slot(self, phase, place):
        group = self.order[phase]
        if self.landing[phase].shape[0] == 1:
            return 0
        return flat([place[a] for a in group], [self.sizes[a] for a in group])

    def copies(self, phase):
        place = grid_position(self.sizes)
        group = self.order[phase]
        out = []
        for k, move in enumerate(moves(self.sizes, group)):
            other = moved(place, self.sizes, group, move)
            part = tuple(other[a] if a in group else slice(None) for a in self.before(phase))
            out.append(
                pltpu.make_async_remote_copy(
                    src_ref=self.held[phase].at[part],
                    dst_ref=self.landing[phase].at[self.slot(phase, place)],
                    send_sem=self.send_sems.at[self.first + sum(len(moves(self.sizes, g)) for g in self.order[:phase]) + k],
                    recv_sem=self.recv_sems.at[self.first + sum(len(moves(self.sizes, g)) for g in self.order[:phase]) + k],
                    device_id=(flat(other, self.sizes),),
                    device_id_type=MESH,
                )
            )
        return out

    def start(self, phase):
        for copy in self.copies(phase):
            copy.start()

    def finish(self, phase):
        for copy in self.copies(phase):
            copy.wait()
        place = grid_position(self.sizes)
        group = self.order[phase]
        held, landed = self.held[phase], self.landing[phase]
        before = self.before(phase)
        left = [a for a in before if a not in group]
        last = phase == len(self.order) - 1
        target = self.result if last else self.held[phase + 1]

        def one(at):
            spot = dict(zip(left, at))
            mine = held[tuple(place[a] if a in group else spot[a] for a in before)]
            at = tuple(at)
            if landed.shape[0] == 1:
                total = mine.astype(F32) + landed[(0,) + at].astype(F32)
            else:
                landed[(self.slot(phase, place),) + at] = mine
                total = landed[(0,) + at].astype(F32)
                for source in range(1, landed.shape[0]):
                    total = total + landed[(source,) + at].astype(F32)
            if at:
                target[at] = total.astype(target.dtype)
            else:
                target[...] = total.astype(target.dtype)

        if not left:
            one(())
        else:
            lead = [self.sizes[a] for a in left]

            def body(count, unused):
                at = []
                for size in reversed(lead):
                    at.append(lax.rem(count, size))
                    count = lax.div(count, size)
                one(at[::-1])
                return unused

            lax.fori_loop(0, int(np.prod(lead)), body, 0)


def firsts(sizes, orders):
    counts = [sum(len(moves(sizes, group)) for group in order) for order in orders]
    return [sum(counts[:k]) for k in range(len(counts))], sum(counts)


def semaphores(sizes, orders):
    return [pltpu.SemaphoreType.DMA((firsts(sizes, orders)[1],))] * 2


def run_actions(actions, parts):
    for action, item, phase in actions:
        getattr(parts[item], action)(phase)


def run_schedule(tick, schedule, parts):
    for at, actions in sorted(schedule.items()):

        @pl.when(tick == at)
        def _(actions=actions):
            run_actions(actions, parts)


LOW=(0,1,2,3,4,5,6,7,8,12,16,32,64,128,256,512)
T=256
NEG=-1e30
def cp(**k): return pltpu.CompilerParams(vmem_limit_bytes=56*2**20, **k)
def dot_nt(a,b): return lax.dot_general(a,b,(((1,),(1,)),((),())),preferred_element_type=jnp.float32)
def dot_nn(a,b): return jnp.dot(a,b,preferred_element_type=jnp.float32)
def dot_tn(a,b): return lax.dot_general(a,b,(((0,),(0,)),((),())),preferred_element_type=jnp.float32)

def bias_of(dist, row):
    out=jnp.zeros(dist.shape,jnp.float32)+row[:,0:1]
    for b in range(1,16):
        out=jnp.where(dist>=LOW[b],row[:,b:b+1],out)
    return jnp.where(dist<0,NEG,out)

def table_row(table_ref,head):
    whole=table_ref[...].astype(jnp.float32)
    at=lax.broadcasted_iota(jnp.int32,whole.shape,0)
    return jnp.sum(jnp.where(at==head,whole,0.0),axis=0,keepdims=True)

H = 128
VARIED = (0, 1, 2, 4)


def build_bias(row, store):
    lane = lax.broadcasted_iota(jnp.int32, (1, 2 * H), 1)
    m = jnp.where(lane < H, lane, lane - 2 * H)
    for n, delta in enumerate(VARIED):
        for transposed in (False, True):
            w = bias_of(delta * H + (m if transposed else -m), row)
            tile = pltpu.roll(jnp.broadcast_to(w, (H, 2 * H)), 0, 1, stride=1, stride_axis=0)
            store(n, transposed, tile[:, :H])


def biased(tile, delta, bias, row):
    if delta < 0:
        return jnp.full((H, H), NEG, F32)
    if delta in VARIED:
        return tile + bias[VARIED.index(delta)]
    return tile + row[:, 14:15] if delta == 3 else tile + row[:, 15:16]

def split3(v):
    hi=v.astype(jnp.bfloat16); r=v-hi.astype(jnp.float32)
    mid=r.astype(jnp.bfloat16); lo=(r-mid.astype(jnp.float32)).astype(jnp.bfloat16)
    return hi,mid,lo

def halves(h, main, extra, rows):
    lane=lax.broadcasted_iota(jnp.int32,(rows,128),1)
    out=jnp.where((lane//64)==h,main,jnp.zeros((),main.dtype))
    base=64*(1-h)
    for n,e in enumerate(extra):
        if e is not None:
            out=jnp.where(lane==base+n,jnp.broadcast_to(e,(rows,128)).astype(jnp.bfloat16),out)
    return out

def ln_parts(v):
    c=v-jnp.mean(v,axis=1,keepdims=True)
    r=lax.rsqrt(jnp.mean(c*c,axis=1,keepdims=True)+EPS)
    return c*r, r
def ln_back(e_in,gain,xhat,r):
    e=e_in*gain
    gv=r*(e-jnp.mean(e,axis=1,keepdims=True)-xhat*jnp.mean(e*xhat,axis=1,keepdims=True))
    return (gv,)

def ffn_kernel(x_ref, m_ref, og_ref, g_ref, wo_ref, wu_ref, wd_ref, out_ref, ga_ref, gm_ref, gwo_ref, gwu_ref, gwd_ref,
               hid_s, gp_s, gb_s, nt_s, ogt_s, mt_s):
    i = pl.program_id(0)
    B = x_ref.shape[0]
    R = hid_s.shape[0]
    blocks = R // B
    C = hid_s.shape[1] // FFN_PARTS

    @pl.when(i < blocks)
    def _():
        at = pl.ds(pl.multiple_of(i * B, B), B)
        m = m_ref[...]
        og = og_ref[...]
        after = x_ref[...].astype(F32) + dot_nn(m, wo_ref[...])
        xhat, r = ln_parts(after)
        gain = g_ref[...]
        n = (xhat * gain).astype(BF)
        c = 0.7978845608028654
        for j in range(FFN_PARTS):
            cols = slice(j * C, (j + 1) * C)
            pre = dot_nn(n, wu_ref[:, cols])
            dh = dot_nt(og, wd_ref[cols, :])
            a = c + (c * 0.044715) * (pre * pre)
            half = 0.5 + 0.5 * jnp.tanh(pre * a)
            h = pre * half
            gp_s[at, cols] = (dh * (half + (h - h * half) * (6.0 * a - 4.0 * c))).astype(BF)
            hid_s[at, cols] = h.astype(BF)
        out_ref[...] = (after + dot_nn(hid_s[at, :], wd_ref[...])).astype(BF)
        dn = dot_nt(gp_s[at, :], wu_ref[...])
        (gv,) = ln_back(dn, gain, xhat, r)
        ga = og.astype(F32) + gv
        ga_ref[...] = ga
        gb = ga.astype(BF)
        gb_s[at, :] = gb
        gm_ref[...] = dot_nt(gb, wo_ref[...]).astype(BF)
        nt_s[:, at] = n.T
        ogt_s[:, at] = og.T
        mt_s[:, at] = m.T

    @pl.when(i >= blocks)
    def _():
        j = i - blocks
        cols = pl.ds(pl.multiple_of(j * C, C), C)
        gwd_ref[...] = dot_nn(ogt_s[...], hid_s[:, cols]).astype(BF).T
        gwu_ref[...] = dot_nn(nt_s[...], gp_s[:, cols]).astype(BF)
        share = mt_s.shape[0] // FFN_PARTS
        gwo_ref[...] = dot_nn(mt_s[pl.ds(pl.multiple_of(j * share, share), share), :], gb_s[...]).astype(BF)


FFN_PARTS = 4


def ffn(x, m, og, gain, wo, wu, wd, B=512):
    R, D = x.shape
    FF = wu.shape[1]
    n = R // B
    C = FF // FFN_PARTS
    row = pl.BlockSpec((B, D), lambda i: (jnp.minimum(i, n - 1), 0))
    late = lambda i: jnp.maximum(i - n, 0)
    return pl.pallas_call(
        ffn_kernel,
        grid=(n + FFN_PARTS,),
        in_specs=[row, row, row, whole_block((1, D)), whole_block((D, D)), whole_block((D, FF)), whole_block((FF, D))],
        out_specs=[
            row, row, row,
            pl.BlockSpec((D // FFN_PARTS, D), lambda i: (late(i), 0)),
            pl.BlockSpec((D, C), lambda i: (0, late(i))),
            pl.BlockSpec((C, D), lambda i: (late(i), 0)),
        ],
        out_shape=[
            jax.ShapeDtypeStruct((R, D), BF), jax.ShapeDtypeStruct((R, D), F32), jax.ShapeDtypeStruct((R, D), BF),
            jax.ShapeDtypeStruct((D, D), BF), jax.ShapeDtypeStruct((D, FF), BF), jax.ShapeDtypeStruct((FF, D), BF),
        ],
        scratch_shapes=[
            pltpu.VMEM((R, FF), BF), pltpu.VMEM((R, FF), BF), pltpu.VMEM((R, D), BF), pltpu.VMEM((D, R), BF),
            pltpu.VMEM((D, R), BF), pltpu.VMEM((D, R), BF),
        ],
        compiler_params=cp(),
    )(x, m, og, gain, wo, wu, wd)


SPREAD = ((0, 1, 2), (3,))
ZYX, ZXY, YZX, XZY, XYZ, YXZ = (
    ((a,), (b,), (c,), (3,)) for a, b, c in ((0, 1, 2), (0, 2, 1), (1, 0, 2), (2, 0, 1), (2, 1, 0), (1, 2, 0))
)
GATHER_ORDERS = {
    "q0": SPREAD,
    "gains": SPREAD,
    "q3": ZYX,
    "q1": XZY,
    "out": ZYX,
    "down0": XYZ,
    "up1": ZXY,
    "q2": ZXY,
    "up0": ZYX,
    "down1": ZXY,
}


def timetable(starts):
    table = {}
    for item, ticks in starts.items():
        for phase, tick in enumerate(ticks):
            if phase:
                table.setdefault(tick, []).append(("finish", item, phase - 1))
            if phase < len(ticks) - 1:
                table.setdefault(tick, []).append(("start", item, phase))
    return table


GATHER_SCHEDULE = timetable(
    {
        "q3": (0, 2, 6, 8, 10),
        "q1": (-1, 0, 3, 7, 7),
        "out": (1, 5, 8, 14, 17),
        "down0": (-1, 0, 2, 20, 23),
        "up1": (1, 7, 11, 18, 20),
        "q2": (0, 4, 7, 10, 13),
        "up0": (1, 8, 13, 20, 25),
        "down1": (1, 11, 15, 22, 25),
    }
)
LAST_TICK = 25


def own_lanes():
    row = lax.broadcasted_iota(jnp.int32, (16, 128), 0)
    lane = lax.broadcasted_iota(jnp.int32, (16, 128), 1)
    return lane == row + 16 * lax.rem(lax.axis_index("dp"), 8)


def placed_gains(first_ref, second_ref):
    row = lax.broadcasted_iota(jnp.int32, (16, 16), 0)
    both = jnp.where(row == 0, first_ref[...].reshape(1, 16).astype(F32), 0.0)
    both = jnp.where(row == 1, second_ref[...].reshape(1, 16).astype(F32), both)
    return dot_nn(both.astype(BF), jnp.where(own_lanes(), 1.0, 0.0).astype(BF)).astype(BF)


def first_kernel(sizes, *refs):
    remote = sizes is not None
    refs = list(refs)
    take = lambda count: [refs.pop(0) for _ in range(count)]
    vl_ref, table_ref, x_ref = take(3)
    if remote:
        first_ref, second_ref, wq_own, wo_own, wu_own, wd_own = take(6)
    else:
        g_ref, w_ref = take(2)
    mixed_ref, qa_ref, qkv_ref, nt_ref, bt_ref = take(5)
    if remote:
        g1_ref, g2_ref, wq_out, wo_ref, wu_ref, wd_ref = take(6)
    bias, bias_t, xhat, xhat_t, n_s, nt_s, held_sem = take(7)
    keep = [pltpu.make_async_copy(nt_s, nt_ref, held_sem.at[0]), pltpu.make_async_copy(bias_t, bt_ref, held_sem.at[1])]
    hp = pl.program_id(0)
    s = pl.program_id(1)
    pairs = pl.num_programs(0)
    S, L = qkv_ref.shape[1:3]
    step = hp * S + s
    R, D = x_ref.shape
    B = 512
    if remote:
        q_own, wq, gains_own, gains, local, send, recv, out_sem = take(8)
        names = list(GATHER_ORDERS)
        own = dict(gains=gains_own, out=wo_own)
        whole = dict(gains=gains, out=wo_ref)
        for half in range(2):
            cols = slice(half * wu_own.shape[1] // 2, (half + 1) * wu_own.shape[1] // 2)
            rows = slice(half * wd_own.shape[0] // 2, (half + 1) * wd_own.shape[0] // 2)
            own["up%d" % half], whole["up%d" % half] = wu_own.at[:, cols], wu_ref.at[:, :, :, :, :, cols]
            own["down%d" % half], whole["down%d" % half] = wd_own.at[rows], wd_ref.at[:, :, :, :, rows]
        for pair in range(4):
            own["q%d" % pair], whole["q%d" % pair] = q_own.at[pair], wq.at[pair]
        place = firsts(sizes, GATHER_ORDERS.values())[0]
        parts = {
            name: Gather(sizes, GATHER_ORDERS[name], own[name], whole[name], local.at[k], send, recv, place[k])
            for k, name in enumerate(names)
        }
        out_copy = lambda pair: pltpu.make_async_copy(wq.at[pair], wq_out.at[pair], out_sem.at[pair])

    def gather_tick(place):
        if remote:
            now = {t // 3: GATHER_SCHEDULE[t + 1] for t in range(place, LAST_TICK - 1, 3) if t + 1 in GATHER_SCHEDULE}
            run_schedule(step, now, parts)

    @pl.when(step == 0)
    def _():
        if remote:
            greet(sizes, SPREAD)
            gains_own[...] = placed_gains(first_ref, second_ref)
            for pair in range(4):
                for part in range(3):
                    q_own[pair, :, part * 128:(part + 1) * 128] = wq_own[:, (part * 4 + pair) * 128:(part * 4 + pair + 1) * 128]

        def all_biases(head, unused):
            def store(n, transposed, tile):
                (bias_t if transposed else bias)[head, n] = tile

            build_bias(table_row(table_ref, head), store)
            return unused

        lax.fori_loop(0, 2 * pairs, all_biases, 0)

        def norm(block, unused):
            at = pl.ds(pl.multiple_of(block * B, B), B)
            xh = ln_parts(x_ref[at, :].astype(F32))[0]
            xhat[at, :] = xh
            return unused

        lax.fori_loop(0, R // B, norm, 0)
        if remote:
            await_greetings(sizes, SPREAD)
            parts["q0"].start(0)
            parts["gains"].start(0)
            run_actions(GATHER_SCHEDULE[-1], parts)

        def turn(block, unused):
            at = pl.ds(pl.multiple_of(block * B, B), B)
            xhat_t[:, at] = xhat[at, :].T
            return unused

        lax.fori_loop(0, R // B, turn, 0)
        if remote:
            parts["gains"].finish(0)
            parts["q0"].finish(0)
            parts["gains"].start(1)
            parts["q0"].start(1)
            run_actions(GATHER_SCHEDULE[0], parts)
            parts["gains"].finish(1)
            tiles = []
            for z in range(sizes[0]):
                tile = jnp.zeros((16, 128), F32)
                for y, a, c in itertools.product(*[range(size) for size in sizes[1:]]):
                    tile = tile + gains[z, y, a, c].astype(F32)
                tiles.append(tile)
            tile = jnp.concatenate(tiles, axis=1)
            g1_ref[...] = tile[0:1, :]
            g2_ref[...] = tile[1:2, :]
            gain = tile[0:1, :]
        else:
            gain = g_ref[...]
        gain_t = jnp.broadcast_to(gain, (8, D)).T[:, 0:1]

        def scale(block, unused):
            at = pl.ds(pl.multiple_of(block * B, B), B)
            n_s[at, :] = (xhat[at, :] * gain).astype(BF)
            nt_s[:, at] = (xhat_t[:, at] * gain_t).astype(BF)
            return unused

        lax.fori_loop(0, R // B, scale, 0)
        for copy in keep:
            copy.start()
        if remote:
            parts["q0"].finish(1)

    gather_tick(0)

    @pl.when(s == 0)
    def _():
        weights = wq[hp].reshape(D, 384) if remote else w_ref[0]
        if remote:
            out_copy(hp).start()
        for seq in range(S):
            for half in range(L // B):
                row = seq * L + half * B
                qkv_ref[0, seq, half * B:(half + 1) * B, :] = dot_nn(n_s[row:row + B, :], weights).astype(BF)

    attend(vl_ref[s], qkv_ref.at[0, s], mixed_ref.at[0], qa_ref.at[0, 0], bias, table_ref, hp, gather_tick)

    @pl.when(step == pairs * S - 1)
    def _():
        for copy in keep:
            copy.wait()
        if remote:
            run_actions(GATHER_SCHEDULE.get(LAST_TICK, []), parts)
            for pair in range(4):
                out_copy(pair).wait()


def attend(valid, qkv_ref, mixed_ref, qa_ref, bias, table_ref, hp, between):
    L = qkv_ref.shape[0]
    nb = L // T
    key = lax.broadcasted_iota(jnp.int32, (L, 1), 0)
    mask = jnp.where(key < valid, 0.0, NEG)
    lane = lax.broadcasted_iota(jnp.int32, (T, 128), 1)
    ks = [halves(h, qkv_ref[:, 128:256], [1.0, 1.0, 1.0, mask], L) for h in range(2)]
    v = qkv_ref[:, 256:384]
    rows = [table_row(table_ref, 2 * hp + h) for h in range(2)]
    for qb in range(nb):
        if qb >= nb - 2:
            between(qb - nb + 3)
        kk = (qb + 1) * T
        qt = qkv_ref[qb * T:(qb + 1) * T, 0:128] * jnp.asarray(0.125, BF)
        outs = []
        for h in range(2):
            qh = halves(h, qt, [None, None, None, 1.0], T)
            sc = dot_nt(qh, ks[h][:kk])
            sc = jnp.concatenate(
                [
                    jnp.concatenate(
                        [
                            biased(sc[i * H:(i + 1) * H, j * H:(j + 1) * H], 2 * qb + i - j, bias.at[2 * hp + h], rows[h])
                            for j in range(kk // H)
                        ],
                        axis=1,
                    )
                    for i in range(2)
                ],
                axis=0,
            )
            mx = jnp.max(sc, axis=1, keepdims=True)
            p = jnp.exp(sc - mx)
            l = jnp.sum(p, axis=1, keepdims=True)
            o = dot_nn(p.astype(BF), v[:kk])
            outs.append(o * (1.0 / l))
            hi, mid, lo = split3(-(mx + jnp.log(l)))
            qa_ref[h, qb * T:(qb + 1) * T, :] = halves(h, qt, [hi, mid, lo, 1.0], T)
        mixed_ref[qb * T:(qb + 1) * T, :] = jnp.where(lane < 64, outs[0], outs[1]).astype(BF)


def whole_block(shape):
    return pl.BlockSpec(shape, lambda *unused: (0,) * len(shape))


def first_half(sizes, vl, table, x, S, weights):
    R, D = x.shape
    L = R // S
    HP = D // 128
    remote = sizes is not None
    anyspace = pl.BlockSpec(memory_space=pl.ANY)
    in_specs = [pl.BlockSpec(memory_space=pltpu.SMEM), whole_block(table.shape), whole_block((R, D))]
    out_specs = [
        pl.BlockSpec((1, L, 128), lambda h, s: (s, 0, h)),
        pl.BlockSpec((1, 1, 2, L, 128), lambda h, s: (s, h, 0, 0, 0)),
        pl.BlockSpec((1, S, L, 384), lambda h, s: (h, 0, 0, 0)),
        anyspace,
        anyspace,
    ]
    out_shape = [
        jax.ShapeDtypeStruct((S, L, D), BF),
        jax.ShapeDtypeStruct((S, HP, 2, L, 128), BF),
        jax.ShapeDtypeStruct((HP, S, L, 384), BF),
        jax.ShapeDtypeStruct((D, R), BF),
        jax.ShapeDtypeStruct((2 * HP, len(VARIED), H, H), F32),
    ]
    scratch = [
        pltpu.VMEM((2 * HP, len(VARIED), H, H), F32), pltpu.VMEM((2 * HP, len(VARIED), H, H), F32), pltpu.VMEM((R, D), F32),
        pltpu.VMEM((D, R), F32), pltpu.VMEM((R, D), BF), pltpu.VMEM((D, R), BF), pltpu.SemaphoreType.DMA((2,)),
    ]
    if remote:
        first, second, wq, wo, wu, wd = weights
        in_specs += [whole_block(first.shape), whole_block(second.shape), whole_block(wq.shape), anyspace, anyspace, anyspace]
        out_specs += [whole_block((1, D)), whole_block((1, D))] + [anyspace] * 4
        out_shape += [jax.ShapeDtypeStruct((1, D), F32)] * 2
        out_shape += [jax.ShapeDtypeStruct((HP,) + sizes + (16, 384), BF)]
        out_shape += [jax.ShapeDtypeStruct(sizes + w.shape, BF) for w in (wo, wu, wd)]
        scratch += [
            pltpu.VMEM((HP, 16, 384), BF),
            pltpu.VMEM((HP,) + sizes + (16, 384), BF),
            pltpu.VMEM((16, 128), BF),
            pltpu.VMEM(sizes + (16, 128), BF),
            pltpu.SemaphoreType.DMA((len(GATHER_ORDERS),)),
        ] + semaphores(sizes, GATHER_ORDERS.values()) + [pltpu.SemaphoreType.DMA((HP,))]
        params = cp(collective_id=1, has_side_effects=True)
    else:
        gain, wq = weights
        in_specs += [whole_block((1, D)), pl.BlockSpec((1, D, 384), lambda h, s: (h, 0, 0))]
        params = cp()
    return pl.pallas_call(
        functools.partial(first_kernel, sizes), grid=(HP, S), in_specs=in_specs, out_specs=out_specs, out_shape=out_shape,
        scratch_shapes=scratch, compiler_params=params,
    )(vl, table, x, *weights)


CXYZ, CYXZ, CXZY, CYZX = (((3,), (a,), (b,), (c,)) for a, b, c in ((2, 1, 0), (1, 2, 0), (2, 0, 1), (1, 0, 2)))
DIRECT = ((3,), (0, 1, 2))
SCATTER_ORDERS = {
    "up0": CYXZ, "down0": CXYZ, "out": CYZX, "up1": CXZY, "down1": CYXZ, "q0": CYZX, "q1": CXZY, "q2": DIRECT, "q3": DIRECT,
}
SCATTER_SCHEDULE = timetable(
    {
        "q3": (8, 9, 12), "out": (1, 2, 3, 5, 6), "up0": (1, 2, 4, 5, 7), "up1": (1, 2, 4, 6, 7), "q1": (4, 5, 6, 7, 8),
        "q0": (2, 3, 5, 7, 8), "down0": (1, 3, 5, 6, 8), "down1": (1, 3, 6, 7, 9), "q2": (6, 7, 11), "table": (8, 9, 11),
    }
)


def last_kernel(sizes, plan, *refs):
    remote = sizes is not None
    refs = list(refs)
    take = lambda count: [refs.pop(0) for _ in range(count)]
    vl_ref, table_ref, bias, qa_ref, qkv_ref, o_ref, g_ref, nt_ref, w_ref, gain_ref, x_ref, ga_ref = take(12)
    if remote:
        wo_terms, wu_terms, wd_terms = take(3)
    gi_ref, tab_ref = take(2)
    if remote:
        results = dict(zip(SCATTER_ORDERS, take(9)))
    else:
        (gw_ref,) = take(1)
    gacc, far, dqt, grads = take(4)
    t = pl.program_id(0)
    pairs = grads.shape[0]
    S = grads.shape[1] // qkv_ref.shape[2]
    steps = pairs * S
    hp = lax.div(t, S)
    s = lax.rem(t, S)
    L = qkv_ref.shape[2]
    R = S * L
    D = x_ref.shape[1]
    if remote:
        wq_terms, tab_own, tab_all, local = take(4)
        terms = dict(out=wo_terms)
        for half in range(2):
            cols = slice(half * wu_terms.shape[5] // 2, (half + 1) * wu_terms.shape[5] // 2)
            rows = slice(half * wd_terms.shape[4] // 2, (half + 1) * wd_terms.shape[4] // 2)
            terms["up%d" % half] = wu_terms.at[:, :, :, :, :, cols]
            terms["down%d" % half] = wd_terms.at[:, :, :, :, rows]
        for pair in range(4):
            terms["q%d" % pair] = wq_terms.at[pair]
        send, recv = refs[-2:]
        place = firsts(sizes, [*SCATTER_ORDERS.values(), SPREAD])[0]
        parts = {}
        for k, name in enumerate(SCATTER_ORDERS):
            sums, landing = plan[name]
            parts[name] = Scatter(
                sizes, SCATTER_ORDERS[name], terms[name], take(len(sums)), take(len(landing)), results[name], send, recv, place[k]
            )
        parts["table"] = Gather(sizes, SPREAD, tab_own, tab_all, local, send, recv, place[-1])

        @pl.when(t == 0)
        def _():
            greet(sizes, SPREAD)

        @pl.when(t == 1)
        def _():
            await_greetings(sizes, SPREAD)

        run_schedule(t, {at: SCATTER_SCHEDULE[at] for at in SCATTER_SCHEDULE if at < 12}, parts)

    @pl.when(t < steps)
    def _():
        @pl.when(s == 0)
        def _():
            gacc[...] = jnp.zeros_like(gacc)
            far[...] = jnp.zeros_like(far)

        at = pl.multiple_of(s * L, L)
        attend_back(vl_ref[s], qa_ref.at[0, 0], qkv_ref.at[0, 0], o_ref[0], g_ref[0], grads, hp, at, bias, table_ref, gacc, far, dqt)

        @pl.when(s == S - 1)
        def _():
            rows = table_terms(gacc, far)
            place = pl.ds(pl.multiple_of(hp * 8, 8), 8)
            (tab_own if remote else tab_ref)[place, :] = rows
            gw = dot_nn(nt_ref[...], grads[hp]).astype(BF)
            if remote:
                wq_terms[hp] = gw.reshape(sizes + (16, 384))
            else:
                gw_ref[hp] = gw

    @pl.when(t >= steps)
    def _():
        B = x_ref.shape[0]
        at = pl.ds(pl.multiple_of((t - steps) * B, B), B)
        xhat, r = ln_parts(x_ref[...].astype(F32))
        dn = dot_nt(
            jnp.concatenate([grads[pair, at, :] for pair in range(pairs)], axis=1),
            jnp.concatenate([w_ref[pair] for pair in range(pairs)], axis=1),
        )
        gi_ref[...] = (ga_ref[...] + ln_back(dn, gain_ref[...], xhat, r)[0]).astype(BF)

    if remote:

        @pl.when(t == pl.num_programs(0) - 1)
        def _():
            run_actions(SCATTER_SCHEDULE[12], parts)
            total = None
            for at in itertools.product(*[range(size) for size in sizes]):
                block = tab_all[at]
                total = block if total is None else total + block
            tab_ref[...] = total


def table_terms(gacc, far):
    lane = lax.broadcasted_iota(jnp.int32, (1, 2 * H), 1)
    m = jnp.where(lane < H, lane, lane - 2 * H)
    bl = lax.broadcasted_iota(jnp.int32, (1, 128), 1)
    rows = []
    for h in range(2):
        row = jnp.zeros((1, 128), F32)
        for b in (14, 15):
            row = row + jnp.where(bl == b, jnp.sum(jnp.sum(far[h, b - 14], axis=0, keepdims=True), axis=1, keepdims=True), 0.0)
        for n, delta in enumerate(VARIED):
            w = jnp.concatenate([gacc[h, n], jnp.zeros((H, H), F32)], axis=1)
            acc = w[:8]
            for a in range(1, H // 8):
                acc = acc + pltpu.roll(w[8 * a:8 * a + 8], 2 * H - 8 * a, 1)
            diag = acc[0:1]
            for a in range(1, 8):
                diag = diag + pltpu.roll(acc[a:a + 1], 2 * H - a, 1)
            dist = delta * H + m
            for b in range(16):
                if LOW[b] >= (delta + 1) * H or (b < 15 and LOW[b + 1] <= (delta - 1) * H):
                    continue
                sel = dist >= LOW[b]
                if b < 15:
                    sel = sel & (dist < LOW[b + 1])
                row = row + jnp.where(bl == b, jnp.sum(jnp.where(sel, diag, 0.0), axis=1, keepdims=True), 0.0)
        rows.append(row)
    return jnp.concatenate(rows + [jnp.zeros((6, 128), F32)], axis=0)


def attend_back(valid, qa_ref, qkv_ref, o, g, grads, hp, first, bias, table_ref, gacc, far, dqt):
    L = qkv_ref.shape[0]
    rows = [table_row(table_ref, 2 * hp + h) for h in range(2)]
    nb = L // T
    key = lax.broadcasted_iota(jnp.int32, (L, 1), 0)
    mask = jnp.where(key < valid, 0.0, NEG)
    lane = lax.broadcasted_iota(jnp.int32, (T, 128), 1)
    prod = g.astype(F32) * o.astype(F32)
    lane_l = lax.broadcasted_iota(jnp.int32, (L, 128), 1)
    k = qkv_ref[:, 128:256]
    ks = [halves(h, k, [1.0, 1.0, 1.0, mask], L) for h in range(2)]
    vs = [halves(h, qkv_ref[:, 256:384], [1.0, 1.0, 1.0], L) for h in range(2)]
    gs = []
    for h in range(2):
        d = jnp.sum(jnp.where((lane_l // 64) == h, prod, 0.0), axis=1, keepdims=True)
        hi, mid, lo = split3(-d)
        gs.append(halves(h, g, [hi, mid, lo], L))
    kt = (k * jnp.asarray(0.125, BF)).T
    for kb in range(nb):
        dks, dvs = [], []
        for h in range(2):
            qh = qa_ref[h]
            st = dot_nt(ks[h][kb * T:(kb + 1) * T], qh[kb * T:])
            dp = dot_nt(vs[h][kb * T:(kb + 1) * T], gs[h][kb * T:])
            st = jnp.concatenate(
                [
                    jnp.concatenate(
                        [biased(st[j * H:(j + 1) * H, i * H:(i + 1) * H], i - j, bias.at[0, h], rows[h]) for i in range(2 * (nb - kb))],
                        axis=1,
                    )
                    for j in range(2)
                ],
                axis=0,
            )
            p = jnp.exp(st)
            ds = p * dp
            pb = p.astype(BF)
            dsb = ds.astype(BF)
            dvs.append(dot_nn(pb, gs[h][kb * T:]))
            dks.append(dot_nn(dsb, qh[kb * T:]))
            for delta in range(2 * (nb - kb)):
                both = [ds[j * H:(j + 1) * H, i * H:(i + 1) * H] for j in range(2) for i in range(2 * (nb - kb)) if i - j == delta]
                both = both[0] if len(both) == 1 else both[0] + both[1]
                if delta in VARIED:
                    gacc[h, VARIED.index(delta)] += both
                else:
                    far[h, 0 if delta == 3 else 1] += jnp.sum(both.reshape(H // 8, 8, H), axis=0)
            r = dot_nn(kt[h * 64:(h + 1) * 64, kb * T:(kb + 1) * T], dsb)
            if kb == 0:
                dqt[h * 64:(h + 1) * 64, :] = r
            else:
                dqt[h * 64:(h + 1) * 64, kb * T:] += r
        at = pl.ds(first + kb * T, T)
        grads[hp, at, 128:256] = jnp.where(lane < 64, dks[0], dks[1]).astype(BF)
        grads[hp, at, 256:384] = jnp.where(lane < 64, dvs[0], dvs[1]).astype(BF)
    grads[hp, pl.ds(first, L), 0:128] = dqt[...].T.astype(BF)


def last_half(sizes, vl, table, bias_t, qa, qkv, mixed, gm, nt, wq, gain, x, ga, ffn_grads):
    HP, S, L, W = qkv.shape
    R, D = x.shape
    B = 512
    steps = HP * S
    remote = sizes is not None
    pair = lambda t: jnp.minimum(t, steps - 1) // S
    seq = lambda t: jnp.minimum(t, steps - 1) % S
    late = pl.BlockSpec((B, D), lambda t: (jnp.maximum(t - steps, 0), 0))
    in_specs = [
        pl.BlockSpec(memory_space=pltpu.SMEM),
        whole_block(table.shape),
        pl.BlockSpec((1, 2, len(VARIED), H, H), lambda t: (pair(t), 0, 0, 0, 0)),
        pl.BlockSpec((1, 1, 2, L, 128), lambda t: (seq(t), pair(t), 0, 0, 0)),
        pl.BlockSpec((1, 1, L, W), lambda t: (pair(t), seq(t), 0, 0)),
        pl.BlockSpec((1, L, 128), lambda t: (seq(t), 0, pair(t))),
        pl.BlockSpec((1, L, 128), lambda t: (seq(t), 0, pair(t))),
        whole_block((D, R)),
        whole_block((HP, D, W)),
        whole_block((1, D)),
        late,
        late,
    ]
    out_specs = [late, whole_block((8 * HP, 128))]
    out_shape = [jax.ShapeDtypeStruct((R, D), BF), jax.ShapeDtypeStruct((8 * HP, 128), F32)]
    scratch = [
        pltpu.VMEM((2, len(VARIED), H, H), F32), pltpu.VMEM((2, 2, 8, H), F32), pltpu.VMEM((128, L), F32),
        pltpu.VMEM((HP, R, W), BF),
    ]
    args = [vl, table, bias_t.reshape(HP, 2, len(VARIED), H, H), qa, qkv, mixed, gm, nt, wq, gain, x, ga]
    plan = None
    if remote:
        count = int(np.prod(sizes))
        terms = [a.reshape(sizes + (a.shape[0] // count, a.shape[1])) for a in ffn_grads]
        args += terms
        in_specs += [whole_block(a.shape) for a in terms]
        (_, D_), (_, U_), (rows_, _) = [a.shape[4:] for a in terms]
        blocks = dict(out=(16, D_), up0=(16, U_ // 2), up1=(16, U_ // 2), down0=(rows_ // 2, D_), down1=(rows_ // 2, D_))
        for k in range(HP):
            blocks["q%d" % k] = (16, W)
        plan = {name: Scatter.shapes(sizes, SCATTER_ORDERS[name], blocks[name]) for name in SCATTER_ORDERS}
        out_specs += [whole_block(blocks[name]) for name in SCATTER_ORDERS]
        out_shape += [jax.ShapeDtypeStruct(blocks[name], F32) for name in SCATTER_ORDERS]
        scratch += [
            pltpu.VMEM((HP,) + sizes + (16, W), BF), pltpu.VMEM((8 * HP, 128), F32), pltpu.VMEM(sizes + (8 * HP, 128), F32),
            pltpu.SemaphoreType.DMA,
        ]
        for name in SCATTER_ORDERS:
            scratch += [pltpu.VMEM(shape, BF) for shape in plan[name][0] + plan[name][1]]
        scratch += semaphores(sizes, [*SCATTER_ORDERS.values(), SPREAD])
        params = cp(collective_id=2, has_side_effects=True)
    else:
        out_specs += [whole_block((HP, D, W))]
        out_shape += [jax.ShapeDtypeStruct((HP, D, W), BF)]
        params = cp()
    return pl.pallas_call(
        functools.partial(last_kernel, sizes, plan), grid=(steps + R // B,), in_specs=in_specs, out_specs=out_specs,
        out_shape=out_shape, scratch_shapes=scratch, compiler_params=params,
    )(*args)


def finish_kernel(*refs):
    refs = list(refs)
    take = lambda count: [refs.pop(0) for _ in range(count)]
    tab_ref, ru0_ref, rd0_ref, ro_ref, ru1_ref, rd1_ref = take(6)
    pieces = take(4)
    first_ref, second_ref, wq_ref, wu_ref = take(4)
    tab_out, wq_out, wo_out, wu_out, wd_out, g1_out, g2_out = refs
    table = jnp.concatenate([tab_ref[8 * pair:8 * pair + 2, :] for pair in range(4)], axis=0)
    tab_out[...] = table[:, :16]
    wo_out[...] = ro_ref[...]
    for half, (ru_ref, rd_ref) in enumerate(((ru0_ref, rd0_ref), (ru1_ref, rd1_ref))):
        wu_out[:, half * ru_ref.shape[1]:(half + 1) * ru_ref.shape[1]] = ru_ref[...]
        wd_out[half * rd_ref.shape[0]:(half + 1) * rd_ref.shape[0], :] = rd_ref[...]
    for pair in range(4):
        for part in range(3):
            wq_out[:, (part * 4 + pair) * 128:(part * 4 + pair + 1) * 128] = pieces[pair][:, part * 128:(part + 1) * 128]
    square = lax.broadcasted_iota(jnp.int32, (16, 16), 0) == lax.broadcasted_iota(jnp.int32, (16, 16), 1)
    for first, w, grad, out in ((first_ref, wq_ref, wq_out, g1_out), (second_ref, wu_ref, wu_out, g2_out)):
        gain = first[...].reshape(1, 16).astype(F32)
        dots = jnp.sum(w[...].astype(F32) * grad[...], axis=1, keepdims=True)
        out[...] = jnp.sum(jnp.where(square, dots, 0.0), axis=0, keepdims=True) / gain


def finish(tab, results, first, second, wq, wu):
    out_shape = [
        jax.ShapeDtypeStruct((8, 16), F32), jax.ShapeDtypeStruct(wq.shape, F32), jax.ShapeDtypeStruct((wu.shape[0], wq.shape[1] // 3), F32),
        jax.ShapeDtypeStruct(wu.shape, F32), jax.ShapeDtypeStruct((2 * results[1].shape[0], wq.shape[1] // 3), F32), jax.ShapeDtypeStruct((1, 16), F32),
        jax.ShapeDtypeStruct((1, 16), F32),
    ]
    return pl.pallas_call(finish_kernel, out_shape=out_shape, compiler_params=cp())(tab, *results, first, second, wq, wu)


def on_device(devices, inputs, valid_len, norm_first, w_qkv, w_out, relative_bucket_table, norm_second, w_up, w_down, output_gradient):
    S, L, D = inputs.shape
    R = S * L
    HP = D // 128
    FFW = w_up.shape[1]
    fast = devices == 32 and D == 512 and S == 2
    table = relative_bucket_table
    x = inputs.reshape(R, D)
    og = output_gradient.reshape(R, D)
    by_pair = lambda w: w.reshape(D, 3, HP, 128).transpose(2, 0, 1, 3).reshape(HP, D, 384)
    if fast:
        sizes = device_grid(devices)
        mixed, qa, qkv, nt, bias_t, g1, g2, wq, wo, wu, wd = first_half(
            sizes, valid_len, table, x, S, [norm_first, norm_second, w_qkv, w_out, w_up, w_down]
        )
        wq, wo, wu, wd = wq.reshape(HP, D, 384), wo.reshape(D, D), wu.reshape(D, FFW), wd.reshape(FFW, D)
    else:
        sizes = None
        g1, wq, wo, g2, wu, wd = [
            lax.all_gather(a, "dp", axis=0, tiled=True) for a in (norm_first, w_qkv, w_out, norm_second, w_up, w_down)
        ]
        g1, g2 = g1.reshape(1, D).astype(F32), g2.reshape(1, D).astype(F32)
        wq = by_pair(wq)
        mixed, qa, qkv, nt, bias_t = first_half(None, valid_len, table, x, S, [g1, wq])
    out, ga, gm, gwo, gwu, gwd = ffn(x, mixed.reshape(R, D), og, g2, wo, wu, wd)
    got = last_half(
        sizes, valid_len, table, bias_t, qa, qkv, mixed, gm.reshape(S, L, D), nt, wq, g1, x, ga, [gwo, gwu, gwd]
    )
    gi, tab = got[:2]
    if fast:
        rt, rq, ro, ru, rd, r1, r2 = finish(tab, got[2:], norm_first, norm_second, w_qkv, w_up)
        r1, r2 = r1.reshape(-1), r2.reshape(-1)
    else:
        gwq = got[2].reshape(HP, D, 3, 128).transpose(1, 2, 0, 3).reshape(D, 3 * D)
        rq, ro, ru, rd = [
            lax.psum_scatter(a.astype(F32), "dp", scatter_dimension=0, tiled=True) for a in (gwq, gwo, gwu, gwd)
        ]
        r1 = jnp.sum(w_qkv.astype(F32) * rq, axis=1) / norm_first.astype(F32)
        r2 = jnp.sum(w_up.astype(F32) * ru, axis=1) / norm_second.astype(F32)
        rt = lax.psum(tab.reshape(HP, 8, 128)[:, :2, :16].reshape(table.shape), "dp")
    return (out.reshape(S, L, D), gi.reshape(S, L, D), r1, rq, ro, rt, r2, ru, rd)


def solution(mesh):
    placed = (
        P("dp", None, None), P("dp"), P("dp"), P("dp", None), P("dp", None), P(), P("dp"), P("dp", None), P("dp", None),
        P("dp", None, None),
    )
    return jax.shard_map(
        functools.partial(on_device, mesh.shape["dp"]),
        mesh=mesh,
        in_specs=placed,
        out_specs=(
            P("dp", None, None), P("dp", None, None), P("dp"), P("dp", None), P("dp", None), P(), P("dp"), P("dp", None),
            P("dp", None),
        ),
        check_vma=False,
    )
```

```python
import functools
import itertools

import jax
import jax.numpy as jnp
import numpy as np
from jax import lax
from jax.experimental import pallas as pl
from jax.experimental.pallas import tpu as pltpu
from jax.sharding import PartitionSpec as P

MESH = pl.DeviceIdType.MESH
F32 = jnp.float32
BF = jnp.bfloat16
EPS = 1e-05


def device_grid(devices):
    return (devices // 8, 2, 2, 2)


def grid_position(sizes):
    rest = lax.axis_index("dp")
    place = []
    for size in reversed(sizes):
        place.append(lax.rem(rest, size))
        rest = lax.div(rest, size)
    return tuple(reversed(place))


def flat(place, sizes):
    index = place[0]
    for one, size in zip(place[1:], sizes[1:]):
        index = index * size + one
    return index


def moves(sizes, group):
    return [m for m in itertools.product(*[range(sizes[a]) for a in group]) if any(m)]


def moved(place, sizes, group, move):
    other = list(place)
    for axis, step in zip(group, move):
        if step:
            other[axis] = lax.rem(place[axis] + step, sizes[axis])
    return tuple(other)


def greet(sizes, groups):
    place = grid_position(sizes)
    barrier = pltpu.get_barrier_semaphore()
    for group in groups:
        for move in moves(sizes, group):
            pl.semaphore_signal(
                barrier,
                inc=1,
                device_id=(flat(moved(place, sizes, group, move), sizes),),
                device_id_type=MESH,
            )


def await_greetings(sizes, groups):
    pl.semaphore_wait(pltpu.get_barrier_semaphore(), sum(len(moves(sizes, group)) for group in groups))


class Gather:
    def __init__(self, sizes, order, own, whole, local_sem, send_sems, recv_sems, first):
        self.sizes, self.order, self.first = sizes, order, first
        self.own, self.whole = own, whole
        self.local_sem, self.send_sems, self.recv_sems = local_sem, send_sems, recv_sems

    def copies(self, phase):
        place = grid_position(self.sizes)
        done = [a for group in self.order[:phase] for a in group]
        group = self.order[phase]
        part = self.whole.at[tuple(slice(None) if a in done else place[a] for a in range(4))]
        return [
            pltpu.make_async_remote_copy(
                src_ref=self.own if phase == 0 else part,
                dst_ref=part,
                send_sem=self.send_sems.at[self.first + sum(len(moves(self.sizes, g)) for g in self.order[:phase]) + k],
                recv_sem=self.recv_sems.at[self.first + sum(len(moves(self.sizes, g)) for g in self.order[:phase]) + k],
                device_id=(flat(moved(place, self.sizes, group, move), self.sizes),),
                device_id_type=MESH,
            )
            for k, move in enumerate(moves(self.sizes, group))
        ]

    def local(self):
        return pltpu.make_async_copy(self.own, self.whole.at[grid_position(self.sizes)], self.local_sem)

    def start(self, phase):
        if phase == 0:
            self.local().start()
        for copy in self.copies(phase):
            copy.start()

    def finish(self, phase):
        if phase == 0:
            self.local().wait()
        for copy in self.copies(phase):
            copy.wait()


class Scatter:
    def __init__(self, sizes, order, terms, sums, landing, result, send_sems, recv_sems, first):
        self.sizes, self.order, self.first = sizes, order, first
        self.held = [terms] + list(sums)
        self.landing, self.result = landing, result
        self.send_sems, self.recv_sems = send_sems, recv_sems

    @staticmethod
    def shapes(sizes, order, block):
        left, sums, landing = set(range(4)), [], []
        for phase, group in enumerate(order):
            left -= set(group)
            lead = tuple(sizes[a] for a in sorted(left))
            slots = int(np.prod([sizes[a] for a in group]))
            landing.append((slots if slots > 2 else 1,) + lead + block)
            if phase < len(order) - 1:
                sums.append(lead + block)
        return sums, landing

    def before(self, phase):
        done = [a for group in self.order[:phase] for a in group]
        return [a for a in range(4) if a not in done]

    def slot(self, phase, place):
        group = self.order[phase]
        if self.landing[phase].shape[0] == 1:
            return 0
        return flat([place[a] for a in group], [self.sizes[a] for a in group])

    def copies(self, phase):
        place = grid_position(self.sizes)
        group = self.order[phase]
        out = []
        for k, move in enumerate(moves(self.sizes, group)):
            other = moved(place, self.sizes, group, move)
            part = tuple(other[a] if a in group else slice(None) for a in self.before(phase))
            out.append(
                pltpu.make_async_remote_copy(
                    src_ref=self.held[phase].at[part],
                    dst_ref=self.landing[phase].at[self.slot(phase, place)],
                    send_sem=self.send_sems.at[self.first + sum(len(moves(self.sizes, g)) for g in self.order[:phase]) + k],
                    recv_sem=self.recv_sems.at[self.first + sum(len(moves(self.sizes, g)) for g in self.order[:phase]) + k],
                    device_id=(flat(other, self.sizes),),
                    device_id_type=MESH,
                )
            )
        return out

    def start(self, phase):
        for copy in self.copies(phase):
            copy.start()

    def finish(self, phase):
        for copy in self.copies(phase):
            copy.wait()
        place = grid_position(self.sizes)
        group = self.order[phase]
        held, landed = self.held[phase], self.landing[phase]
        before = self.before(phase)
        left = [a for a in before if a not in group]
        last = phase == len(self.order) - 1
        target = self.result if last else self.held[phase + 1]

        def one(at):
            spot = dict(zip(left, at))
            mine = held[tuple(place[a] if a in group else spot[a] for a in before)]
            at = tuple(at)
            if landed.shape[0] == 1:
                total = mine.astype(F32) + landed[(0,) + at].astype(F32)
            else:
                landed[(self.slot(phase, place),) + at] = mine
                total = landed[(0,) + at].astype(F32)
                for source in range(1, landed.shape[0]):
                    total = total + landed[(source,) + at].astype(F32)
            if at:
                target[at] = total.astype(target.dtype)
            else:
                target[...] = total.astype(target.dtype)

        if not left:
            one(())
        else:
            lead = [self.sizes[a] for a in left]

            def body(count, unused):
                at = []
                for size in reversed(lead):
                    at.append(lax.rem(count, size))
                    count = lax.div(count, size)
                one(at[::-1])
                return unused

            lax.fori_loop(0, int(np.prod(lead)), body, 0)


def firsts(sizes, orders):
    counts = [sum(len(moves(sizes, group)) for group in order) for order in orders]
    return [sum(counts[:k]) for k in range(len(counts))], sum(counts)


def semaphores(sizes, orders):
    return [pltpu.SemaphoreType.DMA((firsts(sizes, orders)[1],))] * 2


def run_actions(actions, parts):
    for action, item, phase in actions:
        getattr(parts[item], action)(phase)


def run_schedule(tick, schedule, parts):
    for at, actions in sorted(schedule.items()):

        @pl.when(tick == at)
        def _(actions=actions):
            run_actions(actions, parts)


LOW=(0,1,2,3,4,5,6,7,8,12,16,32,64,128,256,512)
T=256
NEG=-1e30
def cp(**k): return pltpu.CompilerParams(vmem_limit_bytes=56*2**20, **k)
def dot_nt(a,b): return lax.dot_general(a,b,(((1,),(1,)),((),())),preferred_element_type=jnp.float32)
def dot_nn(a,b): return jnp.dot(a,b,preferred_element_type=jnp.float32)
def dot_tn(a,b): return lax.dot_general(a,b,(((0,),(0,)),((),())),preferred_element_type=jnp.float32)

def bias_of(dist, row):
    out=jnp.zeros(dist.shape,jnp.float32)+row[:,0:1]
    for b in range(1,16):
        out=jnp.where(dist>=LOW[b],row[:,b:b+1],out)
    return jnp.where(dist<0,NEG,out)

def table_row(table_ref,head):
    whole=table_ref[...].astype(jnp.float32)
    at=lax.broadcasted_iota(jnp.int32,whole.shape,0)
    return jnp.sum(jnp.where(at==head,whole,0.0),axis=0,keepdims=True)

H = 128
VARIED = (0, 1, 2, 4)


def build_bias(row, store):
    lane = lax.broadcasted_iota(jnp.int32, (1, 2 * H), 1)
    m = jnp.where(lane < H, lane, lane - 2 * H)
    for n, delta in enumerate(VARIED):
        for transposed in (False, True):
            w = bias_of(delta * H + (m if transposed else -m), row)
            tile = pltpu.roll(jnp.broadcast_to(w, (H, 2 * H)), 0, 1, stride=1, stride_axis=0)
            store(n, transposed, tile[:, :H])


def biased(tile, delta, bias, row):
    if delta < 0:
        return jnp.full((H, H), NEG, F32)
    if delta in VARIED:
        return tile + bias[VARIED.index(delta)]
    return tile + row[:, 14:15] if delta == 3 else tile + row[:, 15:16]

def split3(v):
    hi=v.astype(jnp.bfloat16); r=v-hi.astype(jnp.float32)
    mid=r.astype(jnp.bfloat16); lo=(r-mid.astype(jnp.float32)).astype(jnp.bfloat16)
    return hi,mid,lo

def halves(h, main, extra, rows):
    lane=lax.broadcasted_iota(jnp.int32,(rows,128),1)
    out=jnp.where((lane//64)==h,main,jnp.zeros((),main.dtype))
    base=64*(1-h)
    for n,e in enumerate(extra):
        if e is not None:
            out=jnp.where(lane==base+n,jnp.broadcast_to(e,(rows,128)).astype(jnp.bfloat16),out)
    return out

def ln_parts(v):
    c=v-jnp.mean(v,axis=1,keepdims=True)
    r=lax.rsqrt(jnp.mean(c*c,axis=1,keepdims=True)+EPS)
    return c*r, r
def ln_back(e_in,gain,xhat,r):
    e=e_in*gain
    gv=r*(e-jnp.mean(e,axis=1,keepdims=True)-xhat*jnp.mean(e*xhat,axis=1,keepdims=True))
    return (gv,)

def ffn_kernel(x_ref, m_ref, og_ref, g_ref, wo_ref, wu_ref, wd_ref, out_ref, ga_ref, gm_ref, gwo_ref, gwu_ref, gwd_ref,
               hid_s, gp_s, gb_s, nt_s, ogt_s, mt_s):
    i = pl.program_id(0)
    B = x_ref.shape[0]
    R = hid_s.shape[0]
    blocks = R // B
    C = hid_s.shape[1] // FFN_PARTS

    @pl.when(i < blocks)
    def _():
        at = pl.ds(pl.multiple_of(i * B, B), B)
        m = m_ref[...]
        og = og_ref[...]
        after = x_ref[...].astype(F32) + dot_nn(m, wo_ref[...])
        xhat, r = ln_parts(after)
        gain = g_ref[...]
        n = (xhat * gain).astype(BF)
        c = 0.7978845608028654
        for j in range(FFN_PARTS):
            cols = slice(j * C, (j + 1) * C)
            pre = dot_nn(n, wu_ref[:, cols])
            dh = dot_nt(og, wd_ref[cols, :])
            a = c + (c * 0.044715) * (pre * pre)
            half = 0.5 + 0.5 * jnp.tanh(pre * a)
            h = pre * half
            gp_s[at, cols] = (dh * (half + (h - h * half) * (6.0 * a - 4.0 * c))).astype(BF)
            hid_s[at, cols] = h.astype(BF)
        out_ref[...] = (after + dot_nn(hid_s[at, :], wd_ref[...])).astype(BF)
        dn = dot_nt(gp_s[at, :], wu_ref[...])
        (gv,) = ln_back(dn, gain, xhat, r)
        ga = og.astype(F32) + gv
        ga_ref[...] = ga
        gb = ga.astype(BF)
        gb_s[at, :] = gb
        gm_ref[...] = dot_nt(gb, wo_ref[...]).astype(BF)
        nt_s[:, at] = n.T
        ogt_s[:, at] = og.T
        mt_s[:, at] = m.T

    @pl.when(i >= blocks)
    def _():
        j = i - blocks
        cols = pl.ds(pl.multiple_of(j * C, C), C)
        gwd_ref[...] = dot_nn(ogt_s[...], hid_s[:, cols]).astype(BF).T
        gwu_ref[...] = dot_nn(nt_s[...], gp_s[:, cols]).astype(BF)
        share = mt_s.shape[0] // FFN_PARTS
        gwo_ref[...] = dot_nn(mt_s[pl.ds(pl.multiple_of(j * share, share), share), :], gb_s[...]).astype(BF)


FFN_PARTS = 4


def ffn(x, m, og, gain, wo, wu, wd, B=512):
    R, D = x.shape
    FF = wu.shape[1]
    n = R // B
    C = FF // FFN_PARTS
    row = pl.BlockSpec((B, D), lambda i: (jnp.minimum(i, n - 1), 0))
    late = lambda i: jnp.maximum(i - n, 0)
    return pl.pallas_call(
        ffn_kernel,
        grid=(n + FFN_PARTS,),
        in_specs=[row, row, row, whole_block((1, D)), whole_block((D, D)), whole_block((D, FF)), whole_block((FF, D))],
        out_specs=[
            row, row, row,
            pl.BlockSpec((D // FFN_PARTS, D), lambda i: (late(i), 0)),
            pl.BlockSpec((D, C), lambda i: (0, late(i))),
            pl.BlockSpec((C, D), lambda i: (late(i), 0)),
        ],
        out_shape=[
            jax.ShapeDtypeStruct((R, D), BF), jax.ShapeDtypeStruct((R, D), F32), jax.ShapeDtypeStruct((R, D), BF),
            jax.ShapeDtypeStruct((D, D), BF), jax.ShapeDtypeStruct((D, FF), BF), jax.ShapeDtypeStruct((FF, D), BF),
        ],
        scratch_shapes=[
            pltpu.VMEM((R, FF), BF), pltpu.VMEM((R, FF), BF), pltpu.VMEM((R, D), BF), pltpu.VMEM((D, R), BF),
            pltpu.VMEM((D, R), BF), pltpu.VMEM((D, R), BF),
        ],
        compiler_params=cp(),
    )(x, m, og, gain, wo, wu, wd)


SPREAD = ((0, 1, 2), (3,))
ZYX, ZXY, YZX, XZY, XYZ, YXZ = (
    ((a,), (b,), (c,), (3,)) for a, b, c in ((0, 1, 2), (0, 2, 1), (1, 0, 2), (2, 0, 1), (2, 1, 0), (1, 2, 0))
)
GATHER_ORDERS = {
    "q0": SPREAD,
    "gains": SPREAD,
    "q3": ZYX,
    "q1": XZY,
    "out": ZYX,
    "down0": XYZ,
    "up1": ZXY,
    "q2": ZXY,
    "up0": ZYX,
    "down1": ZXY,
}


def timetable(starts):
    table = {}
    for item, ticks in starts.items():
        for phase, tick in enumerate(ticks):
            if phase:
                table.setdefault(tick, []).append(("finish", item, phase - 1))
            if phase < len(ticks) - 1:
                table.setdefault(tick, []).append(("start", item, phase))
    return table


GATHER_SCHEDULE = timetable(
    {
        "q3": (0, 2, 6, 8, 10),
        "q1": (-1, 0, 3, 7, 7),
        "out": (1, 5, 8, 14, 17),
        "down0": (-1, 0, 2, 20, 23),
        "up1": (1, 7, 11, 18, 20),
        "q2": (0, 4, 7, 10, 13),
        "up0": (1, 8, 13, 20, 25),
        "down1": (1, 11, 15, 22, 25),
    }
)
LAST_TICK = 25


def own_lanes():
    row = lax.broadcasted_iota(jnp.int32, (16, 128), 0)
    lane = lax.broadcasted_iota(jnp.int32, (16, 128), 1)
    return lane == row + 16 * lax.rem(lax.axis_index("dp"), 8)


def placed_gains(first_ref, second_ref):
    row = lax.broadcasted_iota(jnp.int32, (16, 16), 0)
    both = jnp.where(row == 0, first_ref[...].reshape(1, 16).astype(F32), 0.0)
    both = jnp.where(row == 1, second_ref[...].reshape(1, 16).astype(F32), both)
    return dot_nn(both.astype(BF), jnp.where(own_lanes(), 1.0, 0.0).astype(BF)).astype(BF)


def first_kernel(sizes, *refs):
    remote = sizes is not None
    refs = list(refs)
    take = lambda count: [refs.pop(0) for _ in range(count)]
    vl_ref, table_ref, x_ref = take(3)
    if remote:
        first_ref, second_ref, wq_own, wo_own, wu_own, wd_own = take(6)
    else:
        g_ref, w_ref = take(2)
    mixed_ref, qa_ref, qkv_ref, nt_ref, bt_ref = take(5)
    if remote:
        g1_ref, g2_ref, wq_out, wo_ref, wu_ref, wd_ref = take(6)
    bias, bias_t, xhat, xhat_t, n_s, nt_s, held_sem = take(7)
    keep = [pltpu.make_async_copy(nt_s, nt_ref, held_sem.at[0]), pltpu.make_async_copy(bias_t, bt_ref, held_sem.at[1])]
    hp = pl.program_id(0)
    s = pl.program_id(1)
    pairs = pl.num_programs(0)
    S, L = qkv_ref.shape[1:3]
    step = hp * S + s
    R, D = x_ref.shape
    B = 512
    if remote:
        q_own, wq, gains_own, gains, local, send, recv, out_sem = take(8)
        names = list(GATHER_ORDERS)
        own = dict(gains=gains_own, out=wo_own)
        whole = dict(gains=gains, out=wo_ref)
        for half in range(2):
            cols = slice(half * wu_own.shape[1] // 2, (half + 1) * wu_own.shape[1] // 2)
            rows = slice(half * wd_own.shape[0] // 2, (half + 1) * wd_own.shape[0] // 2)
            own["up%d" % half], whole["up%d" % half] = wu_own.at[:, cols], wu_ref.at[:, :, :, :, :, cols]
            own["down%d" % half], whole["down%d" % half] = wd_own.at[rows], wd_ref.at[:, :, :, :, rows]
        for pair in range(4):
            own["q%d" % pair], whole["q%d" % pair] = q_own.at[pair], wq.at[pair]
        place = firsts(sizes, GATHER_ORDERS.values())[0]
        parts = {
            name: Gather(sizes, GATHER_ORDERS[name], own[name], whole[name], local.at[k], send, recv, place[k])
            for k, name in enumerate(names)
        }
        out_copy = lambda pair: pltpu.make_async_copy(wq.at[pair], wq_out.at[pair], out_sem.at[pair])

    def gather_tick(place):
        if remote:
            now = {t // 3: GATHER_SCHEDULE[t + 1] for t in range(place, LAST_TICK - 1, 3) if t + 1 in GATHER_SCHEDULE}
            run_schedule(step, now, parts)

    @pl.when(step == 0)
    def _():
        if remote:
            greet(sizes, SPREAD)
            gains_own[...] = placed_gains(first_ref, second_ref)
            for pair in range(4):
                for part in range(3):
                    q_own[pair, :, part * 128:(part + 1) * 128] = wq_own[:, (part * 4 + pair) * 128:(part * 4 + pair + 1) * 128]

        def all_biases(head, unused):
            def store(n, transposed, tile):
                (bias_t if transposed else bias)[head, n] = tile

            build_bias(table_row(table_ref, head), store)
            return unused

        lax.fori_loop(0, 2 * pairs, all_biases, 0)

        def norm(block, unused):
            at = pl.ds(pl.multiple_of(block * B, B), B)
            xh = ln_parts(x_ref[at, :].astype(F32))[0]
            xhat[at, :] = xh
            return unused

        lax.fori_loop(0, R // B, norm, 0)
        if remote:
            await_greetings(sizes, SPREAD)
            parts["q0"].start(0)
            parts["gains"].start(0)
            run_actions(GATHER_SCHEDULE[-1], parts)

        def turn(block, unused):
            at = pl.ds(pl.multiple_of(block * B, B), B)
            xhat_t[:, at] = xhat[at, :].T
            return unused

        lax.fori_loop(0, R // B, turn, 0)
        if remote:
            parts["gains"].finish(0)
            parts["q0"].finish(0)
            parts["gains"].start(1)
            parts["q0"].start(1)
            run_actions(GATHER_SCHEDULE[0], parts)
            parts["gains"].finish(1)
            tiles = []
            for z in range(sizes[0]):
                tile = jnp.zeros((16, 128), F32)
                for y, a, c in itertools.product(*[range(size) for size in sizes[1:]]):
                    tile = tile + gains[z, y, a, c].astype(F32)
                tiles.append(tile)
            tile = jnp.concatenate(tiles, axis=1)
            g1_ref[...] = tile[0:1, :]
            g2_ref[...] = tile[1:2, :]
            gain = tile[0:1, :]
        else:
            gain = g_ref[...]
        gain_t = jnp.broadcast_to(gain, (8, D)).T[:, 0:1]

        def scale(block, unused):
            at = pl.ds(pl.multiple_of(block * B, B), B)
            n_s[at, :] = (xhat[at, :] * gain).astype(BF)
            nt_s[:, at] = (xhat_t[:, at] * gain_t).astype(BF)
            return unused

        lax.fori_loop(0, R // B, scale, 0)
        for copy in keep:
            copy.start()
        if remote:
            parts["q0"].finish(1)

    gather_tick(0)

    @pl.when(s == 0)
    def _():
        weights = wq[hp].reshape(D, 384) if remote else w_ref[0]
        if remote:
            out_copy(hp).start()
        for seq in range(S):
            for half in range(L // B):
                row = seq * L + half * B
                qkv_ref[0, seq, half * B:(half + 1) * B, :] = dot_nn(n_s[row:row + B, :], weights).astype(BF)

    attend(vl_ref[s], qkv_ref.at[0, s], mixed_ref.at[0], qa_ref.at[0, 0], bias, table_ref, hp, gather_tick)

    @pl.when(step == pairs * S - 1)
    def _():
        for copy in keep:
            copy.wait()
        if remote:
            run_actions(GATHER_SCHEDULE.get(LAST_TICK, []), parts)
            for pair in range(4):
                out_copy(pair).wait()


def attend(valid, qkv_ref, mixed_ref, qa_ref, bias, table_ref, hp, between):
    L = qkv_ref.shape[0]
    nb = L // T
    key = lax.broadcasted_iota(jnp.int32, (L, 1), 0)
    mask = jnp.where(key < valid, 0.0, NEG)
    lane = lax.broadcasted_iota(jnp.int32, (T, 128), 1)
    ks = [halves(h, qkv_ref[:, 128:256], [1.0, 1.0, 1.0, mask], L) for h in range(2)]
    vs = [halves(h, qkv_ref[:, 256:384], [1.0], L) for h in range(2)]
    rows = [table_row(table_ref, 2 * hp + h) for h in range(2)]
    for qb in range(nb):
        if qb >= nb - 2:
            between(qb - nb + 3)
        kk = (qb + 1) * T
        qt = qkv_ref[qb * T:(qb + 1) * T, 0:128] * jnp.asarray(0.125, BF)
        outs = []
        for h in range(2):
            qh = halves(h, qt, [None, None, None, 1.0], T)
            sc = dot_nt(qh, ks[h][:kk])
            sc = jnp.concatenate(
                [
                    jnp.concatenate(
                        [
                            biased(sc[i * H:(i + 1) * H, j * H:(j + 1) * H], 2 * qb + i - j, bias.at[2 * hp + h], rows[h])
                            for j in range(kk // H)
                        ],
                        axis=1,
                    )
                    for i in range(2)
                ],
                axis=0,
            )
            mx = jnp.max(sc, axis=1, keepdims=True)
            p = jnp.exp(sc - mx)
            o = dot_nn(p.astype(BF), vs[h][:kk])
            l = o[:, 64 - 64 * h:65 - 64 * h]
            outs.append(o * (1.0 / l))
            hi, mid, lo = split3(-(mx + jnp.log(l)))
            qa_ref[h, qb * T:(qb + 1) * T, :] = halves(h, qt, [hi, mid, lo, 1.0], T)
        mixed_ref[qb * T:(qb + 1) * T, :] = jnp.where(lane < 64, outs[0], outs[1]).astype(BF)


def whole_block(shape):
    return pl.BlockSpec(shape, lambda *unused: (0,) * len(shape))


def first_half(sizes, vl, table, x, S, weights):
    R, D = x.shape
    L = R // S
    HP = D // 128
    remote = sizes is not None
    anyspace = pl.BlockSpec(memory_space=pl.ANY)
    in_specs = [pl.BlockSpec(memory_space=pltpu.SMEM), whole_block(table.shape), whole_block((R, D))]
    out_specs = [
        pl.BlockSpec((1, L, 128), lambda h, s: (s, 0, h)),
        pl.BlockSpec((1, 1, 2, L, 128), lambda h, s: (s, h, 0, 0, 0)),
        pl.BlockSpec((1, S, L, 384), lambda h, s: (h, 0, 0, 0)),
        anyspace,
        anyspace,
    ]
    out_shape = [
        jax.ShapeDtypeStruct((S, L, D), BF),
        jax.ShapeDtypeStruct((S, HP, 2, L, 128), BF),
        jax.ShapeDtypeStruct((HP, S, L, 384), BF),
        jax.ShapeDtypeStruct((D, R), BF),
        jax.ShapeDtypeStruct((2 * HP, len(VARIED), H, H), F32),
    ]
    scratch = [
        pltpu.VMEM((2 * HP, len(VARIED), H, H), F32), pltpu.VMEM((2 * HP, len(VARIED), H, H), F32), pltpu.VMEM((R, D), F32),
        pltpu.VMEM((D, R), F32), pltpu.VMEM((R, D), BF), pltpu.VMEM((D, R), BF), pltpu.SemaphoreType.DMA((2,)),
    ]
    if remote:
        first, second, wq, wo, wu, wd = weights
        in_specs += [whole_block(first.shape), whole_block(second.shape), whole_block(wq.shape), anyspace, anyspace, anyspace]
        out_specs += [whole_block((1, D)), whole_block((1, D))] + [anyspace] * 4
        out_shape += [jax.ShapeDtypeStruct((1, D), F32)] * 2
        out_shape += [jax.ShapeDtypeStruct((HP,) + sizes + (16, 384), BF)]
        out_shape += [jax.ShapeDtypeStruct(sizes + w.shape, BF) for w in (wo, wu, wd)]
        scratch += [
            pltpu.VMEM((HP, 16, 384), BF),
            pltpu.VMEM((HP,) + sizes + (16, 384), BF),
            pltpu.VMEM((16, 128), BF),
            pltpu.VMEM(sizes + (16, 128), BF),
            pltpu.SemaphoreType.DMA((len(GATHER_ORDERS),)),
        ] + semaphores(sizes, GATHER_ORDERS.values()) + [pltpu.SemaphoreType.DMA((HP,))]
        params = cp(collective_id=1, has_side_effects=True)
    else:
        gain, wq = weights
        in_specs += [whole_block((1, D)), pl.BlockSpec((1, D, 384), lambda h, s: (h, 0, 0))]
        params = cp()
    return pl.pallas_call(
        functools.partial(first_kernel, sizes), grid=(HP, S), in_specs=in_specs, out_specs=out_specs, out_shape=out_shape,
        scratch_shapes=scratch, compiler_params=params,
    )(vl, table, x, *weights)


CXYZ, CYXZ, CXZY, CYZX = (((3,), (a,), (b,), (c,)) for a, b, c in ((2, 1, 0), (1, 2, 0), (2, 0, 1), (1, 0, 2)))
DIRECT = ((3,), (0, 1, 2))
SCATTER_ORDERS = {
    "up0": CYXZ, "down0": CXYZ, "out": CYZX, "up1": CXZY, "down1": CYXZ, "q0": CYZX, "q1": CXZY, "q2": DIRECT, "q3": DIRECT,
}
SCATTER_SCHEDULE = timetable(
    {
        "q3": (8, 9, 12), "out": (1, 2, 3, 5, 6), "up0": (1, 2, 4, 5, 7), "up1": (1, 2, 4, 6, 7), "q1": (4, 5, 6, 7, 8),
        "q0": (2, 3, 5, 7, 8), "down0": (1, 3, 5, 6, 8), "down1": (1, 3, 6, 7, 9), "q2": (6, 7, 11), "table": (8, 9, 11),
    }
)


def last_kernel(sizes, plan, *refs):
    remote = sizes is not None
    refs = list(refs)
    take = lambda count: [refs.pop(0) for _ in range(count)]
    vl_ref, table_ref, bias, qa_ref, qkv_ref, o_ref, g_ref, nt_any, w_any, gain_ref, x_ref, ga_ref = take(12)
    if remote:
        terms_any = take(3)
    gi_ref, tab_ref = take(2)
    if remote:
        results = dict(zip(SCATTER_ORDERS, take(9)))
    else:
        (gw_ref,) = take(1)
    gacc, far, dqt, grads, nt_ref, w_ref, load_sem = take(7)
    loads = [(nt_any, nt_ref), (w_any, w_ref)]
    if remote:
        wo_terms, wu_terms, wd_terms = terms_vm = take(3)
        loads += list(zip(terms_any, terms_vm))
    loads = [pltpu.make_async_copy(a, b, load_sem.at[k]) for k, (a, b) in enumerate(loads)]
    t = pl.program_id(0)
    pairs = grads.shape[0]
    S = grads.shape[1] // qkv_ref.shape[2]
    steps = pairs * S
    hp = lax.div(t, S)
    s = lax.rem(t, S)
    L = qkv_ref.shape[2]
    R = S * L
    D = x_ref.shape[1]

    @pl.when(t == 0)
    def _():
        for load in loads:
            load.start()

    @pl.when(t == 1)
    def _():
        for load in loads:
            load.wait()

    if remote:
        wq_terms, tab_own, tab_all, local = take(4)
        terms = dict(out=wo_terms)
        for half in range(2):
            cols = slice(half * wu_terms.shape[5] // 2, (half + 1) * wu_terms.shape[5] // 2)
            rows = slice(half * wd_terms.shape[4] // 2, (half + 1) * wd_terms.shape[4] // 2)
            terms["up%d" % half] = wu_terms.at[:, :, :, :, :, cols]
            terms["down%d" % half] = wd_terms.at[:, :, :, :, rows]
        for pair in range(4):
            terms["q%d" % pair] = wq_terms.at[pair]
        send, recv = refs[-2:]
        place = firsts(sizes, [*SCATTER_ORDERS.values(), SPREAD])[0]
        parts = {}
        for k, name in enumerate(SCATTER_ORDERS):
            sums, landing = plan[name]
            parts[name] = Scatter(
                sizes, SCATTER_ORDERS[name], terms[name], take(len(sums)), take(len(landing)), results[name], send, recv, place[k]
            )
        parts["table"] = Gather(sizes, SPREAD, tab_own, tab_all, local, send, recv, place[-1])

        @pl.when(t == 0)
        def _():
            greet(sizes, SPREAD)

        @pl.when(t == 1)
        def _():
            await_greetings(sizes, SPREAD)

        run_schedule(t, {at: SCATTER_SCHEDULE[at] for at in SCATTER_SCHEDULE if at < 12}, parts)

    @pl.when(t < steps)
    def _():
        @pl.when(s == 0)
        def _():
            gacc[...] = jnp.zeros_like(gacc)
            far[...] = jnp.zeros_like(far)

        at = pl.multiple_of(s * L, L)
        attend_back(vl_ref[s], qa_ref.at[0, 0], qkv_ref.at[0, 0], o_ref[0], g_ref[0], grads, hp, at, bias, table_ref, gacc, far, dqt)

        @pl.when(s == S - 1)
        def _():
            rows = table_terms(gacc, far)
            place = pl.ds(pl.multiple_of(hp * 8, 8), 8)
            (tab_own if remote else tab_ref)[place, :] = rows
            gw = dot_nn(nt_ref[...], grads[hp]).astype(BF)
            if remote:
                wq_terms[hp] = gw.reshape(sizes + (16, 384))
            else:
                gw_ref[hp] = gw

    @pl.when(t >= steps)
    def _():
        B = x_ref.shape[0]
        at = pl.ds(pl.multiple_of((t - steps) * B, B), B)
        xhat, r = ln_parts(x_ref[...].astype(F32))
        dn = dot_nt(
            jnp.concatenate([grads[pair, at, :] for pair in range(pairs)], axis=1),
            jnp.concatenate([w_ref[pair] for pair in range(pairs)], axis=1),
        )
        gi_ref[...] = (ga_ref[...] + ln_back(dn, gain_ref[...], xhat, r)[0]).astype(BF)

    if remote:

        @pl.when(t == pl.num_programs(0) - 1)
        def _():
            run_actions(SCATTER_SCHEDULE[12], parts)
            total = None
            for at in itertools.product(*[range(size) for size in sizes]):
                block = tab_all[at]
                total = block if total is None else total + block
            tab_ref[...] = total


def table_terms(gacc, far):
    lane = lax.broadcasted_iota(jnp.int32, (1, 2 * H), 1)
    m = jnp.where(lane < H, lane, lane - 2 * H)
    bl = lax.broadcasted_iota(jnp.int32, (1, 128), 1)
    rows = []
    for h in range(2):
        row = jnp.zeros((1, 128), F32)
        for b in (14, 15):
            row = row + jnp.where(bl == b, jnp.sum(jnp.sum(far[h, b - 14], axis=0, keepdims=True), axis=1, keepdims=True), 0.0)
        for n, delta in enumerate(VARIED):
            w = jnp.concatenate([gacc[h, n], jnp.zeros((H, H), F32)], axis=1)
            acc = w[:8]
            for a in range(1, H // 8):
                acc = acc + pltpu.roll(w[8 * a:8 * a + 8], 2 * H - 8 * a, 1)
            diag = acc[0:1]
            for a in range(1, 8):
                diag = diag + pltpu.roll(acc[a:a + 1], 2 * H - a, 1)
            dist = delta * H + m
            for b in range(16):
                if LOW[b] >= (delta + 1) * H or (b < 15 and LOW[b + 1] <= (delta - 1) * H):
                    continue
                sel = dist >= LOW[b]
                if b < 15:
                    sel = sel & (dist < LOW[b + 1])
                row = row + jnp.where(bl == b, jnp.sum(jnp.where(sel, diag, 0.0), axis=1, keepdims=True), 0.0)
        rows.append(row)
    return jnp.concatenate(rows + [jnp.zeros((6, 128), F32)], axis=0)


def attend_back(valid, qa_ref, qkv_ref, o, g, grads, hp, first, bias, table_ref, gacc, far, dqt):
    L = qkv_ref.shape[0]
    rows = [table_row(table_ref, 2 * hp + h) for h in range(2)]
    nb = L // T
    key = lax.broadcasted_iota(jnp.int32, (L, 1), 0)
    mask = jnp.where(key < valid, 0.0, NEG)
    lane = lax.broadcasted_iota(jnp.int32, (T, 128), 1)
    prod = g.astype(F32) * o.astype(F32)
    lane_l = lax.broadcasted_iota(jnp.int32, (L, 128), 1)
    k = qkv_ref[:, 128:256]
    ks = [halves(h, k, [1.0, 1.0, 1.0, mask], L) for h in range(2)]
    vs = [halves(h, qkv_ref[:, 256:384], [1.0, 1.0, 1.0], L) for h in range(2)]
    gs = []
    for h in range(2):
        d = jnp.sum(jnp.where((lane_l // 64) == h, prod, 0.0), axis=1, keepdims=True)
        hi, mid, lo = split3(-d)
        gs.append(halves(h, g, [hi, mid, lo], L))
    kt = (k * jnp.asarray(0.125, BF)).T
    for kb in range(nb):
        dks, dvs = [], []
        for h in range(2):
            qh = qa_ref[h]
            st = dot_nt(ks[h][kb * T:(kb + 1) * T], qh[kb * T:])
            dp = dot_nt(vs[h][kb * T:(kb + 1) * T], gs[h][kb * T:])
            st = jnp.concatenate(
                [
                    jnp.concatenate(
                        [biased(st[j * H:(j + 1) * H, i * H:(i + 1) * H], i - j, bias.at[0, h], rows[h]) for i in range(2 * (nb - kb))],
                        axis=1,
                    )
                    for j in range(2)
                ],
                axis=0,
            )
            p = jnp.exp(st)
            ds = p * dp
            pb = p.astype(BF)
            dsb = ds.astype(BF)
            dvs.append(dot_nn(pb, gs[h][kb * T:]))
            dks.append(dot_nn(dsb, qh[kb * T:]))
            for delta in range(2 * (nb - kb)):
                both = [ds[j * H:(j + 1) * H, i * H:(i + 1) * H] for j in range(2) for i in range(2 * (nb - kb)) if i - j == delta]
                both = both[0] if len(both) == 1 else both[0] + both[1]
                if delta in VARIED:
                    gacc[h, VARIED.index(delta)] += both
                else:
                    far[h, 0 if delta == 3 else 1] += jnp.sum(both.reshape(H // 8, 8, H), axis=0)
            r = dot_nn(kt[h * 64:(h + 1) * 64, kb * T:(kb + 1) * T], dsb)
            if kb == 0:
                dqt[h * 64:(h + 1) * 64, :] = r
            else:
                dqt[h * 64:(h + 1) * 64, kb * T:] += r
        at = pl.ds(first + kb * T, T)
        grads[hp, at, 128:256] = jnp.where(lane < 64, dks[0], dks[1]).astype(BF)
        grads[hp, at, 256:384] = jnp.where(lane < 64, dvs[0], dvs[1]).astype(BF)
    grads[hp, pl.ds(first, L), 0:128] = dqt[...].T.astype(BF)


def last_half(sizes, vl, table, bias_t, qa, qkv, mixed, gm, nt, wq, gain, x, ga, ffn_grads):
    HP, S, L, W = qkv.shape
    R, D = x.shape
    B = 512
    steps = HP * S
    remote = sizes is not None
    pair = lambda t: jnp.minimum(t, steps - 1) // S
    seq = lambda t: jnp.minimum(t, steps - 1) % S
    late = pl.BlockSpec((B, D), lambda t: (jnp.maximum(t - steps, 0), 0))
    in_specs = [
        pl.BlockSpec(memory_space=pltpu.SMEM),
        whole_block(table.shape),
        pl.BlockSpec((1, 2, len(VARIED), H, H), lambda t: (pair(t), 0, 0, 0, 0)),
        pl.BlockSpec((1, 1, 2, L, 128), lambda t: (seq(t), pair(t), 0, 0, 0)),
        pl.BlockSpec((1, 1, L, W), lambda t: (pair(t), seq(t), 0, 0)),
        pl.BlockSpec((1, L, 128), lambda t: (seq(t), 0, pair(t))),
        pl.BlockSpec((1, L, 128), lambda t: (seq(t), 0, pair(t))),
        pl.BlockSpec(memory_space=pl.ANY),
        pl.BlockSpec(memory_space=pl.ANY),
        whole_block((1, D)),
        late,
        late,
    ]
    out_specs = [late, whole_block((8 * HP, 128))]
    out_shape = [jax.ShapeDtypeStruct((R, D), BF), jax.ShapeDtypeStruct((8 * HP, 128), F32)]
    scratch = [
        pltpu.VMEM((2, len(VARIED), H, H), F32), pltpu.VMEM((2, 2, 8, H), F32), pltpu.VMEM((128, L), F32),
        pltpu.VMEM((HP, R, W), BF), pltpu.VMEM((D, R), BF), pltpu.VMEM((HP, D, W), BF),
        pltpu.SemaphoreType.DMA((5 if remote else 2,)),
    ]
    args = [vl, table, bias_t.reshape(HP, 2, len(VARIED), H, H), qa, qkv, mixed, gm, nt, wq, gain, x, ga]
    plan = None
    if remote:
        count = int(np.prod(sizes))
        terms = [a.reshape(sizes + (a.shape[0] // count, a.shape[1])) for a in ffn_grads]
        args += terms
        in_specs += [pl.BlockSpec(memory_space=pl.ANY) for a in terms]
        scratch += [pltpu.VMEM(a.shape, BF) for a in terms]
        (_, D_), (_, U_), (rows_, _) = [a.shape[4:] for a in terms]
        blocks = dict(out=(16, D_), up0=(16, U_ // 2), up1=(16, U_ // 2), down0=(rows_ // 2, D_), down1=(rows_ // 2, D_))
        for k in range(HP):
            blocks["q%d" % k] = (16, W)
        plan = {name: Scatter.shapes(sizes, SCATTER_ORDERS[name], blocks[name]) for name in SCATTER_ORDERS}
        out_specs += [whole_block(blocks[name]) for name in SCATTER_ORDERS]
        out_shape += [jax.ShapeDtypeStruct(blocks[name], F32) for name in SCATTER_ORDERS]
        scratch += [
            pltpu.VMEM((HP,) + sizes + (16, W), BF), pltpu.VMEM((8 * HP, 128), F32), pltpu.VMEM(sizes + (8 * HP, 128), F32),
            pltpu.SemaphoreType.DMA,
        ]
        for name in SCATTER_ORDERS:
            scratch += [pltpu.VMEM(shape, BF) for shape in plan[name][0] + plan[name][1]]
        scratch += semaphores(sizes, [*SCATTER_ORDERS.values(), SPREAD])
        params = cp(collective_id=2, has_side_effects=True)
    else:
        out_specs += [whole_block((HP, D, W))]
        out_shape += [jax.ShapeDtypeStruct((HP, D, W), BF)]
        params = cp()
    return pl.pallas_call(
        functools.partial(last_kernel, sizes, plan), grid=(steps + R // B,), in_specs=in_specs, out_specs=out_specs,
        out_shape=out_shape, scratch_shapes=scratch, compiler_params=params,
    )(*args)


def finish_kernel(*refs):
    refs = list(refs)
    take = lambda count: [refs.pop(0) for _ in range(count)]
    tab_ref, ru0_ref, rd0_ref, ro_ref, ru1_ref, rd1_ref = take(6)
    pieces = take(4)
    first_ref, second_ref, wq_ref, wu_ref = take(4)
    tab_out, wq_out, wo_out, wu_out, wd_out, g1_out, g2_out = refs
    table = jnp.concatenate([tab_ref[8 * pair:8 * pair + 2, :] for pair in range(4)], axis=0)
    tab_out[...] = table[:, :16]
    wo_out[...] = ro_ref[...]
    for half, (ru_ref, rd_ref) in enumerate(((ru0_ref, rd0_ref), (ru1_ref, rd1_ref))):
        wu_out[:, half * ru_ref.shape[1]:(half + 1) * ru_ref.shape[1]] = ru_ref[...]
        wd_out[half * rd_ref.shape[0]:(half + 1) * rd_ref.shape[0], :] = rd_ref[...]
    for pair in range(4):
        for part in range(3):
            wq_out[:, (part * 4 + pair) * 128:(part * 4 + pair + 1) * 128] = pieces[pair][:, part * 128:(part + 1) * 128]
    square = lax.broadcasted_iota(jnp.int32, (16, 16), 0) == lax.broadcasted_iota(jnp.int32, (16, 16), 1)
    for first, w, grad, out in ((first_ref, wq_ref, wq_out, g1_out), (second_ref, wu_ref, wu_out, g2_out)):
        gain = first[...].reshape(1, 16).astype(F32)
        dots = jnp.sum(w[...].astype(F32) * grad[...], axis=1, keepdims=True)
        out[...] = jnp.sum(jnp.where(square, dots, 0.0), axis=0, keepdims=True) / gain


def finish(tab, results, first, second, wq, wu):
    out_shape = [
        jax.ShapeDtypeStruct((8, 16), F32), jax.ShapeDtypeStruct(wq.shape, F32), jax.ShapeDtypeStruct((wu.shape[0], wq.shape[1] // 3), F32),
        jax.ShapeDtypeStruct(wu.shape, F32), jax.ShapeDtypeStruct((2 * results[1].shape[0], wq.shape[1] // 3), F32), jax.ShapeDtypeStruct((1, 16), F32),
        jax.ShapeDtypeStruct((1, 16), F32),
    ]
    return pl.pallas_call(finish_kernel, out_shape=out_shape, compiler_params=cp())(tab, *results, first, second, wq, wu)


def on_device(devices, inputs, valid_len, norm_first, w_qkv, w_out, relative_bucket_table, norm_second, w_up, w_down, output_gradient):
    S, L, D = inputs.shape
    R = S * L
    HP = D // 128
    FFW = w_up.shape[1]
    fast = devices == 32 and D == 512 and S == 2
    table = relative_bucket_table
    x = inputs.reshape(R, D)
    og = output_gradient.reshape(R, D)
    by_pair = lambda w: w.reshape(D, 3, HP, 128).transpose(2, 0, 1, 3).reshape(HP, D, 384)
    if fast:
        sizes = device_grid(devices)
        mixed, qa, qkv, nt, bias_t, g1, g2, wq, wo, wu, wd = first_half(
            sizes, valid_len, table, x, S, [norm_first, norm_second, w_qkv, w_out, w_up, w_down]
        )
        wq, wo, wu, wd = wq.reshape(HP, D, 384), wo.reshape(D, D), wu.reshape(D, FFW), wd.reshape(FFW, D)
    else:
        sizes = None
        g1, wq, wo, g2, wu, wd = [
            lax.all_gather(a, "dp", axis=0, tiled=True) for a in (norm_first, w_qkv, w_out, norm_second, w_up, w_down)
        ]
        g1, g2 = g1.reshape(1, D).astype(F32), g2.reshape(1, D).astype(F32)
        wq = by_pair(wq)
        mixed, qa, qkv, nt, bias_t = first_half(None, valid_len, table, x, S, [g1, wq])
    out, ga, gm, gwo, gwu, gwd = ffn(x, mixed.reshape(R, D), og, g2, wo, wu, wd)
    got = last_half(
        sizes, valid_len, table, bias_t, qa, qkv, mixed, gm.reshape(S, L, D), nt, wq, g1, x, ga, [gwo, gwu, gwd]
    )
    gi, tab = got[:2]
    if fast:
        rt, rq, ro, ru, rd, r1, r2 = finish(tab, got[2:], norm_first, norm_second, w_qkv, w_up)
        r1, r2 = r1.reshape(-1), r2.reshape(-1)
    else:
        gwq = got[2].reshape(HP, D, 3, 128).transpose(1, 2, 0, 3).reshape(D, 3 * D)
        rq, ro, ru, rd = [
            lax.psum_scatter(a.astype(F32), "dp", scatter_dimension=0, tiled=True) for a in (gwq, gwo, gwu, gwd)
        ]
        r1 = jnp.sum(w_qkv.astype(F32) * rq, axis=1) / norm_first.astype(F32)
        r2 = jnp.sum(w_up.astype(F32) * ru, axis=1) / norm_second.astype(F32)
        rt = lax.psum(tab.reshape(HP, 8, 128)[:, :2, :16].reshape(table.shape), "dp")
    return (out.reshape(S, L, D), gi.reshape(S, L, D), r1, rq, ro, rt, r2, ru, rd)


def solution(mesh):
    placed = (
        P("dp", None, None), P("dp"), P("dp"), P("dp", None), P("dp", None), P(), P("dp"), P("dp", None), P("dp", None),
        P("dp", None, None),
    )
    return jax.shard_map(
        functools.partial(on_device, mesh.shape["dp"]),
        mesh=mesh,
        in_specs=placed,
        out_specs=(
            P("dp", None, None), P("dp", None, None), P("dp"), P("dp", None), P("dp", None), P(), P("dp"), P("dp", None),
            P("dp", None),
        ),
        check_vma=False,
    )
```

```python
import functools
import itertools

import jax
import jax.numpy as jnp
import numpy as np
from jax import lax
from jax.experimental import pallas as pl
from jax.experimental.pallas import tpu as pltpu
from jax.sharding import PartitionSpec as P

MESH = pl.DeviceIdType.MESH
F32 = jnp.float32
BF = jnp.bfloat16
EPS = 1e-05


def device_grid(devices):
    return (devices // 8, 2, 2, 2)


def grid_position(sizes):
    rest = lax.axis_index("dp")
    place = []
    for size in reversed(sizes):
        place.append(lax.rem(rest, size))
        rest = lax.div(rest, size)
    return tuple(reversed(place))


def flat(place, sizes):
    index = place[0]
    for one, size in zip(place[1:], sizes[1:]):
        index = index * size + one
    return index


def moves(sizes, group):
    return [m for m in itertools.product(*[range(sizes[a]) for a in group]) if any(m)]


def moved(place, sizes, group, move):
    other = list(place)
    for axis, step in zip(group, move):
        if step:
            other[axis] = lax.rem(place[axis] + step, sizes[axis])
    return tuple(other)


def greet(sizes, groups):
    place = grid_position(sizes)
    barrier = pltpu.get_barrier_semaphore()
    for group in groups:
        for move in moves(sizes, group):
            pl.semaphore_signal(
                barrier,
                inc=1,
                device_id=(flat(moved(place, sizes, group, move), sizes),),
                device_id_type=MESH,
            )


def await_greetings(sizes, groups):
    pl.semaphore_wait(pltpu.get_barrier_semaphore(), sum(len(moves(sizes, group)) for group in groups))


class Gather:
    def __init__(self, sizes, order, own, whole, local_sem, send_sems, recv_sems, first):
        self.sizes, self.order, self.first = sizes, order, first
        self.own, self.whole = own, whole
        self.local_sem, self.send_sems, self.recv_sems = local_sem, send_sems, recv_sems

    def joined(self, phase):
        return len(self.order[phase]) == 1

    def sem(self, phase, k):
        counts = [1 if self.joined(p) else len(moves(self.sizes, self.order[p])) for p in range(phase)]
        return self.first + sum(counts) + (0 if self.joined(phase) else k)

    def settle(self, phase):
        count = len(moves(self.sizes, self.order[phase]))
        if not self.joined(phase) or count == 1:
            for copy in self.copies(phase):
                copy.wait()
        else:
            every = self.bulk(phase, count)
            for sems in (self.send_sems, self.recv_sems):
                pltpu.make_async_copy(every, every, sems.at[self.sem(phase, 0)]).wait()

    def bulk(self, phase, count):
        place = grid_position(self.sizes)
        done = [a for group in self.order[:phase] for a in group]
        (axis,) = self.order[phase]
        return self.whole.at[
            tuple(slice(0, count) if a == axis else slice(None) if a in done else place[a] for a in range(4))
        ]

    def copies(self, phase):
        place = grid_position(self.sizes)
        done = [a for group in self.order[:phase] for a in group]
        group = self.order[phase]
        part = self.whole.at[tuple(slice(None) if a in done else place[a] for a in range(4))]
        return [
            pltpu.make_async_remote_copy(
                src_ref=self.own if phase == 0 else part,
                dst_ref=part,
                send_sem=self.send_sems.at[self.sem(phase, k)],
                recv_sem=self.recv_sems.at[self.sem(phase, k)],
                device_id=(flat(moved(place, self.sizes, group, move), self.sizes),),
                device_id_type=MESH,
            )
            for k, move in enumerate(moves(self.sizes, group))
        ]

    def local(self):
        return pltpu.make_async_copy(self.own, self.whole.at[grid_position(self.sizes)], self.local_sem)

    def start(self, phase):
        if phase == 0:
            self.local().start()
        for copy in self.copies(phase):
            copy.start()

    def finish(self, phase):
        if phase == 0:
            self.local().wait()
        self.settle(phase)


class Scatter:
    def __init__(self, sizes, order, terms, sums, landing, result, send_sems, recv_sems, first):
        self.sizes, self.order, self.first = sizes, order, first
        self.held = [terms] + list(sums)
        self.landing, self.result = landing, result
        self.send_sems, self.recv_sems = send_sems, recv_sems

    @staticmethod
    def shapes(sizes, order, block):
        left, sums, landing = set(range(4)), [], []
        for phase, group in enumerate(order):
            left -= set(group)
            lead = tuple(sizes[a] for a in sorted(left))
            slots = int(np.prod([sizes[a] for a in group]))
            landing.append((slots if slots > 2 else 1,) + lead + block)
            if phase < len(order) - 1:
                sums.append(lead + block)
        return sums, landing

    def before(self, phase):
        done = [a for group in self.order[:phase] for a in group]
        return [a for a in range(4) if a not in done]

    def slot(self, phase, place):
        group = self.order[phase]
        if self.landing[phase].shape[0] == 1:
            return 0
        return flat([place[a] for a in group], [self.sizes[a] for a in group])

    def joined(self, phase):
        return True

    def sem(self, phase, k):
        counts = [1 if self.joined(p) else len(moves(self.sizes, self.order[p])) for p in range(phase)]
        return self.first + sum(counts) + (0 if self.joined(phase) else k)

    def settle(self, phase):
        count = len(moves(self.sizes, self.order[phase]))
        if not self.joined(phase) or count == 1:
            for copy in self.copies(phase):
                copy.wait()
        else:
            every = self.bulk(phase, count)
            for sems in (self.send_sems, self.recv_sems):
                pltpu.make_async_copy(every, every, sems.at[self.sem(phase, 0)]).wait()

    def bulk(self, phase, count):
        return self.landing[phase].at[slice(0, count)]

    def copies(self, phase):
        place = grid_position(self.sizes)
        group = self.order[phase]
        out = []
        for k, move in enumerate(moves(self.sizes, group)):
            other = moved(place, self.sizes, group, move)
            part = tuple(other[a] if a in group else slice(None) for a in self.before(phase))
            out.append(
                pltpu.make_async_remote_copy(
                    src_ref=self.held[phase].at[part],
                    dst_ref=self.landing[phase].at[self.slot(phase, place)],
                    send_sem=self.send_sems.at[self.sem(phase, k)],
                    recv_sem=self.recv_sems.at[self.sem(phase, k)],
                    device_id=(flat(other, self.sizes),),
                    device_id_type=MESH,
                )
            )
        return out

    def start(self, phase):
        for copy in self.copies(phase):
            copy.start()

    def finish(self, phase):
        self.settle(phase)
        place = grid_position(self.sizes)
        group = self.order[phase]
        held, landed = self.held[phase], self.landing[phase]
        before = self.before(phase)
        left = [a for a in before if a not in group]
        last = phase == len(self.order) - 1
        target = self.result if last else self.held[phase + 1]

        def one(at):
            spot = dict(zip(left, at))
            mine = held[tuple(place[a] if a in group else spot[a] for a in before)]
            at = tuple(at)
            if landed.shape[0] == 1:
                total = mine.astype(F32) + landed[(0,) + at].astype(F32)
            else:
                landed[(self.slot(phase, place),) + at] = mine
                total = landed[(0,) + at].astype(F32)
                for source in range(1, landed.shape[0]):
                    total = total + landed[(source,) + at].astype(F32)
            if at:
                target[at] = total.astype(target.dtype)
            else:
                target[...] = total.astype(target.dtype)

        if not left:
            one(())
        else:
            lead = [self.sizes[a] for a in left]

            def body(count, unused):
                at = []
                for size in reversed(lead):
                    at.append(lax.rem(count, size))
                    count = lax.div(count, size)
                one(at[::-1])
                return unused

            lax.fori_loop(0, int(np.prod(lead)), body, 0)


def firsts(sizes, orders, joins_groups):
    counts = [
        sum(1 if joins_groups[k] or len(group) == 1 else len(moves(sizes, group)) for group in order)
        for k, order in enumerate(orders)
    ]
    return [sum(counts[:k]) for k in range(len(counts))], sum(counts)


def semaphores(sizes, orders, joins_groups):
    return [pltpu.SemaphoreType.DMA((firsts(sizes, orders, joins_groups)[1],))] * 2


def run_actions(actions, parts):
    for action, item, phase in actions:
        getattr(parts[item], action)(phase)


def run_schedule(tick, schedule, parts):
    for at, actions in sorted(schedule.items()):

        @pl.when(tick == at)
        def _(actions=actions):
            run_actions(actions, parts)


LOW=(0,1,2,3,4,5,6,7,8,12,16,32,64,128,256,512)
T=256
NEG=-1e30
def cp(**k): return pltpu.CompilerParams(vmem_limit_bytes=56*2**20, **k)
def dot_nt(a,b): return lax.dot_general(a,b,(((1,),(1,)),((),())),preferred_element_type=jnp.float32)
def dot_nn(a,b): return jnp.dot(a,b,preferred_element_type=jnp.float32)
def dot_tn(a,b): return lax.dot_general(a,b,(((0,),(0,)),((),())),preferred_element_type=jnp.float32)

def bias_of(dist, row):
    out=jnp.zeros(dist.shape,jnp.float32)+row[:,0:1]
    for b in range(1,16):
        out=jnp.where(dist>=LOW[b],row[:,b:b+1],out)
    return jnp.where(dist<0,NEG,out)

def table_row(table_ref,head):
    whole=table_ref[...].astype(jnp.float32)
    at=lax.broadcasted_iota(jnp.int32,whole.shape,0)
    return jnp.sum(jnp.where(at==head,whole,0.0),axis=0,keepdims=True)

H = 128
VARIED = (0, 1, 2, 4)


def build_bias(row, store):
    lane = lax.broadcasted_iota(jnp.int32, (1, 2 * H), 1)
    m = jnp.where(lane < H, lane, lane - 2 * H)
    for n, delta in enumerate(VARIED):
        for transposed in (False, True):
            w = bias_of(delta * H + (m if transposed else -m), row)
            tile = pltpu.roll(jnp.broadcast_to(w, (H, 2 * H)), 0, 1, stride=1, stride_axis=0)
            store(n, transposed, tile[:, :H])


def biased(tile, delta, bias, row):
    if delta < 0:
        return jnp.full((H, H), NEG, F32)
    if delta in VARIED:
        return tile + bias[VARIED.index(delta)]
    return tile + row[:, 14:15] if delta == 3 else tile + row[:, 15:16]

def split3(v):
    hi=v.astype(jnp.bfloat16); r=v-hi.astype(jnp.float32)
    mid=r.astype(jnp.bfloat16); lo=(r-mid.astype(jnp.float32)).astype(jnp.bfloat16)
    return hi,mid,lo

def halves(h, main, extra, rows):
    lane=lax.broadcasted_iota(jnp.int32,(rows,128),1)
    out=jnp.where((lane//64)==h,main,jnp.zeros((),main.dtype))
    base=64*(1-h)
    for n,e in enumerate(extra):
        if e is not None:
            out=jnp.where(lane==base+n,jnp.broadcast_to(e,(rows,128)).astype(jnp.bfloat16),out)
    return out

def ln_parts(v):
    c=v-jnp.mean(v,axis=1,keepdims=True)
    r=lax.rsqrt(jnp.mean(c*c,axis=1,keepdims=True)+EPS)
    return c*r, r
def ln_back(e_in,gain,xhat,r):
    e=e_in*gain
    gv=r*(e-jnp.mean(e,axis=1,keepdims=True)-xhat*jnp.mean(e*xhat,axis=1,keepdims=True))
    return (gv,)

def ffn_kernel(x_ref, m_ref, og_ref, g_ref, wo_ref, wu_ref, wd_ref, out_ref, ga_ref, gm_ref, gwo_ref, gwu_ref, gwd_ref,
               hid_s, gp_s, gb_s, nt_s, ogt_s, mt_s):
    i = pl.program_id(0)
    B = x_ref.shape[0]
    R = hid_s.shape[0]
    blocks = R // B
    C = hid_s.shape[1] // FFN_PARTS

    @pl.when(i < blocks)
    def _():
        at = pl.ds(pl.multiple_of(i * B, B), B)
        m = m_ref[...]
        og = og_ref[...]
        after = x_ref[...].astype(F32) + dot_nn(m, wo_ref[...])
        xhat, r = ln_parts(after)
        gain = g_ref[...]
        n = (xhat * gain).astype(BF)
        c = 0.7978845608028654
        for j in range(FFN_PARTS):
            cols = slice(j * C, (j + 1) * C)
            pre = dot_nn(n, wu_ref[:, cols])
            dh = dot_nt(og, wd_ref[cols, :])
            a = c + (c * 0.044715) * (pre * pre)
            half = 0.5 + 0.5 * jnp.tanh(pre * a)
            h = pre * half
            gp_s[at, cols] = (dh * (half + (h - h * half) * (6.0 * a - 4.0 * c))).astype(BF)
            hid_s[at, cols] = h.astype(BF)
        out_ref[...] = (after + dot_nn(hid_s[at, :], wd_ref[...])).astype(BF)
        dn = dot_nt(gp_s[at, :], wu_ref[...])
        (gv,) = ln_back(dn, gain, xhat, r)
        ga = og.astype(F32) + gv
        ga_ref[...] = ga
        gb = ga.astype(BF)
        gb_s[at, :] = gb
        gm_ref[...] = dot_nt(gb, wo_ref[...]).astype(BF)
        nt_s[:, at] = n.T
        ogt_s[:, at] = og.T
        mt_s[:, at] = m.T

    @pl.when(i >= blocks)
    def _():
        j = i - blocks
        cols = pl.ds(pl.multiple_of(j * C, C), C)
        gwd_ref[...] = dot_nn(ogt_s[...], hid_s[:, cols]).astype(BF).T
        gwu_ref[...] = dot_nn(nt_s[...], gp_s[:, cols]).astype(BF)
        share = mt_s.shape[0] // FFN_PARTS
        gwo_ref[...] = dot_nn(mt_s[pl.ds(pl.multiple_of(j * share, share), share), :], gb_s[...]).astype(BF)


FFN_PARTS = 4


def ffn(x, m, og, gain, wo, wu, wd, B=512):
    R, D = x.shape
    FF = wu.shape[1]
    n = R // B
    C = FF // FFN_PARTS
    row = pl.BlockSpec((B, D), lambda i: (jnp.minimum(i, n - 1), 0))
    late = lambda i: jnp.maximum(i - n, 0)
    return pl.pallas_call(
        ffn_kernel,
        grid=(n + FFN_PARTS,),
        in_specs=[row, row, row, whole_block((1, D)), whole_block((D, D)), whole_block((D, FF)), whole_block((FF, D))],
        out_specs=[
            row, row, row,
            pl.BlockSpec((D // FFN_PARTS, D), lambda i: (late(i), 0)),
            pl.BlockSpec((D, C), lambda i: (0, late(i))),
            pl.BlockSpec((C, D), lambda i: (late(i), 0)),
        ],
        out_shape=[
            jax.ShapeDtypeStruct((R, D), BF), jax.ShapeDtypeStruct((R, D), F32), jax.ShapeDtypeStruct((R, D), BF),
            jax.ShapeDtypeStruct((D, D), BF), jax.ShapeDtypeStruct((D, FF), BF), jax.ShapeDtypeStruct((FF, D), BF),
        ],
        scratch_shapes=[
            pltpu.VMEM((R, FF), BF), pltpu.VMEM((R, FF), BF), pltpu.VMEM((R, D), BF), pltpu.VMEM((D, R), BF),
            pltpu.VMEM((D, R), BF), pltpu.VMEM((D, R), BF),
        ],
        compiler_params=cp(),
    )(x, m, og, gain, wo, wu, wd)


SPREAD = ((0, 1, 2), (3,))
ZYX, ZXY, YZX, XZY, XYZ, YXZ = (
    ((a,), (b,), (c,), (3,)) for a, b, c in ((0, 1, 2), (0, 2, 1), (1, 0, 2), (2, 0, 1), (2, 1, 0), (1, 2, 0))
)
GATHER_ORDERS = {
    "q0": SPREAD,
    "gains": SPREAD,
    "q3": ZYX,
    "q1": XZY,
    "out": ZYX,
    "down0": XYZ,
    "up1": ZXY,
    "q2": ZXY,
    "up0": ZYX,
    "down1": ZXY,
}


def timetable(starts):
    table = {}
    for item, ticks in starts.items():
        for phase, tick in enumerate(ticks):
            if phase:
                table.setdefault(tick, []).append(("finish", item, phase - 1))
            if phase < len(ticks) - 1:
                table.setdefault(tick, []).append(("start", item, phase))
    return table


GATHER_SCHEDULE = timetable(
    {
        "q3": (0, 2, 6, 8, 10),
        "q1": (-1, 0, 3, 7, 7),
        "out": (1, 5, 8, 14, 17),
        "down0": (-1, 0, 2, 20, 23),
        "up1": (1, 7, 11, 18, 20),
        "q2": (0, 4, 7, 10, 13),
        "up0": (1, 8, 13, 20, 25),
        "down1": (1, 11, 15, 22, 25),
    }
)
LAST_TICK = 25


def own_lanes():
    row = lax.broadcasted_iota(jnp.int32, (16, 128), 0)
    lane = lax.broadcasted_iota(jnp.int32, (16, 128), 1)
    return lane == row + 16 * lax.rem(lax.axis_index("dp"), 8)


def placed_gains(first_ref, second_ref):
    row = lax.broadcasted_iota(jnp.int32, (16, 16), 0)
    both = jnp.where(row == 0, first_ref[...].reshape(1, 16).astype(F32), 0.0)
    both = jnp.where(row == 1, second_ref[...].reshape(1, 16).astype(F32), both)
    return dot_nn(both.astype(BF), jnp.where(own_lanes(), 1.0, 0.0).astype(BF)).astype(BF)


def first_kernel(sizes, *refs):
    remote = sizes is not None
    refs = list(refs)
    take = lambda count: [refs.pop(0) for _ in range(count)]
    vl_ref, table_ref, x_ref = take(3)
    if remote:
        first_ref, second_ref, wq_own, wo_own, wu_own, wd_own = take(6)
    else:
        g_ref, w_ref = take(2)
    mixed_ref, qa_ref, qkv_ref, nt_ref, bt_ref = take(5)
    if remote:
        g1_ref, g2_ref, wq_out, wo_ref, wu_ref, wd_ref = take(6)
    bias, bias_t, xhat, xhat_t, n_s, nt_s, held_sem = take(7)
    keep = [pltpu.make_async_copy(nt_s, nt_ref, held_sem.at[0]), pltpu.make_async_copy(bias_t, bt_ref, held_sem.at[1])]
    hp = pl.program_id(0)
    s = pl.program_id(1)
    pairs = pl.num_programs(0)
    S, L = qkv_ref.shape[1:3]
    step = hp * S + s
    R, D = x_ref.shape
    B = 512
    if remote:
        q_own, wq, gains_own, gains, local, send, recv, out_sem = take(8)
        names = list(GATHER_ORDERS)
        own = dict(gains=gains_own, out=wo_own)
        whole = dict(gains=gains, out=wo_ref)
        for half in range(2):
            cols = slice(half * wu_own.shape[1] // 2, (half + 1) * wu_own.shape[1] // 2)
            rows = slice(half * wd_own.shape[0] // 2, (half + 1) * wd_own.shape[0] // 2)
            own["up%d" % half], whole["up%d" % half] = wu_own.at[:, cols], wu_ref.at[:, :, :, :, :, cols]
            own["down%d" % half], whole["down%d" % half] = wd_own.at[rows], wd_ref.at[:, :, :, :, rows]
        for pair in range(4):
            own["q%d" % pair], whole["q%d" % pair] = q_own.at[pair], wq.at[pair]
        place = firsts(sizes, GATHER_ORDERS.values(), [False] * len(GATHER_ORDERS))[0]
        parts = {
            name: Gather(sizes, GATHER_ORDERS[name], own[name], whole[name], local.at[k], send, recv, place[k])
            for k, name in enumerate(names)
        }
        out_copy = lambda pair: pltpu.make_async_copy(wq.at[pair], wq_out.at[pair], out_sem.at[pair])

    def gather_tick(place):
        if remote:
            now = {t // 3: GATHER_SCHEDULE[t + 1] for t in range(place, LAST_TICK - 1, 3) if t + 1 in GATHER_SCHEDULE}
            run_schedule(step, now, parts)

    @pl.when(step == 0)
    def _():
        if remote:
            greet(sizes, SPREAD)
            gains_own[...] = placed_gains(first_ref, second_ref)
            for pair in range(4):
                for part in range(3):
                    q_own[pair, :, part * 128:(part + 1) * 128] = wq_own[:, (part * 4 + pair) * 128:(part * 4 + pair + 1) * 128]

        def all_biases(head, unused):
            def store(n, transposed, tile):
                (bias_t if transposed else bias)[head, n] = tile

            build_bias(table_row(table_ref, head), store)
            return unused

        lax.fori_loop(0, 2 * pairs, all_biases, 0)

        def norm(block, unused):
            at = pl.ds(pl.multiple_of(block * B, B), B)
            xh = ln_parts(x_ref[at, :].astype(F32))[0]
            xhat[at, :] = xh
            return unused

        lax.fori_loop(0, R // B, norm, 0)
        if remote:
            await_greetings(sizes, SPREAD)
            parts["q0"].start(0)
            parts["gains"].start(0)
            run_actions(GATHER_SCHEDULE[-1], parts)

        def turn(block, unused):
            at = pl.ds(pl.multiple_of(block * B, B), B)
            xhat_t[:, at] = xhat[at, :].T
            return unused

        lax.fori_loop(0, R // B, turn, 0)
        if remote:
            parts["gains"].finish(0)
            parts["q0"].finish(0)
            parts["gains"].start(1)
            parts["q0"].start(1)
            run_actions(GATHER_SCHEDULE[0], parts)
            parts["gains"].finish(1)
            tiles = []
            for z in range(sizes[0]):
                tile = jnp.zeros((16, 128), F32)
                for y, a, c in itertools.product(*[range(size) for size in sizes[1:]]):
                    tile = tile + gains[z, y, a, c].astype(F32)
                tiles.append(tile)
            tile = jnp.concatenate(tiles, axis=1)
            g1_ref[...] = tile[0:1, :]
            g2_ref[...] = tile[1:2, :]
            gain = tile[0:1, :]
        else:
            gain = g_ref[...]
        gain_t = jnp.broadcast_to(gain, (8, D)).T[:, 0:1]

        def scale(block, unused):
            at = pl.ds(pl.multiple_of(block * B, B), B)
            n_s[at, :] = (xhat[at, :] * gain).astype(BF)
            nt_s[:, at] = (xhat_t[:, at] * gain_t).astype(BF)
            return unused

        lax.fori_loop(0, R // B, scale, 0)
        for copy in keep:
            copy.start()
        if remote:
            parts["q0"].finish(1)

    gather_tick(0)

    @pl.when(s == 0)
    def _():
        weights = wq[hp].reshape(D, 384) if remote else w_ref[0]
        if remote:
            out_copy(hp).start()
        for seq in range(S):
            for half in range(L // B):
                row = seq * L + half * B
                qkv_ref[0, seq, half * B:(half + 1) * B, :] = dot_nn(n_s[row:row + B, :], weights).astype(BF)

    attend(vl_ref[s], qkv_ref.at[0, s], mixed_ref.at[0], qa_ref.at[0, 0], bias, table_ref, hp, gather_tick)

    @pl.when(step == pairs * S - 1)
    def _():
        for copy in keep:
            copy.wait()
        if remote:
            run_actions(GATHER_SCHEDULE.get(LAST_TICK, []), parts)
            for pair in range(4):
                out_copy(pair).wait()


def attend(valid, qkv_ref, mixed_ref, qa_ref, bias, table_ref, hp, between):
    L = qkv_ref.shape[0]
    nb = L // T
    key = lax.broadcasted_iota(jnp.int32, (L, 1), 0)
    mask = jnp.where(key < valid, 0.0, NEG)
    lane = lax.broadcasted_iota(jnp.int32, (T, 128), 1)
    ks = [halves(h, qkv_ref[:, 128:256], [1.0, 1.0, 1.0, mask], L) for h in range(2)]
    vs = [halves(h, qkv_ref[:, 256:384], [1.0], L) for h in range(2)]
    rows = [table_row(table_ref, 2 * hp + h) for h in range(2)]
    for qb in range(nb):
        if qb >= nb - 2:
            between(qb - nb + 3)
        kk = (qb + 1) * T
        qt = qkv_ref[qb * T:(qb + 1) * T, 0:128] * jnp.asarray(0.125, BF)
        outs = []
        for h in range(2):
            qh = halves(h, qt, [None, None, None, 1.0], T)
            sc = dot_nt(qh, ks[h][:kk])
            sc = jnp.concatenate(
                [
                    jnp.concatenate(
                        [
                            biased(sc[i * H:(i + 1) * H, j * H:(j + 1) * H], 2 * qb + i - j, bias.at[2 * hp + h], rows[h])
                            for j in range(kk // H)
                        ],
                        axis=1,
                    )
                    for i in range(2)
                ],
                axis=0,
            )
            mx = jnp.max(sc, axis=1, keepdims=True)
            p = jnp.exp(sc - mx)
            o = dot_nn(p.astype(BF), vs[h][:kk])
            l = o[:, 64 - 64 * h:65 - 64 * h]
            outs.append(o * (1.0 / l))
            hi, mid, lo = split3(-(mx + jnp.log(l)))
            qa_ref[h, qb * T:(qb + 1) * T, :] = halves(h, qt, [hi, mid, lo, 1.0], T)
        mixed_ref[qb * T:(qb + 1) * T, :] = jnp.where(lane < 64, outs[0], outs[1]).astype(BF)


def whole_block(shape):
    return pl.BlockSpec(shape, lambda *unused: (0,) * len(shape))


def first_half(sizes, vl, table, x, S, weights):
    R, D = x.shape
    L = R // S
    HP = D // 128
    remote = sizes is not None
    anyspace = pl.BlockSpec(memory_space=pl.ANY)
    in_specs = [pl.BlockSpec(memory_space=pltpu.SMEM), whole_block(table.shape), whole_block((R, D))]
    out_specs = [
        pl.BlockSpec((1, L, 128), lambda h, s: (s, 0, h)),
        pl.BlockSpec((1, 1, 2, L, 128), lambda h, s: (s, h, 0, 0, 0)),
        pl.BlockSpec((1, S, L, 384), lambda h, s: (h, 0, 0, 0)),
        anyspace,
        anyspace,
    ]
    out_shape = [
        jax.ShapeDtypeStruct((S, L, D), BF),
        jax.ShapeDtypeStruct((S, HP, 2, L, 128), BF),
        jax.ShapeDtypeStruct((HP, S, L, 384), BF),
        jax.ShapeDtypeStruct((D, R), BF),
        jax.ShapeDtypeStruct((2 * HP, len(VARIED), H, H), F32),
    ]
    scratch = [
        pltpu.VMEM((2 * HP, len(VARIED), H, H), F32), pltpu.VMEM((2 * HP, len(VARIED), H, H), F32), pltpu.VMEM((R, D), F32),
        pltpu.VMEM((D, R), F32), pltpu.VMEM((R, D), BF), pltpu.VMEM((D, R), BF), pltpu.SemaphoreType.DMA((2,)),
    ]
    if remote:
        first, second, wq, wo, wu, wd = weights
        in_specs += [whole_block(first.shape), whole_block(second.shape), whole_block(wq.shape), anyspace, anyspace, anyspace]
        out_specs += [whole_block((1, D)), whole_block((1, D))] + [anyspace] * 4
        out_shape += [jax.ShapeDtypeStruct((1, D), F32)] * 2
        out_shape += [jax.ShapeDtypeStruct((HP,) + sizes + (16, 384), BF)]
        out_shape += [jax.ShapeDtypeStruct(sizes + w.shape, BF) for w in (wo, wu, wd)]
        scratch += [
            pltpu.VMEM((HP, 16, 384), BF),
            pltpu.VMEM((HP,) + sizes + (16, 384), BF),
            pltpu.VMEM((16, 128), BF),
            pltpu.VMEM(sizes + (16, 128), BF),
            pltpu.SemaphoreType.DMA((len(GATHER_ORDERS),)),
        ] + semaphores(sizes, GATHER_ORDERS.values(), [False] * len(GATHER_ORDERS)) + [pltpu.SemaphoreType.DMA((HP,))]
        params = cp(collective_id=1, has_side_effects=True)
    else:
        gain, wq = weights
        in_specs += [whole_block((1, D)), pl.BlockSpec((1, D, 384), lambda h, s: (h, 0, 0))]
        params = cp()
    return pl.pallas_call(
        functools.partial(first_kernel, sizes), grid=(HP, S), in_specs=in_specs, out_specs=out_specs, out_shape=out_shape,
        scratch_shapes=scratch, compiler_params=params,
    )(vl, table, x, *weights)


CXYZ, CYXZ, CXZY, CYZX = (((3,), (a,), (b,), (c,)) for a, b, c in ((2, 1, 0), (1, 2, 0), (2, 0, 1), (1, 0, 2)))
DIRECT = ((3,), (0, 1, 2))
SCATTER_ORDERS = {
    "up0": CYXZ, "down0": CXYZ, "out": CYZX, "up1": CXZY, "down1": CYXZ, "q0": CYZX, "q1": CXZY, "q2": DIRECT, "q3": DIRECT,
}
SCATTER_SCHEDULE = timetable(
    {
        "q3": (8, 9, 12), "out": (1, 2, 3, 5, 6), "up0": (1, 2, 4, 5, 7), "up1": (1, 2, 4, 6, 7), "q1": (4, 5, 6, 7, 8),
        "q0": (2, 3, 5, 7, 8), "down0": (1, 3, 5, 6, 8), "down1": (1, 3, 6, 7, 9), "q2": (6, 7, 11), "table": (8, 9, 11),
    }
)


def last_kernel(sizes, plan, *refs):
    remote = sizes is not None
    refs = list(refs)
    take = lambda count: [refs.pop(0) for _ in range(count)]
    vl_ref, table_ref, bias, qa_ref, qkv_ref, o_ref, g_ref, nt_any, w_any, gain_ref, x_ref, ga_ref = take(12)
    if remote:
        terms_any = take(3)
    gi_ref, tab_ref = take(2)
    if remote:
        results = dict(zip(SCATTER_ORDERS, take(9)))
    else:
        (gw_ref,) = take(1)
    gacc, far, dqt, grads, nt_ref, w_ref, load_sem = take(7)
    loads = [(nt_any, nt_ref), (w_any, w_ref)]
    if remote:
        wo_terms, wu_terms, wd_terms = terms_vm = take(3)
        loads += list(zip(terms_any, terms_vm))
    loads = [pltpu.make_async_copy(a, b, load_sem.at[k]) for k, (a, b) in enumerate(loads)]
    t = pl.program_id(0)
    pairs = grads.shape[0]
    S = grads.shape[1] // qkv_ref.shape[2]
    steps = pairs * S
    hp = lax.div(t, S)
    s = lax.rem(t, S)
    L = qkv_ref.shape[2]
    R = S * L
    D = x_ref.shape[1]

    @pl.when(t == 0)
    def _():
        for load in loads:
            load.start()

    @pl.when(t == 1)
    def _():
        for load in loads:
            load.wait()

    if remote:
        wq_terms, tab_own, tab_all, local = take(4)
        terms = dict(out=wo_terms)
        for half in range(2):
            cols = slice(half * wu_terms.shape[5] // 2, (half + 1) * wu_terms.shape[5] // 2)
            rows = slice(half * wd_terms.shape[4] // 2, (half + 1) * wd_terms.shape[4] // 2)
            terms["up%d" % half] = wu_terms.at[:, :, :, :, :, cols]
            terms["down%d" % half] = wd_terms.at[:, :, :, :, rows]
        for pair in range(4):
            terms["q%d" % pair] = wq_terms.at[pair]
        send, recv = refs[-2:]
        place = firsts(sizes, [*SCATTER_ORDERS.values(), SPREAD], [True] * len(SCATTER_ORDERS) + [False])[0]
        parts = {}
        for k, name in enumerate(SCATTER_ORDERS):
            sums, landing = plan[name]
            parts[name] = Scatter(
                sizes, SCATTER_ORDERS[name], terms[name], take(len(sums)), take(len(landing)), results[name], send, recv, place[k]
            )
        parts["table"] = Gather(sizes, SPREAD, tab_own, tab_all, local, send, recv, place[-1])

        @pl.when(t == 0)
        def _():
            greet(sizes, SPREAD)

        @pl.when(t == 1)
        def _():
            await_greetings(sizes, SPREAD)

        run_schedule(t, {at: SCATTER_SCHEDULE[at] for at in SCATTER_SCHEDULE if at < 12}, parts)

    @pl.when(t < steps)
    def _():
        @pl.when(s == 0)
        def _():
            gacc[...] = jnp.zeros_like(gacc)
            far[...] = jnp.zeros_like(far)

        at = pl.multiple_of(s * L, L)
        attend_back(vl_ref[s], qa_ref.at[0, 0], qkv_ref.at[0, 0], o_ref[0], g_ref[0], grads, hp, at, bias, table_ref, gacc, far, dqt)

        @pl.when(s == S - 1)
        def _():
            rows = table_terms(gacc, far)
            place = pl.ds(pl.multiple_of(hp * 8, 8), 8)
            (tab_own if remote else tab_ref)[place, :] = rows
            gw = dot_nn(nt_ref[...], grads[hp]).astype(BF)
            if remote:
                wq_terms[hp] = gw.reshape(sizes + (16, 384))
            else:
                gw_ref[hp] = gw

    @pl.when(t >= steps)
    def _():
        B = x_ref.shape[0]
        at = pl.ds(pl.multiple_of((t - steps) * B, B), B)
        xhat, r = ln_parts(x_ref[...].astype(F32))
        dn = dot_nt(
            jnp.concatenate([grads[pair, at, :] for pair in range(pairs)], axis=1),
            jnp.concatenate([w_ref[pair] for pair in range(pairs)], axis=1),
        )
        gi_ref[...] = (ga_ref[...] + ln_back(dn, gain_ref[...], xhat, r)[0]).astype(BF)

    if remote:

        @pl.when(t == pl.num_programs(0) - 1)
        def _():
            run_actions(SCATTER_SCHEDULE[12], parts)
            total = None
            for at in itertools.product(*[range(size) for size in sizes]):
                block = tab_all[at]
                total = block if total is None else total + block
            tab_ref[...] = total


def table_terms(gacc, far):
    lane = lax.broadcasted_iota(jnp.int32, (1, 2 * H), 1)
    m = jnp.where(lane < H, lane, lane - 2 * H)
    bl = lax.broadcasted_iota(jnp.int32, (1, 128), 1)
    rows = []
    for h in range(2):
        row = jnp.zeros((1, 128), F32)
        for b in (14, 15):
            row = row + jnp.where(bl == b, jnp.sum(jnp.sum(far[h, b - 14], axis=0, keepdims=True), axis=1, keepdims=True), 0.0)
        for n, delta in enumerate(VARIED):
            w = jnp.concatenate([gacc[h, n], jnp.zeros((H, H), F32)], axis=1)
            acc = w[:8]
            for a in range(1, H // 8):
                acc = acc + pltpu.roll(w[8 * a:8 * a + 8], 2 * H - 8 * a, 1)
            diag = acc[0:1]
            for a in range(1, 8):
                diag = diag + pltpu.roll(acc[a:a + 1], 2 * H - a, 1)
            dist = delta * H + m
            for b in range(16):
                if LOW[b] >= (delta + 1) * H or (b < 15 and LOW[b + 1] <= (delta - 1) * H):
                    continue
                sel = dist >= LOW[b]
                if b < 15:
                    sel = sel & (dist < LOW[b + 1])
                row = row + jnp.where(bl == b, jnp.sum(jnp.where(sel, diag, 0.0), axis=1, keepdims=True), 0.0)
        rows.append(row)
    return jnp.concatenate(rows + [jnp.zeros((6, 128), F32)], axis=0)


def attend_back(valid, qa_ref, qkv_ref, o, g, grads, hp, first, bias, table_ref, gacc, far, dqt):
    L = qkv_ref.shape[0]
    rows = [table_row(table_ref, 2 * hp + h) for h in range(2)]
    nb = L // T
    key = lax.broadcasted_iota(jnp.int32, (L, 1), 0)
    mask = jnp.where(key < valid, 0.0, NEG)
    lane = lax.broadcasted_iota(jnp.int32, (T, 128), 1)
    prod = g.astype(F32) * o.astype(F32)
    lane_l = lax.broadcasted_iota(jnp.int32, (L, 128), 1)
    k = qkv_ref[:, 128:256]
    ks = [halves(h, k, [1.0, 1.0, 1.0, mask], L) for h in range(2)]
    vs = [halves(h, qkv_ref[:, 256:384], [1.0, 1.0, 1.0], L) for h in range(2)]
    gs = []
    for h in range(2):
        d = jnp.sum(jnp.where((lane_l // 64) == h, prod, 0.0), axis=1, keepdims=True)
        hi, mid, lo = split3(-d)
        gs.append(halves(h, g, [hi, mid, lo], L))
    kt = (k * jnp.asarray(0.125, BF)).T
    for kb in range(nb):
        dks, dvs = [], []
        for h in range(2):
            qh = qa_ref[h]
            st = dot_nt(ks[h][kb * T:(kb + 1) * T], qh[kb * T:])
            dp = dot_nt(vs[h][kb * T:(kb + 1) * T], gs[h][kb * T:])
            st = jnp.concatenate(
                [
                    jnp.concatenate(
                        [biased(st[j * H:(j + 1) * H, i * H:(i + 1) * H], i - j, bias.at[0, h], rows[h]) for i in range(2 * (nb - kb))],
                        axis=1,
                    )
                    for j in range(2)
                ],
                axis=0,
            )
            p = jnp.exp(st)
            ds = p * dp
            pb = p.astype(BF)
            dsb = ds.astype(BF)
            dvs.append(dot_nn(pb, gs[h][kb * T:]))
            dks.append(dot_nn(dsb, qh[kb * T:]))
            for delta in range(2 * (nb - kb)):
                both = [ds[j * H:(j + 1) * H, i * H:(i + 1) * H] for j in range(2) for i in range(2 * (nb - kb)) if i - j == delta]
                both = both[0] if len(both) == 1 else both[0] + both[1]
                if delta in VARIED:
                    gacc[h, VARIED.index(delta)] += both
                else:
                    far[h, 0 if delta == 3 else 1] += jnp.sum(both.reshape(H // 8, 8, H), axis=0)
            r = dot_nn(kt[h * 64:(h + 1) * 64, kb * T:(kb + 1) * T], dsb)
            if kb == 0:
                dqt[h * 64:(h + 1) * 64, :] = r
            else:
                dqt[h * 64:(h + 1) * 64, kb * T:] += r
        at = pl.ds(first + kb * T, T)
        grads[hp, at, 128:256] = jnp.where(lane < 64, dks[0], dks[1]).astype(BF)
        grads[hp, at, 256:384] = jnp.where(lane < 64, dvs[0], dvs[1]).astype(BF)
    grads[hp, pl.ds(first, L), 0:128] = dqt[...].T.astype(BF)


def last_half(sizes, vl, table, bias_t, qa, qkv, mixed, gm, nt, wq, gain, x, ga, ffn_grads):
    HP, S, L, W = qkv.shape
    R, D = x.shape
    B = 512
    steps = HP * S
    remote = sizes is not None
    pair = lambda t: jnp.minimum(t, steps - 1) // S
    seq = lambda t: jnp.minimum(t, steps - 1) % S
    late = pl.BlockSpec((B, D), lambda t: (jnp.maximum(t - steps, 0), 0))
    in_specs = [
        pl.BlockSpec(memory_space=pltpu.SMEM),
        whole_block(table.shape),
        pl.BlockSpec((1, 2, len(VARIED), H, H), lambda t: (pair(t), 0, 0, 0, 0)),
        pl.BlockSpec((1, 1, 2, L, 128), lambda t: (seq(t), pair(t), 0, 0, 0)),
        pl.BlockSpec((1, 1, L, W), lambda t: (pair(t), seq(t), 0, 0)),
        pl.BlockSpec((1, L, 128), lambda t: (seq(t), 0, pair(t))),
        pl.BlockSpec((1, L, 128), lambda t: (seq(t), 0, pair(t))),
        pl.BlockSpec(memory_space=pl.ANY),
        pl.BlockSpec(memory_space=pl.ANY),
        whole_block((1, D)),
        late,
        late,
    ]
    out_specs = [late, whole_block((8 * HP, 128))]
    out_shape = [jax.ShapeDtypeStruct((R, D), BF), jax.ShapeDtypeStruct((8 * HP, 128), F32)]
    scratch = [
        pltpu.VMEM((2, len(VARIED), H, H), F32), pltpu.VMEM((2, 2, 8, H), F32), pltpu.VMEM((128, L), F32),
        pltpu.VMEM((HP, R, W), BF), pltpu.VMEM((D, R), BF), pltpu.VMEM((HP, D, W), BF),
        pltpu.SemaphoreType.DMA((5 if remote else 2,)),
    ]
    args = [vl, table, bias_t.reshape(HP, 2, len(VARIED), H, H), qa, qkv, mixed, gm, nt, wq, gain, x, ga]
    plan = None
    if remote:
        count = int(np.prod(sizes))
        terms = [a.reshape(sizes + (a.shape[0] // count, a.shape[1])) for a in ffn_grads]
        args += terms
        in_specs += [pl.BlockSpec(memory_space=pl.ANY) for a in terms]
        scratch += [pltpu.VMEM(a.shape, BF) for a in terms]
        (_, D_), (_, U_), (rows_, _) = [a.shape[4:] for a in terms]
        blocks = dict(out=(16, D_), up0=(16, U_ // 2), up1=(16, U_ // 2), down0=(rows_ // 2, D_), down1=(rows_ // 2, D_))
        for k in range(HP):
            blocks["q%d" % k] = (16, W)
        plan = {name: Scatter.shapes(sizes, SCATTER_ORDERS[name], blocks[name]) for name in SCATTER_ORDERS}
        out_specs += [whole_block(blocks[name]) for name in SCATTER_ORDERS]
        out_shape += [jax.ShapeDtypeStruct(blocks[name], F32) for name in SCATTER_ORDERS]
        scratch += [
            pltpu.VMEM((HP,) + sizes + (16, W), BF), pltpu.VMEM((8 * HP, 128), F32), pltpu.VMEM(sizes + (8 * HP, 128), F32),
            pltpu.SemaphoreType.DMA,
        ]
        for name in SCATTER_ORDERS:
            scratch += [pltpu.VMEM(shape, BF) for shape in plan[name][0] + plan[name][1]]
        scratch += semaphores(sizes, [*SCATTER_ORDERS.values(), SPREAD], [True] * len(SCATTER_ORDERS) + [False])
        params = cp(collective_id=2, has_side_effects=True)
    else:
        out_specs += [whole_block((HP, D, W))]
        out_shape += [jax.ShapeDtypeStruct((HP, D, W), BF)]
        params = cp()
    return pl.pallas_call(
        functools.partial(last_kernel, sizes, plan), grid=(steps + R // B,), in_specs=in_specs, out_specs=out_specs,
        out_shape=out_shape, scratch_shapes=scratch, compiler_params=params,
    )(*args)


def finish_kernel(*refs):
    refs = list(refs)
    take = lambda count: [refs.pop(0) for _ in range(count)]
    tab_ref, ru0_ref, rd0_ref, ro_ref, ru1_ref, rd1_ref = take(6)
    pieces = take(4)
    first_ref, second_ref, wq_ref, wu_ref, gi_ref = take(5)
    tab_out, wq_out, wo_out, wu_out, wd_out, g1_out, g2_out, gi_out, held, sems = refs
    share = gi_ref.shape[0] // 4
    places = [pl.ds(k * share, share) for k in range(4)]
    moves_in = [pltpu.make_async_copy(gi_ref.at[at], held.at[at], sems.at[k]) for k, at in enumerate(places)]
    moves_out = [pltpu.make_async_copy(held.at[at], gi_out.at[at], sems.at[4 + k]) for k, at in enumerate(places)]
    for move in moves_in:
        move.start()
    for move_in, move_out in zip(moves_in, moves_out):
        move_in.wait()
        move_out.start()
    table = jnp.concatenate([tab_ref[8 * pair:8 * pair + 2, :] for pair in range(4)], axis=0)
    tab_out[...] = table[:, :16]
    wo_out[...] = ro_ref[...]
    for half, (ru_ref, rd_ref) in enumerate(((ru0_ref, rd0_ref), (ru1_ref, rd1_ref))):
        wu_out[:, half * ru_ref.shape[1]:(half + 1) * ru_ref.shape[1]] = ru_ref[...]
        wd_out[half * rd_ref.shape[0]:(half + 1) * rd_ref.shape[0], :] = rd_ref[...]
    for pair in range(4):
        for part in range(3):
            wq_out[:, (part * 4 + pair) * 128:(part * 4 + pair + 1) * 128] = pieces[pair][:, part * 128:(part + 1) * 128]
    square = lax.broadcasted_iota(jnp.int32, (16, 16), 0) == lax.broadcasted_iota(jnp.int32, (16, 16), 1)
    for first, w, grad, out in ((first_ref, wq_ref, wq_out, g1_out), (second_ref, wu_ref, wu_out, g2_out)):
        gain = first[...].reshape(1, 16).astype(F32)
        dots = jnp.sum(w[...].astype(F32) * grad[...], axis=1, keepdims=True)
        out[...] = jnp.sum(jnp.where(square, dots, 0.0), axis=0, keepdims=True) / gain
    for move in moves_out:
        move.wait()


def finish(tab, results, first, second, wq, wu, gi):
    out_shape = [
        jax.ShapeDtypeStruct((8, 16), F32), jax.ShapeDtypeStruct(wq.shape, F32), jax.ShapeDtypeStruct((wu.shape[0], wq.shape[1] // 3), F32),
        jax.ShapeDtypeStruct(wu.shape, F32), jax.ShapeDtypeStruct((2 * results[1].shape[0], wq.shape[1] // 3), F32), jax.ShapeDtypeStruct((1, 16), F32),
        jax.ShapeDtypeStruct((1, 16), F32),
    ]
    args = [tab, *results, first, second, wq, wu, gi]
    anyspace = pl.BlockSpec(memory_space=pl.ANY)
    return pl.pallas_call(
        finish_kernel,
        in_specs=[whole_block(a.shape) for a in args[:-1]] + [anyspace],
        out_specs=[whole_block(s.shape) for s in out_shape] + [anyspace],
        out_shape=out_shape + [jax.ShapeDtypeStruct(gi.shape, gi.dtype)],
        scratch_shapes=[pltpu.VMEM(gi.shape, gi.dtype), pltpu.SemaphoreType.DMA((8,))],
        compiler_params=cp(),
    )(*args)


def on_device(devices, inputs, valid_len, norm_first, w_qkv, w_out, relative_bucket_table, norm_second, w_up, w_down, output_gradient):
    S, L, D = inputs.shape
    R = S * L
    HP = D // 128
    FFW = w_up.shape[1]
    fast = devices == 32 and D == 512 and S == 2
    table = relative_bucket_table
    x = inputs.reshape(R, D)
    og = output_gradient.reshape(R, D)
    by_pair = lambda w: w.reshape(D, 3, HP, 128).transpose(2, 0, 1, 3).reshape(HP, D, 384)
    if fast:
        sizes = device_grid(devices)
        mixed, qa, qkv, nt, bias_t, g1, g2, wq, wo, wu, wd = first_half(
            sizes, valid_len, table, x, S, [norm_first, norm_second, w_qkv, w_out, w_up, w_down]
        )
        wq, wo, wu, wd = wq.reshape(HP, D, 384), wo.reshape(D, D), wu.reshape(D, FFW), wd.reshape(FFW, D)
    else:
        sizes = None
        g1, wq, wo, g2, wu, wd = [
            lax.all_gather(a, "dp", axis=0, tiled=True) for a in (norm_first, w_qkv, w_out, norm_second, w_up, w_down)
        ]
        g1, g2 = g1.reshape(1, D).astype(F32), g2.reshape(1, D).astype(F32)
        wq = by_pair(wq)
        mixed, qa, qkv, nt, bias_t = first_half(None, valid_len, table, x, S, [g1, wq])
    out, ga, gm, gwo, gwu, gwd = ffn(x, mixed.reshape(R, D), og, g2, wo, wu, wd)
    got = last_half(
        sizes, valid_len, table, bias_t, qa, qkv, mixed, gm.reshape(S, L, D), nt, wq, g1, x, ga, [gwo, gwu, gwd]
    )
    gi, tab = got[:2]
    if fast:
        rt, rq, ro, ru, rd, r1, r2, gi = finish(tab, got[2:], norm_first, norm_second, w_qkv, w_up, gi)
        r1, r2 = r1.reshape(-1), r2.reshape(-1)
    else:
        gwq = got[2].reshape(HP, D, 3, 128).transpose(1, 2, 0, 3).reshape(D, 3 * D)
        rq, ro, ru, rd = [
            lax.psum_scatter(a.astype(F32), "dp", scatter_dimension=0, tiled=True) for a in (gwq, gwo, gwu, gwd)
        ]
        r1 = jnp.sum(w_qkv.astype(F32) * rq, axis=1) / norm_first.astype(F32)
        r2 = jnp.sum(w_up.astype(F32) * ru, axis=1) / norm_second.astype(F32)
        rt = lax.psum(tab.reshape(HP, 8, 128)[:, :2, :16].reshape(table.shape), "dp")
    return (out.reshape(S, L, D), gi.reshape(S, L, D), r1, rq, ro, rt, r2, ru, rd)


def solution(mesh):
    placed = (
        P("dp", None, None), P("dp"), P("dp"), P("dp", None), P("dp", None), P(), P("dp"), P("dp", None), P("dp", None),
        P("dp", None, None),
    )
    return jax.shard_map(
        functools.partial(on_device, mesh.shape["dp"]),
        mesh=mesh,
        in_specs=placed,
        out_specs=(
            P("dp", None, None), P("dp", None, None), P("dp"), P("dp", None), P("dp", None), P(), P("dp"), P("dp", None),
            P("dp", None),
        ),
        check_vma=False,
    )
```

```python
import functools
import itertools

import jax
import jax.numpy as jnp
import numpy as np
from jax import lax
from jax.experimental import pallas as pl
from jax.experimental.pallas import tpu as pltpu
from jax.sharding import PartitionSpec as P

MESH = pl.DeviceIdType.MESH
F32 = jnp.float32
BF = jnp.bfloat16
EPS = 1e-05


def device_grid(devices):
    return (devices // 8, 2, 2, 2)


def grid_position(sizes):
    rest = lax.axis_index("dp")
    place = []
    for size in reversed(sizes):
        place.append(lax.rem(rest, size))
        rest = lax.div(rest, size)
    return tuple(reversed(place))


def flat(place, sizes):
    index = place[0]
    for one, size in zip(place[1:], sizes[1:]):
        index = index * size + one
    return index


def moves(sizes, group):
    return [m for m in itertools.product(*[range(sizes[a]) for a in group]) if any(m)]


def moved(place, sizes, group, move):
    other = list(place)
    for axis, step in zip(group, move):
        if step:
            other[axis] = lax.rem(place[axis] + step, sizes[axis])
    return tuple(other)


def greet(sizes, groups):
    place = grid_position(sizes)
    barrier = pltpu.get_barrier_semaphore()
    for group in groups:
        for move in moves(sizes, group):
            pl.semaphore_signal(
                barrier,
                inc=1,
                device_id=(flat(moved(place, sizes, group, move), sizes),),
                device_id_type=MESH,
            )


def await_greetings(sizes, groups):
    pl.semaphore_wait(pltpu.get_barrier_semaphore(), sum(len(moves(sizes, group)) for group in groups))


class Gather:
    def __init__(self, sizes, order, own, whole, local_sem, send_sems, recv_sems, first):
        self.sizes, self.order, self.first = sizes, order, first
        self.own, self.whole = own, whole
        self.local_sem, self.send_sems, self.recv_sems = local_sem, send_sems, recv_sems

    def joined(self, phase):
        return len(self.order[phase]) == 1

    def sem(self, phase, k):
        counts = [1 if self.joined(p) else len(moves(self.sizes, self.order[p])) for p in range(phase)]
        return self.first + sum(counts) + (0 if self.joined(phase) else k)

    def settle(self, phase):
        count = len(moves(self.sizes, self.order[phase]))
        if not self.joined(phase) or count == 1:
            for copy in self.copies(phase):
                copy.wait()
        else:
            every = self.bulk(phase, count)
            for sems in (self.send_sems, self.recv_sems):
                pltpu.make_async_copy(every, every, sems.at[self.sem(phase, 0)]).wait()

    def bulk(self, phase, count):
        place = grid_position(self.sizes)
        done = [a for group in self.order[:phase] for a in group]
        (axis,) = self.order[phase]
        return self.whole.at[
            tuple(slice(0, count) if a == axis else slice(None) if a in done else place[a] for a in range(4))
        ]

    def copies(self, phase):
        place = grid_position(self.sizes)
        done = [a for group in self.order[:phase] for a in group]
        group = self.order[phase]
        part = self.whole.at[tuple(slice(None) if a in done else place[a] for a in range(4))]
        return [
            pltpu.make_async_remote_copy(
                src_ref=self.own if phase == 0 else part,
                dst_ref=part,
                send_sem=self.send_sems.at[self.sem(phase, k)],
                recv_sem=self.recv_sems.at[self.sem(phase, k)],
                device_id=(flat(moved(place, self.sizes, group, move), self.sizes),),
                device_id_type=MESH,
            )
            for k, move in enumerate(moves(self.sizes, group))
        ]

    def local(self):
        return pltpu.make_async_copy(self.own, self.whole.at[grid_position(self.sizes)], self.local_sem)

    def start(self, phase):
        if phase == 0:
            self.local().start()
        for copy in self.copies(phase):
            copy.start()

    def finish(self, phase):
        if phase == 0:
            self.local().wait()
        self.settle(phase)


class Scatter:
    def __init__(self, sizes, order, terms, sums, landing, result, send_sems, recv_sems, first):
        self.sizes, self.order, self.first = sizes, order, first
        self.held = [terms] + list(sums)
        self.landing, self.result = landing, result
        self.send_sems, self.recv_sems = send_sems, recv_sems

    @staticmethod
    def shapes(sizes, order, block):
        left, sums, landing = set(range(4)), [], []
        for phase, group in enumerate(order):
            left -= set(group)
            lead = tuple(sizes[a] for a in sorted(left))
            slots = int(np.prod([sizes[a] for a in group]))
            landing.append((slots if slots > 2 else 1,) + lead + block)
            if phase < len(order) - 1:
                sums.append(lead + block)
        return sums, landing

    def before(self, phase):
        done = [a for group in self.order[:phase] for a in group]
        return [a for a in range(4) if a not in done]

    def slot(self, phase, place):
        group = self.order[phase]
        if self.landing[phase].shape[0] == 1:
            return 0
        return flat([place[a] for a in group], [self.sizes[a] for a in group])

    def joined(self, phase):
        return True

    def sem(self, phase, k):
        counts = [1 if self.joined(p) else len(moves(self.sizes, self.order[p])) for p in range(phase)]
        return self.first + sum(counts) + (0 if self.joined(phase) else k)

    def settle(self, phase):
        count = len(moves(self.sizes, self.order[phase]))
        if not self.joined(phase) or count == 1:
            for copy in self.copies(phase):
                copy.wait()
        else:
            every = self.bulk(phase, count)
            for sems in (self.send_sems, self.recv_sems):
                pltpu.make_async_copy(every, every, sems.at[self.sem(phase, 0)]).wait()

    def bulk(self, phase, count):
        return self.landing[phase].at[slice(0, count)]

    def copies(self, phase):
        place = grid_position(self.sizes)
        group = self.order[phase]
        out = []
        for k, move in enumerate(moves(self.sizes, group)):
            other = moved(place, self.sizes, group, move)
            part = tuple(other[a] if a in group else slice(None) for a in self.before(phase))
            out.append(
                pltpu.make_async_remote_copy(
                    src_ref=self.held[phase].at[part],
                    dst_ref=self.landing[phase].at[self.slot(phase, place)],
                    send_sem=self.send_sems.at[self.sem(phase, k)],
                    recv_sem=self.recv_sems.at[self.sem(phase, k)],
                    device_id=(flat(other, self.sizes),),
                    device_id_type=MESH,
                )
            )
        return out

    def start(self, phase):
        for copy in self.copies(phase):
            copy.start()

    def finish(self, phase):
        self.settle(phase)
        place = grid_position(self.sizes)
        group = self.order[phase]
        held, landed = self.held[phase], self.landing[phase]
        before = self.before(phase)
        left = [a for a in before if a not in group]
        last = phase == len(self.order) - 1
        target = self.result if last else self.held[phase + 1]

        def one(at):
            spot = dict(zip(left, at))
            mine = held[tuple(place[a] if a in group else spot[a] for a in before)]
            at = tuple(at)
            if landed.shape[0] == 1:
                total = mine.astype(F32) + landed[(0,) + at].astype(F32)
            else:
                landed[(self.slot(phase, place),) + at] = mine
                total = landed[(0,) + at].astype(F32)
                for source in range(1, landed.shape[0]):
                    total = total + landed[(source,) + at].astype(F32)
            if at:
                target[at] = total.astype(target.dtype)
            else:
                target[...] = total.astype(target.dtype)

        if not left:
            one(())
        else:
            lead = [self.sizes[a] for a in left]

            def body(count, unused):
                at = []
                for size in reversed(lead):
                    at.append(lax.rem(count, size))
                    count = lax.div(count, size)
                one(at[::-1])
                return unused

            lax.fori_loop(0, int(np.prod(lead)), body, 0)


def firsts(sizes, orders, joins_groups):
    counts = [
        sum(1 if joins_groups[k] or len(group) == 1 else len(moves(sizes, group)) for group in order)
        for k, order in enumerate(orders)
    ]
    return [sum(counts[:k]) for k in range(len(counts))], sum(counts)


def semaphores(sizes, orders, joins_groups):
    return [pltpu.SemaphoreType.DMA((firsts(sizes, orders, joins_groups)[1],))] * 2


def run_actions(actions, parts):
    for action, item, phase in actions:
        getattr(parts[item], action)(phase)


def run_schedule(tick, schedule, parts):
    for at, actions in sorted(schedule.items()):

        @pl.when(tick == at)
        def _(actions=actions):
            run_actions(actions, parts)


LOW=(0,1,2,3,4,5,6,7,8,12,16,32,64,128,256,512)
T=256
NEG=-1e30
def cp(**k): return pltpu.CompilerParams(vmem_limit_bytes=56*2**20, **k)
def dot_nt(a,b): return lax.dot_general(a,b,(((1,),(1,)),((),())),preferred_element_type=jnp.float32)
def dot_nn(a,b): return jnp.dot(a,b,preferred_element_type=jnp.float32)
def dot_tn(a,b): return lax.dot_general(a,b,(((0,),(0,)),((),())),preferred_element_type=jnp.float32)

def bias_of(dist, row):
    out=jnp.zeros(dist.shape,jnp.float32)+row[:,0:1]
    for b in range(1,16):
        out=jnp.where(dist>=LOW[b],row[:,b:b+1],out)
    return jnp.where(dist<0,NEG,out)

def table_row(table_ref,head):
    whole=table_ref[...].astype(jnp.float32)
    at=lax.broadcasted_iota(jnp.int32,whole.shape,0)
    return jnp.sum(jnp.where(at==head,whole,0.0),axis=0,keepdims=True)

H = 128
VARIED = (0, 1, 2, 4)


def build_bias(row, store):
    lane = lax.broadcasted_iota(jnp.int32, (1, 2 * H), 1)
    m = jnp.where(lane < H, lane, lane - 2 * H)
    for n, delta in enumerate(VARIED):
        for transposed in (False, True):
            w = bias_of(delta * H + (m if transposed else -m), row)
            tile = pltpu.roll(jnp.broadcast_to(w, (H, 2 * H)), 0, 1, stride=1, stride_axis=0)
            store(n, transposed, tile[:, :H])


def biased(tile, delta, bias, row):
    if delta < 0:
        return jnp.full((H, H), NEG, F32)
    if delta in VARIED:
        return tile + bias[VARIED.index(delta)]
    return tile + row[:, 14:15] if delta == 3 else tile + row[:, 15:16]

def split3(v):
    hi=v.astype(jnp.bfloat16); r=v-hi.astype(jnp.float32)
    mid=r.astype(jnp.bfloat16); lo=(r-mid.astype(jnp.float32)).astype(jnp.bfloat16)
    return hi,mid,lo

def halves(h, main, extra, rows):
    lane=lax.broadcasted_iota(jnp.int32,(rows,128),1)
    out=jnp.where((lane//64)==h,main,jnp.zeros((),main.dtype))
    base=64*(1-h)
    for n,e in enumerate(extra):
        if e is not None:
            out=jnp.where(lane==base+n,jnp.broadcast_to(e,(rows,128)).astype(jnp.bfloat16),out)
    return out

def ln_parts(v):
    c=v-jnp.mean(v,axis=1,keepdims=True)
    r=lax.rsqrt(jnp.mean(c*c,axis=1,keepdims=True)+EPS)
    return c*r, r
def ln_back(e_in,gain,xhat,r):
    e=e_in*gain
    gv=r*(e-jnp.mean(e,axis=1,keepdims=True)-xhat*jnp.mean(e*xhat,axis=1,keepdims=True))
    return (gv,)

def ffn_kernel(x_ref, m_ref, og_ref, g_ref, wo_ref, wu_ref, wd_ref, out_ref, ga_ref, gm_ref, gwo_ref, gwu_ref, gwd_ref,
               hid_s, gp_s, gb_s, nt_s, ogt_s, mt_s):
    i = pl.program_id(0)
    B = x_ref.shape[0]
    R = hid_s.shape[0]
    blocks = R // B
    C = hid_s.shape[1] // FFN_PARTS

    @pl.when(i < blocks)
    def _():
        at = pl.ds(pl.multiple_of(i * B, B), B)
        m = m_ref[...]
        og = og_ref[...]
        after = x_ref[...].astype(F32) + dot_nn(m, wo_ref[...])
        xhat, r = ln_parts(after)
        gain = g_ref[...]
        n = (xhat * gain).astype(BF)
        c = 0.7978845608028654
        for j in range(FFN_PARTS):
            cols = slice(j * C, (j + 1) * C)
            pre = dot_nn(n, wu_ref[:, cols])
            dh = dot_nt(og, wd_ref[cols, :])
            a = c + (c * 0.044715) * (pre * pre)
            half = 0.5 + 0.5 * jnp.tanh(pre * a)
            h = pre * half
            gp_s[at, cols] = (dh * (half + (h - h * half) * (6.0 * a - 4.0 * c))).astype(BF)
            hid_s[at, cols] = h.astype(BF)
        out_ref[...] = (after + dot_nn(hid_s[at, :], wd_ref[...])).astype(BF)
        dn = dot_nt(gp_s[at, :], wu_ref[...])
        (gv,) = ln_back(dn, gain, xhat, r)
        ga = og.astype(F32) + gv
        ga_ref[...] = ga
        gb = ga.astype(BF)
        gb_s[at, :] = gb
        gm_ref[...] = dot_nt(gb, wo_ref[...]).astype(BF)
        nt_s[:, at] = n.T
        ogt_s[:, at] = og.T
        mt_s[:, at] = m.T

    @pl.when(i >= blocks)
    def _():
        j = i - blocks
        cols = pl.ds(pl.multiple_of(j * C, C), C)
        gwd_ref[...] = dot_nn(ogt_s[...], hid_s[:, cols]).astype(BF).T
        gwu_ref[...] = dot_nn(nt_s[...], gp_s[:, cols]).astype(BF)
        share = mt_s.shape[0] // FFN_PARTS
        gwo_ref[...] = dot_nn(mt_s[pl.ds(pl.multiple_of(j * share, share), share), :], gb_s[...]).astype(BF)


FFN_PARTS = 4


def ffn(x, m, og, gain, wo, wu, wd, B=512):
    R, D = x.shape
    FF = wu.shape[1]
    n = R // B
    C = FF // FFN_PARTS
    row = pl.BlockSpec((B, D), lambda i: (jnp.minimum(i, n - 1), 0))
    late = lambda i: jnp.maximum(i - n, 0)
    return pl.pallas_call(
        ffn_kernel,
        grid=(n + FFN_PARTS,),
        in_specs=[row, row, row, whole_block((1, D)), whole_block((D, D)), whole_block((D, FF)), whole_block((FF, D))],
        out_specs=[
            row, row, row,
            pl.BlockSpec((D // FFN_PARTS, D), lambda i: (late(i), 0)),
            pl.BlockSpec((D, C), lambda i: (0, late(i))),
            pl.BlockSpec((C, D), lambda i: (late(i), 0)),
        ],
        out_shape=[
            jax.ShapeDtypeStruct((R, D), BF), jax.ShapeDtypeStruct((R, D), F32), jax.ShapeDtypeStruct((R, D), BF),
            jax.ShapeDtypeStruct((D, D), BF), jax.ShapeDtypeStruct((D, FF), BF), jax.ShapeDtypeStruct((FF, D), BF),
        ],
        scratch_shapes=[
            pltpu.VMEM((R, FF), BF), pltpu.VMEM((R, FF), BF), pltpu.VMEM((R, D), BF), pltpu.VMEM((D, R), BF),
            pltpu.VMEM((D, R), BF), pltpu.VMEM((D, R), BF),
        ],
        compiler_params=cp(),
    )(x, m, og, gain, wo, wu, wd)


SPREAD = ((0, 1, 2), (3,))
ZYX, ZXY, YZX, XZY, XYZ, YXZ = (
    ((a,), (b,), (c,), (3,)) for a, b, c in ((0, 1, 2), (0, 2, 1), (1, 0, 2), (2, 0, 1), (2, 1, 0), (1, 2, 0))
)
GATHER_ORDERS = {
    "q0": SPREAD,
    "gains": SPREAD,
    "q3": ZYX,
    "q1": XZY,
    "out": ZYX,
    "down0": XYZ,
    "up1": ZXY,
    "q2": ZXY,
    "up0": ZYX,
    "down1": ZXY,
}


def timetable(starts):
    table = {}
    for item, ticks in starts.items():
        for phase, tick in enumerate(ticks):
            if phase:
                table.setdefault(tick, []).append(("finish", item, phase - 1))
            if phase < len(ticks) - 1:
                table.setdefault(tick, []).append(("start", item, phase))
    return table


GATHER_SCHEDULE = timetable(
    {
        "q3": (0, 2, 6, 8, 10),
        "q1": (-1, 0, 3, 7, 7),
        "out": (1, 5, 8, 14, 17),
        "down0": (-1, 0, 2, 20, 23),
        "up1": (1, 7, 11, 18, 20),
        "q2": (0, 4, 7, 10, 13),
        "up0": (1, 8, 13, 20, 25),
        "down1": (1, 11, 15, 22, 25),
    }
)
LAST_TICK = 25


def own_lanes():
    row = lax.broadcasted_iota(jnp.int32, (16, 128), 0)
    lane = lax.broadcasted_iota(jnp.int32, (16, 128), 1)
    return lane == row + 16 * lax.rem(lax.axis_index("dp"), 8)


def placed_gains(first_ref, second_ref):
    row = lax.broadcasted_iota(jnp.int32, (16, 16), 0)
    both = jnp.where(row == 0, first_ref[...].reshape(1, 16).astype(F32), 0.0)
    both = jnp.where(row == 1, second_ref[...].reshape(1, 16).astype(F32), both)
    return dot_nn(both.astype(BF), jnp.where(own_lanes(), 1.0, 0.0).astype(BF)).astype(BF)


def first_kernel(sizes, *refs):
    remote = sizes is not None
    refs = list(refs)
    take = lambda count: [refs.pop(0) for _ in range(count)]
    vl_ref, table_ref, x_ref = take(3)
    if remote:
        first_ref, second_ref, wq_own, wo_own, wu_own, wd_own = take(6)
    else:
        g_ref, w_ref = take(2)
    mixed_ref, qa_ref, qkv_ref, nt_ref, bt_ref = take(5)
    if remote:
        g1_ref, g2_ref, wq_out, wo_ref, wu_ref, wd_ref = take(6)
    bias, bias_t, xhat, xhat_t, n_s, nt_s, held_sem = take(7)
    keep = [pltpu.make_async_copy(nt_s, nt_ref, held_sem.at[0]), pltpu.make_async_copy(bias_t, bt_ref, held_sem.at[1])]
    hp = pl.program_id(0)
    s = pl.program_id(1)
    pairs = pl.num_programs(0)
    S, L = qkv_ref.shape[1:3]
    step = hp * S + s
    R, D = x_ref.shape
    B = 512
    if remote:
        q_own, wq, gains_own, gains, local, send, recv, out_sem = take(8)
        names = list(GATHER_ORDERS)
        own = dict(gains=gains_own, out=wo_own)
        whole = dict(gains=gains, out=wo_ref)
        for half in range(2):
            cols = slice(half * wu_own.shape[1] // 2, (half + 1) * wu_own.shape[1] // 2)
            rows = slice(half * wd_own.shape[0] // 2, (half + 1) * wd_own.shape[0] // 2)
            own["up%d" % half], whole["up%d" % half] = wu_own.at[:, cols], wu_ref.at[:, :, :, :, :, cols]
            own["down%d" % half], whole["down%d" % half] = wd_own.at[rows], wd_ref.at[:, :, :, :, rows]
        for pair in range(4):
            own["q%d" % pair], whole["q%d" % pair] = q_own.at[pair], wq.at[pair]
        place = firsts(sizes, GATHER_ORDERS.values(), [False] * len(GATHER_ORDERS))[0]
        parts = {
            name: Gather(sizes, GATHER_ORDERS[name], own[name], whole[name], local.at[k], send, recv, place[k])
            for k, name in enumerate(names)
        }
        out_copy = lambda pair: pltpu.make_async_copy(wq.at[pair], wq_out.at[pair], out_sem.at[pair])

    def gather_tick(place):
        if remote:
            now = {t // 3: GATHER_SCHEDULE[t + 1] for t in range(place, LAST_TICK - 1, 3) if t + 1 in GATHER_SCHEDULE}
            run_schedule(step, now, parts)

    @pl.when(step == 0)
    def _():
        if remote:
            greet(sizes, SPREAD)
            gains_own[...] = placed_gains(first_ref, second_ref)
            for pair in range(4):
                for part in range(3):
                    q_own[pair, :, part * 128:(part + 1) * 128] = wq_own[:, (part * 4 + pair) * 128:(part * 4 + pair + 1) * 128]

        def all_biases(head, unused):
            def store(n, transposed, tile):
                (bias_t if transposed else bias)[head, n] = tile

            build_bias(table_row(table_ref, head), store)
            return unused

        lax.fori_loop(0, 2 * pairs, all_biases, 0)

        def norm(block, unused):
            at = pl.ds(pl.multiple_of(block * B, B), B)
            xh = ln_parts(x_ref[at, :].astype(F32))[0]
            xhat[at, :] = xh
            return unused

        lax.fori_loop(0, R // B, norm, 0)
        if remote:
            await_greetings(sizes, SPREAD)
            parts["gains"].start(0)
            parts["q0"].start(0)
            run_actions(GATHER_SCHEDULE[-1], parts)

        def turn(block, unused):
            at = pl.ds(pl.multiple_of(block * B, B), B)
            xhat_t[:, at] = xhat[at, :].T
            return unused

        lax.fori_loop(0, R // B, turn, 0)
        if remote:
            parts["gains"].finish(0)
            parts["gains"].start(1)
            parts["q0"].finish(0)
            parts["q0"].start(1)
            run_actions(GATHER_SCHEDULE[0], parts)
            parts["gains"].finish(1)
            tiles = []
            for z in range(sizes[0]):
                tile = jnp.zeros((16, 128), F32)
                for y, a, c in itertools.product(*[range(size) for size in sizes[1:]]):
                    tile = tile + gains[z, y, a, c].astype(F32)
                tiles.append(tile)
            tile = jnp.concatenate(tiles, axis=1)
            g1_ref[...] = tile[0:1, :]
            g2_ref[...] = tile[1:2, :]
            gain = tile[0:1, :]
        else:
            gain = g_ref[...]
        gain_t = jnp.broadcast_to(gain, (8, D)).T[:, 0:1]

        def scale(block, unused):
            at = pl.ds(pl.multiple_of(block * B, B), B)
            n_s[at, :] = (xhat[at, :] * gain).astype(BF)
            nt_s[:, at] = (xhat_t[:, at] * gain_t).astype(BF)
            return unused

        lax.fori_loop(0, R // B, scale, 0)
        for copy in keep:
            copy.start()
        if remote:
            parts["q0"].finish(1)

    gather_tick(0)

    @pl.when(s == 0)
    def _():
        weights = wq[hp].reshape(D, 384) if remote else w_ref[0]
        if remote:
            out_copy(hp).start()
        for seq in range(S):
            for half in range(L // B):
                row = seq * L + half * B
                qkv_ref[0, seq, half * B:(half + 1) * B, :] = dot_nn(n_s[row:row + B, :], weights).astype(BF)

    attend(vl_ref[s], qkv_ref.at[0, s], mixed_ref.at[0], qa_ref.at[0, 0], bias, table_ref, hp, gather_tick)

    @pl.when(step == pairs * S - 1)
    def _():
        for copy in keep:
            copy.wait()
        if remote:
            run_actions(GATHER_SCHEDULE.get(LAST_TICK, []), parts)
            for pair in range(4):
                out_copy(pair).wait()


def attend(valid, qkv_ref, mixed_ref, qa_ref, bias, table_ref, hp, between):
    L = qkv_ref.shape[0]
    nb = L // T
    key = lax.broadcasted_iota(jnp.int32, (L, 1), 0)
    mask = jnp.where(key < valid, 0.0, NEG)
    lane = lax.broadcasted_iota(jnp.int32, (T, 128), 1)
    ks = [halves(h, qkv_ref[:, 128:256], [1.0, 1.0, 1.0, mask], L) for h in range(2)]
    vs = [halves(h, qkv_ref[:, 256:384], [1.0], L) for h in range(2)]
    rows = [table_row(table_ref, 2 * hp + h) for h in range(2)]
    for qb in range(nb):
        if qb >= nb - 2:
            between(qb - nb + 3)
        kk = (qb + 1) * T
        qt = qkv_ref[qb * T:(qb + 1) * T, 0:128] * jnp.asarray(0.125, BF)
        outs = []
        for h in range(2):
            qh = halves(h, qt, [None, None, None, 1.0], T)
            sc = dot_nt(qh, ks[h][:kk])
            sc = jnp.concatenate(
                [
                    jnp.concatenate(
                        [
                            biased(sc[i * H:(i + 1) * H, j * H:(j + 1) * H], 2 * qb + i - j, bias.at[2 * hp + h], rows[h])
                            for j in range(kk // H)
                        ],
                        axis=1,
                    )
                    for i in range(2)
                ],
                axis=0,
            )
            mx = jnp.max(sc, axis=1, keepdims=True)
            p = jnp.exp(sc - mx)
            o = dot_nn(p.astype(BF), vs[h][:kk])
            l = o[:, 64 - 64 * h:65 - 64 * h]
            outs.append(o * (1.0 / l))
            hi, mid, lo = split3(-(mx + jnp.log(l)))
            qa_ref[h, qb * T:(qb + 1) * T, :] = halves(h, qt, [hi, mid, lo, 1.0], T)
        mixed_ref[qb * T:(qb + 1) * T, :] = jnp.where(lane < 64, outs[0], outs[1]).astype(BF)


def whole_block(shape):
    return pl.BlockSpec(shape, lambda *unused: (0,) * len(shape))


def first_half(sizes, vl, table, x, S, weights):
    R, D = x.shape
    L = R // S
    HP = D // 128
    remote = sizes is not None
    anyspace = pl.BlockSpec(memory_space=pl.ANY)
    in_specs = [pl.BlockSpec(memory_space=pltpu.SMEM), whole_block(table.shape), whole_block((R, D))]
    out_specs = [
        pl.BlockSpec((1, L, 128), lambda h, s: (s, 0, h)),
        pl.BlockSpec((1, 1, 2, L, 128), lambda h, s: (s, h, 0, 0, 0)),
        pl.BlockSpec((1, S, L, 384), lambda h, s: (h, 0, 0, 0)),
        anyspace,
        anyspace,
    ]
    out_shape = [
        jax.ShapeDtypeStruct((S, L, D), BF),
        jax.ShapeDtypeStruct((S, HP, 2, L, 128), BF),
        jax.ShapeDtypeStruct((HP, S, L, 384), BF),
        jax.ShapeDtypeStruct((D, R), BF),
        jax.ShapeDtypeStruct((2 * HP, len(VARIED), H, H), F32),
    ]
    scratch = [
        pltpu.VMEM((2 * HP, len(VARIED), H, H), F32), pltpu.VMEM((2 * HP, len(VARIED), H, H), F32), pltpu.VMEM((R, D), F32),
        pltpu.VMEM((D, R), F32), pltpu.VMEM((R, D), BF), pltpu.VMEM((D, R), BF), pltpu.SemaphoreType.DMA((2,)),
    ]
    if remote:
        first, second, wq, wo, wu, wd = weights
        in_specs += [whole_block(first.shape), whole_block(second.shape), whole_block(wq.shape), anyspace, anyspace, anyspace]
        out_specs += [whole_block((1, D)), whole_block((1, D))] + [anyspace] * 4
        out_shape += [jax.ShapeDtypeStruct((1, D), F32)] * 2
        out_shape += [jax.ShapeDtypeStruct((HP,) + sizes + (16, 384), BF)]
        out_shape += [jax.ShapeDtypeStruct(sizes + w.shape, BF) for w in (wo, wu, wd)]
        scratch += [
            pltpu.VMEM((HP, 16, 384), BF),
            pltpu.VMEM((HP,) + sizes + (16, 384), BF),
            pltpu.VMEM((16, 128), BF),
            pltpu.VMEM(sizes + (16, 128), BF),
            pltpu.SemaphoreType.DMA((len(GATHER_ORDERS),)),
        ] + semaphores(sizes, GATHER_ORDERS.values(), [False] * len(GATHER_ORDERS)) + [pltpu.SemaphoreType.DMA((HP,))]
        params = cp(collective_id=1, has_side_effects=True)
    else:
        gain, wq = weights
        in_specs += [whole_block((1, D)), pl.BlockSpec((1, D, 384), lambda h, s: (h, 0, 0))]
        params = cp()
    return pl.pallas_call(
        functools.partial(first_kernel, sizes), grid=(HP, S), in_specs=in_specs, out_specs=out_specs, out_shape=out_shape,
        scratch_shapes=scratch, compiler_params=params,
    )(vl, table, x, *weights)


CXYZ, CYXZ, CXZY, CYZX = (((3,), (a,), (b,), (c,)) for a, b, c in ((2, 1, 0), (1, 2, 0), (2, 0, 1), (1, 0, 2)))
DIRECT = ((3,), (0, 1, 2))
SCATTER_ORDERS = {
    "up0": CYXZ, "down0": CXYZ, "out": CYZX, "up1": CXZY, "down1": CYXZ, "q0": CYZX, "q1": CXZY, "q2": DIRECT, "q3": DIRECT,
}
SCATTER_SCHEDULE = timetable(
    {
        "q3": (8, 9, 12), "out": (1, 2, 3, 5, 6), "up0": (1, 2, 4, 5, 7), "up1": (1, 2, 4, 6, 7), "q1": (4, 5, 6, 7, 8),
        "q0": (2, 3, 5, 7, 8), "down0": (1, 3, 5, 6, 8), "down1": (1, 3, 6, 7, 9), "q2": (6, 7, 11), "table": (8, 9, 11),
    }
)


def last_kernel(sizes, plan, *refs):
    remote = sizes is not None
    refs = list(refs)
    take = lambda count: [refs.pop(0) for _ in range(count)]
    vl_ref, table_ref, bias, qa_ref, qkv_ref, o_ref, g_ref, nt_any, w_any, gain_ref, x_ref, ga_ref = take(12)
    if remote:
        terms_any = take(3)
    gi_ref, tab_ref = take(2)
    if remote:
        results = dict(zip(SCATTER_ORDERS, take(9)))
    else:
        (gw_ref,) = take(1)
    gacc, far, dqt, grads, nt_ref, w_ref, load_sem = take(7)
    loads = [(nt_any, nt_ref), (w_any, w_ref)]
    if remote:
        wo_terms, wu_terms, wd_terms = terms_vm = take(3)
        loads += list(zip(terms_any, terms_vm))
    loads = [pltpu.make_async_copy(a, b, load_sem.at[k]) for k, (a, b) in enumerate(loads)]
    t = pl.program_id(0)
    pairs = grads.shape[0]
    S = grads.shape[1] // qkv_ref.shape[2]
    steps = pairs * S
    hp = lax.div(t, S)
    s = lax.rem(t, S)
    L = qkv_ref.shape[2]
    R = S * L
    D = x_ref.shape[1]

    @pl.when(t == 0)
    def _():
        for load in loads:
            load.start()

    @pl.when(t == 1)
    def _():
        for load in loads:
            load.wait()

    if remote:
        wq_terms, tab_own, tab_all, local = take(4)
        terms = dict(out=wo_terms)
        for half in range(2):
            cols = slice(half * wu_terms.shape[5] // 2, (half + 1) * wu_terms.shape[5] // 2)
            rows = slice(half * wd_terms.shape[4] // 2, (half + 1) * wd_terms.shape[4] // 2)
            terms["up%d" % half] = wu_terms.at[:, :, :, :, :, cols]
            terms["down%d" % half] = wd_terms.at[:, :, :, :, rows]
        for pair in range(4):
            terms["q%d" % pair] = wq_terms.at[pair]
        send, recv = refs[-2:]
        place = firsts(sizes, [*SCATTER_ORDERS.values(), SPREAD], [True] * len(SCATTER_ORDERS) + [False])[0]
        parts = {}
        for k, name in enumerate(SCATTER_ORDERS):
            sums, landing = plan[name]
            parts[name] = Scatter(
                sizes, SCATTER_ORDERS[name], terms[name], take(len(sums)), take(len(landing)), results[name], send, recv, place[k]
            )
        parts["table"] = Gather(sizes, SPREAD, tab_own, tab_all, local, send, recv, place[-1])

        @pl.when(t == 0)
        def _():
            greet(sizes, SPREAD)

        @pl.when(t == 1)
        def _():
            await_greetings(sizes, SPREAD)

        run_schedule(t, {at: SCATTER_SCHEDULE[at] for at in SCATTER_SCHEDULE if at < 12}, parts)

    @pl.when(t < steps)
    def _():
        @pl.when(s == 0)
        def _():
            gacc[...] = jnp.zeros_like(gacc)
            far[...] = jnp.zeros_like(far)

        at = pl.multiple_of(s * L, L)
        attend_back(vl_ref[s], qa_ref.at[0, 0], qkv_ref.at[0, 0], o_ref[0], g_ref[0], grads, hp, at, bias, table_ref, gacc, far, dqt)

        @pl.when(s == S - 1)
        def _():
            rows = table_terms(gacc, far)
            place = pl.ds(pl.multiple_of(hp * 8, 8), 8)
            (tab_own if remote else tab_ref)[place, :] = rows
            gw = dot_nn(nt_ref[...], grads[hp]).astype(BF)
            if remote:
                wq_terms[hp] = gw.reshape(sizes + (16, 384))
            else:
                gw_ref[hp] = gw

    @pl.when(t >= steps)
    def _():
        B = x_ref.shape[0]
        at = pl.ds(pl.multiple_of((t - steps) * B, B), B)
        xhat, r = ln_parts(x_ref[...].astype(F32))
        dn = dot_nt(
            jnp.concatenate([grads[pair, at, :] for pair in range(pairs)], axis=1),
            jnp.concatenate([w_ref[pair] for pair in range(pairs)], axis=1),
        )
        gi_ref[...] = (ga_ref[...] + ln_back(dn, gain_ref[...], xhat, r)[0]).astype(BF)

    if remote:

        @pl.when(t == pl.num_programs(0) - 1)
        def _():
            run_actions(SCATTER_SCHEDULE[12], parts)
            total = None
            for at in itertools.product(*[range(size) for size in sizes]):
                block = tab_all[at]
                total = block if total is None else total + block
            tab_ref[...] = total


def table_terms(gacc, far):
    lane = lax.broadcasted_iota(jnp.int32, (1, 2 * H), 1)
    m = jnp.where(lane < H, lane, lane - 2 * H)
    bl = lax.broadcasted_iota(jnp.int32, (1, 128), 1)
    rows = []
    for h in range(2):
        row = jnp.zeros((1, 128), F32)
        for b in (14, 15):
            row = row + jnp.where(bl == b, jnp.sum(jnp.sum(far[h, b - 14], axis=0, keepdims=True), axis=1, keepdims=True), 0.0)
        for n, delta in enumerate(VARIED):
            w = jnp.concatenate([gacc[h, n], jnp.zeros((H, H), F32)], axis=1)
            acc = w[:8]
            for a in range(1, H // 8):
                acc = acc + pltpu.roll(w[8 * a:8 * a + 8], 2 * H - 8 * a, 1)
            diag = acc[0:1]
            for a in range(1, 8):
                diag = diag + pltpu.roll(acc[a:a + 1], 2 * H - a, 1)
            dist = delta * H + m
            for b in range(16):
                if LOW[b] >= (delta + 1) * H or (b < 15 and LOW[b + 1] <= (delta - 1) * H):
                    continue
                sel = dist >= LOW[b]
                if b < 15:
                    sel = sel & (dist < LOW[b + 1])
                row = row + jnp.where(bl == b, jnp.sum(jnp.where(sel, diag, 0.0), axis=1, keepdims=True), 0.0)
        rows.append(row)
    return jnp.concatenate(rows + [jnp.zeros((6, 128), F32)], axis=0)


def attend_back(valid, qa_ref, qkv_ref, o, g, grads, hp, first, bias, table_ref, gacc, far, dqt):
    L = qkv_ref.shape[0]
    rows = [table_row(table_ref, 2 * hp + h) for h in range(2)]
    nb = L // T
    key = lax.broadcasted_iota(jnp.int32, (L, 1), 0)
    mask = jnp.where(key < valid, 0.0, NEG)
    lane = lax.broadcasted_iota(jnp.int32, (T, 128), 1)
    prod = g.astype(F32) * o.astype(F32)
    lane_l = lax.broadcasted_iota(jnp.int32, (L, 128), 1)
    k = qkv_ref[:, 128:256]
    ks = [halves(h, k, [1.0, 1.0, 1.0, mask], L) for h in range(2)]
    vs = [halves(h, qkv_ref[:, 256:384], [1.0, 1.0, 1.0], L) for h in range(2)]
    gs = []
    for h in range(2):
        d = jnp.sum(jnp.where((lane_l // 64) == h, prod, 0.0), axis=1, keepdims=True)
        hi, mid, lo = split3(-d)
        gs.append(halves(h, g, [hi, mid, lo], L))
    kt = (k * jnp.asarray(0.125, BF)).T
    for kb in range(nb):
        dks, dvs = [], []
        for h in range(2):
            qh = qa_ref[h]
            st = dot_nt(ks[h][kb * T:(kb + 1) * T], qh[kb * T:])
            dp = dot_nt(vs[h][kb * T:(kb + 1) * T], gs[h][kb * T:])
            st = jnp.concatenate(
                [
                    jnp.concatenate(
                        [biased(st[j * H:(j + 1) * H, i * H:(i + 1) * H], i - j, bias.at[0, h], rows[h]) for i in range(2 * (nb - kb))],
                        axis=1,
                    )
                    for j in range(2)
                ],
                axis=0,
            )
            p = jnp.exp(st)
            ds = p * dp
            pb = p.astype(BF)
            dsb = ds.astype(BF)
            dvs.append(dot_nn(pb, gs[h][kb * T:]))
            dks.append(dot_nn(dsb, qh[kb * T:]))
            for delta in range(2 * (nb - kb)):
                both = [ds[j * H:(j + 1) * H, i * H:(i + 1) * H] for j in range(2) for i in range(2 * (nb - kb)) if i - j == delta]
                both = both[0] if len(both) == 1 else both[0] + both[1]
                if delta in VARIED:
                    gacc[h, VARIED.index(delta)] += both
                else:
                    far[h, 0 if delta == 3 else 1] += jnp.sum(both.reshape(H // 8, 8, H), axis=0)
            r = dot_nn(kt[h * 64:(h + 1) * 64, kb * T:(kb + 1) * T], dsb)
            if kb == 0:
                dqt[h * 64:(h + 1) * 64, :] = r
            else:
                dqt[h * 64:(h + 1) * 64, kb * T:] += r
        at = pl.ds(first + kb * T, T)
        grads[hp, at, 128:256] = jnp.where(lane < 64, dks[0], dks[1]).astype(BF)
        grads[hp, at, 256:384] = jnp.where(lane < 64, dvs[0], dvs[1]).astype(BF)
    grads[hp, pl.ds(first, L), 0:128] = dqt[...].T.astype(BF)


def last_half(sizes, vl, table, bias_t, qa, qkv, mixed, gm, nt, wq, gain, x, ga, ffn_grads):
    HP, S, L, W = qkv.shape
    R, D = x.shape
    B = 512
    steps = HP * S
    remote = sizes is not None
    pair = lambda t: jnp.minimum(t, steps - 1) // S
    seq = lambda t: jnp.minimum(t, steps - 1) % S
    late = pl.BlockSpec((B, D), lambda t: (jnp.maximum(t - steps, 0), 0))
    in_specs = [
        pl.BlockSpec(memory_space=pltpu.SMEM),
        whole_block(table.shape),
        pl.BlockSpec((1, 2, len(VARIED), H, H), lambda t: (pair(t), 0, 0, 0, 0)),
        pl.BlockSpec((1, 1, 2, L, 128), lambda t: (seq(t), pair(t), 0, 0, 0)),
        pl.BlockSpec((1, 1, L, W), lambda t: (pair(t), seq(t), 0, 0)),
        pl.BlockSpec((1, L, 128), lambda t: (seq(t), 0, pair(t))),
        pl.BlockSpec((1, L, 128), lambda t: (seq(t), 0, pair(t))),
        pl.BlockSpec(memory_space=pl.ANY),
        pl.BlockSpec(memory_space=pl.ANY),
        whole_block((1, D)),
        late,
        late,
    ]
    out_specs = [late, whole_block((8 * HP, 128))]
    out_shape = [jax.ShapeDtypeStruct((R, D), BF), jax.ShapeDtypeStruct((8 * HP, 128), F32)]
    scratch = [
        pltpu.VMEM((2, len(VARIED), H, H), F32), pltpu.VMEM((2, 2, 8, H), F32), pltpu.VMEM((128, L), F32),
        pltpu.VMEM((HP, R, W), BF), pltpu.VMEM((D, R), BF), pltpu.VMEM((HP, D, W), BF),
        pltpu.SemaphoreType.DMA((5 if remote else 2,)),
    ]
    args = [vl, table, bias_t.reshape(HP, 2, len(VARIED), H, H), qa, qkv, mixed, gm, nt, wq, gain, x, ga]
    plan = None
    if remote:
        count = int(np.prod(sizes))
        terms = [a.reshape(sizes + (a.shape[0] // count, a.shape[1])) for a in ffn_grads]
        args += terms
        in_specs += [pl.BlockSpec(memory_space=pl.ANY) for a in terms]
        scratch += [pltpu.VMEM(a.shape, BF) for a in terms]
        (_, D_), (_, U_), (rows_, _) = [a.shape[4:] for a in terms]
        blocks = dict(out=(16, D_), up0=(16, U_ // 2), up1=(16, U_ // 2), down0=(rows_ // 2, D_), down1=(rows_ // 2, D_))
        for k in range(HP):
            blocks["q%d" % k] = (16, W)
        plan = {name: Scatter.shapes(sizes, SCATTER_ORDERS[name], blocks[name]) for name in SCATTER_ORDERS}
        out_specs += [whole_block(blocks[name]) for name in SCATTER_ORDERS]
        out_shape += [jax.ShapeDtypeStruct(blocks[name], F32) for name in SCATTER_ORDERS]
        scratch += [
            pltpu.VMEM((HP,) + sizes + (16, W), BF), pltpu.VMEM((8 * HP, 128), F32), pltpu.VMEM(sizes + (8 * HP, 128), F32),
            pltpu.SemaphoreType.DMA,
        ]
        for name in SCATTER_ORDERS:
            scratch += [pltpu.VMEM(shape, BF) for shape in plan[name][0] + plan[name][1]]
        scratch += semaphores(sizes, [*SCATTER_ORDERS.values(), SPREAD], [True] * len(SCATTER_ORDERS) + [False])
        params = cp(collective_id=2, has_side_effects=True)
    else:
        out_specs += [whole_block((HP, D, W))]
        out_shape += [jax.ShapeDtypeStruct((HP, D, W), BF)]
        params = cp()
    return pl.pallas_call(
        functools.partial(last_kernel, sizes, plan), grid=(steps + R // B,), in_specs=in_specs, out_specs=out_specs,
        out_shape=out_shape, scratch_shapes=scratch, compiler_params=params,
    )(*args)


def finish_kernel(*refs):
    refs = list(refs)
    take = lambda count: [refs.pop(0) for _ in range(count)]
    tab_ref, ru0_ref, rd0_ref, ro_ref, ru1_ref, rd1_ref = take(6)
    pieces = take(4)
    first_ref, second_ref, wq_ref, wu_ref, gi_ref = take(5)
    tab_out, wq_out, wo_out, wu_out, wd_out, g1_out, g2_out, gi_out, held, sems = refs
    share = gi_ref.shape[0] // 4
    places = [pl.ds(k * share, share) for k in range(4)]
    moves_in = [pltpu.make_async_copy(gi_ref.at[at], held.at[at], sems.at[k]) for k, at in enumerate(places)]
    moves_out = [pltpu.make_async_copy(held.at[at], gi_out.at[at], sems.at[4 + k]) for k, at in enumerate(places)]
    for move in moves_in:
        move.start()
    for move_in, move_out in zip(moves_in, moves_out):
        move_in.wait()
        move_out.start()
    table = jnp.concatenate([tab_ref[8 * pair:8 * pair + 2, :] for pair in range(4)], axis=0)
    tab_out[...] = table[:, :16]
    wo_out[...] = ro_ref[...]
    for half, (ru_ref, rd_ref) in enumerate(((ru0_ref, rd0_ref), (ru1_ref, rd1_ref))):
        wu_out[:, half * ru_ref.shape[1]:(half + 1) * ru_ref.shape[1]] = ru_ref[...]
        wd_out[half * rd_ref.shape[0]:(half + 1) * rd_ref.shape[0], :] = rd_ref[...]
    for pair in range(4):
        for part in range(3):
            wq_out[:, (part * 4 + pair) * 128:(part * 4 + pair + 1) * 128] = pieces[pair][:, part * 128:(part + 1) * 128]
    square = lax.broadcasted_iota(jnp.int32, (16, 16), 0) == lax.broadcasted_iota(jnp.int32, (16, 16), 1)
    for first, w, grad, out in ((first_ref, wq_ref, wq_out, g1_out), (second_ref, wu_ref, wu_out, g2_out)):
        gain = first[...].reshape(1, 16).astype(F32)
        dots = jnp.sum(w[...].astype(F32) * grad[...], axis=1, keepdims=True)
        out[...] = jnp.sum(jnp.where(square, dots, 0.0), axis=0, keepdims=True) / gain
    for move in moves_out:
        move.wait()


def finish(tab, results, first, second, wq, wu, gi):
    out_shape = [
        jax.ShapeDtypeStruct((8, 16), F32), jax.ShapeDtypeStruct(wq.shape, F32), jax.ShapeDtypeStruct((wu.shape[0], wq.shape[1] // 3), F32),
        jax.ShapeDtypeStruct(wu.shape, F32), jax.ShapeDtypeStruct((2 * results[1].shape[0], wq.shape[1] // 3), F32), jax.ShapeDtypeStruct((1, 16), F32),
        jax.ShapeDtypeStruct((1, 16), F32),
    ]
    args = [tab, *results, first, second, wq, wu, gi]
    anyspace = pl.BlockSpec(memory_space=pl.ANY)
    return pl.pallas_call(
        finish_kernel,
        in_specs=[whole_block(a.shape) for a in args[:-1]] + [anyspace],
        out_specs=[whole_block(s.shape) for s in out_shape] + [anyspace],
        out_shape=out_shape + [jax.ShapeDtypeStruct(gi.shape, gi.dtype)],
        scratch_shapes=[pltpu.VMEM(gi.shape, gi.dtype), pltpu.SemaphoreType.DMA((8,))],
        compiler_params=cp(),
    )(*args)


def on_device(devices, inputs, valid_len, norm_first, w_qkv, w_out, relative_bucket_table, norm_second, w_up, w_down, output_gradient):
    S, L, D = inputs.shape
    R = S * L
    HP = D // 128
    FFW = w_up.shape[1]
    fast = devices == 32 and D == 512 and S == 2
    table = relative_bucket_table
    x = inputs.reshape(R, D)
    og = output_gradient.reshape(R, D)
    by_pair = lambda w: w.reshape(D, 3, HP, 128).transpose(2, 0, 1, 3).reshape(HP, D, 384)
    if fast:
        sizes = device_grid(devices)
        mixed, qa, qkv, nt, bias_t, g1, g2, wq, wo, wu, wd = first_half(
            sizes, valid_len, table, x, S, [norm_first, norm_second, w_qkv, w_out, w_up, w_down]
        )
        wq, wo, wu, wd = wq.reshape(HP, D, 384), wo.reshape(D, D), wu.reshape(D, FFW), wd.reshape(FFW, D)
    else:
        sizes = None
        g1, wq, wo, g2, wu, wd = [
            lax.all_gather(a, "dp", axis=0, tiled=True) for a in (norm_first, w_qkv, w_out, norm_second, w_up, w_down)
        ]
        g1, g2 = g1.reshape(1, D).astype(F32), g2.reshape(1, D).astype(F32)
        wq = by_pair(wq)
        mixed, qa, qkv, nt, bias_t = first_half(None, valid_len, table, x, S, [g1, wq])
    out, ga, gm, gwo, gwu, gwd = ffn(x, mixed.reshape(R, D), og, g2, wo, wu, wd)
    got = last_half(
        sizes, valid_len, table, bias_t, qa, qkv, mixed, gm.reshape(S, L, D), nt, wq, g1, x, ga, [gwo, gwu, gwd]
    )
    gi, tab = got[:2]
    if fast:
        rt, rq, ro, ru, rd, r1, r2, gi = finish(tab, got[2:], norm_first, norm_second, w_qkv, w_up, gi)
        r1, r2 = r1.reshape(-1), r2.reshape(-1)
    else:
        gwq = got[2].reshape(HP, D, 3, 128).transpose(1, 2, 0, 3).reshape(D, 3 * D)
        rq, ro, ru, rd = [
            lax.psum_scatter(a.astype(F32), "dp", scatter_dimension=0, tiled=True) for a in (gwq, gwo, gwu, gwd)
        ]
        r1 = jnp.sum(w_qkv.astype(F32) * rq, axis=1) / norm_first.astype(F32)
        r2 = jnp.sum(w_up.astype(F32) * ru, axis=1) / norm_second.astype(F32)
        rt = lax.psum(tab.reshape(HP, 8, 128)[:, :2, :16].reshape(table.shape), "dp")
    return (out.reshape(S, L, D), gi.reshape(S, L, D), r1, rq, ro, rt, r2, ru, rd)


def solution(mesh):
    placed = (
        P("dp", None, None), P("dp"), P("dp"), P("dp", None), P("dp", None), P(), P("dp"), P("dp", None), P("dp", None),
        P("dp", None, None),
    )
    return jax.shard_map(
        functools.partial(on_device, mesh.shape["dp"]),
        mesh=mesh,
        in_specs=placed,
        out_specs=(
            P("dp", None, None), P("dp", None, None), P("dp"), P("dp", None), P("dp", None), P(), P("dp"), P("dp", None),
            P("dp", None),
        ),
        check_vma=False,
    )
```
